32 devices in a mesh: wide: 8 (over y, x, core), narrow: 4 (over z).
Axes of the slice: x: 2, y: 2, z: 4, core: 2. Of those that a mesh axis runs over, the one named last changes fastest.
Arguments:
- state: float32 [512, 512, 128], P('wide', 'narrow'), may hold values from -6 to 6
- volatility: float32 [512, 512, 128], P('wide', 'narrow'), may hold values from 0.2 to 1.2
- cotangent: float32 [512, 512, 128], P('wide', 'narrow'), may hold values from -6 to 6
- solve_first: float32 [512, 512], replicated, may hold values from -2 to 2
- solve_second: float32 [512, 512], replicated, may hold values from -2 to 2
- solve_third: float32 [128, 128], replicated, may hold values from -2 to 2
- patch_index: int32 [512, 512], P('wide', 'narrow'), may hold values from 0 to 3071
Outputs:
- adjoint: float32 [512, 512, 128], P('wide', 'narrow')
- vega: float32 [3072], P(('wide', 'narrow'))
The draws below stay inside these ranges and needn't reach their ends.
All inputs are finite; a program needn't handle non-finite values.
Results may differ from the reference program's by a relative error of at most 0.000071.
Values sent between devices are 32-bit elements; how exact they have to be, the bound alone decides.
No kernel may reach another device: no remote copies, remote signals or barrier semaphores. Data moves between devices by JAX's collectives and lax.ppermute only.
A program may use at most 320 MiB of HBM per device.

```python
import math
import jax
import jax.numpy as jnp
from jax import lax

NX = 512
NY = 512
NZ = 128
PATCHES = 3072


def draw_solve_first(key, part):
    key = jax.random.fold_in(key, 11)
    key_diag, key_rest = jax.random.split(key)
    diagonal_part = jax.random.uniform(key_diag, (NX,), jnp.float32, 0.8, 1.2)
    spread = 0.35 * jax.random.normal(key_rest, (NX, NX), jnp.float32)
    return spread / math.sqrt(NX) + jnp.diag(diagonal_part)


def draw_solve_second(key, part):
    key = jax.random.fold_in(key, 23)
    key_diag, key_rest = jax.random.split(key)
    diagonal_part = jax.random.uniform(key_diag, (NY,), jnp.float32, 0.8, 1.2)
    spread = 0.35 * jax.random.normal(key_rest, (NY, NY), jnp.float32)
    return spread / math.sqrt(NY) + jnp.diag(diagonal_part)


def draw_solve_third(key, part):
    key = jax.random.fold_in(key, 37)
    key_diag, key_rest = jax.random.split(key)
    diagonal_part = jax.random.uniform(key_diag, (NZ,), jnp.float32, 0.8, 1.2)
    spread = 0.35 * jax.random.normal(key_rest, (NZ, NZ), jnp.float32)
    return spread / math.sqrt(NZ) + jnp.diag(diagonal_part)


def place_ends(array, stream_key, low, high):
    shape = array.shape
    spot = [jax.random.randint(jax.random.fold_in(stream_key, axis), (), 0, shape[axis]) for axis in range(len(shape))]
    array = array.at[tuple(spot)].set(low)
    longest = shape.index(max(shape))
    spot[longest] = (spot[longest] + 1) % shape[longest]
    return array.at[tuple(spot)].set(high)


def block_scale(own_key, extent, cuts, smallest, largest):
    loudness = 1.0
    for dim, shards_of in cuts:
        steps = jax.random.uniform(jax.random.fold_in(jax.random.fold_in(own_key, 6), dim), (shards_of,), jnp.float32, smallest / len(cuts), largest / len(cuts))
        loudness = loudness * jnp.repeat(jnp.exp(steps), extent[dim] // shards_of).reshape((-1,) + (1,) * (len(extent) - 1 - dim))
    return loudness


def gaussian(stream_key, shape, width, limit, cuts=(), held_as=jnp.bfloat16):
    factor_of = block_scale(stream_key, shape, cuts, -0.22, 0.18) if cuts else 1.0
    array = jax.random.normal(stream_key, shape, jnp.float32) * width * factor_of
    return jnp.minimum(jnp.maximum(array, -limit), limit).astype(held_as)


def setup_inputs(seed: int = 0) -> dict:
    key_list = jax.random.split(jax.random.key(seed), 8)
    state = gaussian(key_list[0], (NX, NY, NZ), 1.0, 6.0, ((0, 8), (1, 4)), jnp.float32)
    volatility = jnp.clip(jnp.exp(math.log(1.2) - 1.7917595 * jax.random.uniform(key_list[1], (NX, NY, NZ), jnp.float32) ** block_scale(key_list[1], (NX, NY, NZ), ((0, 8), (1, 4)), -0.2, 0.2)), 0.2, 1.2)
    cotangent = gaussian(key_list[2], (NX, NY, NZ), 1.0, 6.0, ((0, 8), (1, 4)), jnp.float32)
    solve_first = draw_solve_first(jax.random.fold_in(key_list[7], 71), 0)
    solve_second = draw_solve_second(jax.random.fold_in(key_list[7], 71), 0)
    solve_third = draw_solve_third(jax.random.fold_in(key_list[7], 71), 0)
    patch_index = place_ends(jax.random.randint(key_list[6], (NX, NY), 0, PATCHES), jax.random.fold_in(key_list[6], 1), 0, PATCHES - 1).astype(jnp.int32)
    return dict(state=state, volatility=volatility, cotangent=cotangent, solve_first=solve_first, solve_second=solve_second, solve_third=solve_third, patch_index=patch_index)


time_step = 0.4
theta_weight = 0.5
frozen_coef = 0.2
correction = 0.5 * 0.4
vega_scale = 1.0 / 32.0
correlations = ((0, 1, 0.5), (0, 2, 0.3), (1, 2, -0.4))


def shifted(padded, offsets):
    lead = padded.ndim - 3
    slices = [slice(None)] * lead
    for position, offset in enumerate(offsets):
        length = padded.shape[lead + position]
        slices.append(slice(1 + offset, length - 1 + offset))
    return padded[tuple(slices)]


def second_parts(padded):
    centre = shifted(padded, [0, 0, 0])
    result = []
    for axis_number in range(3):
        upward = [0, 0, 0]
        upward[axis_number] = 1
        downward = [0, 0, 0]
        downward[axis_number] = -1
        result.append(shifted(padded, upward) + shifted(padded, downward) - 2.0 * centre)
    return tuple(result)


def cross_term(padded, first_axis, second_axis):
    def corner(sign_first, sign_second):
        offsets = [0, 0, 0]
        offsets[first_axis] = sign_first
        offsets[second_axis] = sign_second
        return shifted(padded, offsets)

    return 0.25 * (corner(1, 1) - corner(1, -1) - corner(-1, 1) + corner(-1, -1))


def mixed_of(padded):
    total = None
    for first_axis, second_axis, weight in correlations:
        term = weight * cross_term(padded, first_axis, second_axis)
        total = term if total is None else total + term
    return total


def contract(matrix, field, axis_number, transposed):
    letters = "xyz"
    source = letters[axis_number]
    matrix_form = source + "w" if transposed else "w" + source
    result_form = letters.replace(source, "w")
    return jnp.einsum(matrix_form + "," + letters + "->" + result_form, matrix, field,
                      precision=lax.Precision.HIGHEST)


def reference(state, volatility, cotangent, solve_first, solve_second, solve_third, patch_index):
    coefficient = 0.5 * volatility * volatility
    padded = jnp.pad(state, 1)
    second_x, second_y, second_z = second_parts(padded)
    source = mixed_of(padded) + second_x + second_y + second_z
    start = state + time_step * coefficient * source
    damping = theta_weight * time_step * frozen_coef
    level = contract(solve_first, start - damping * second_x, 0, False)
    level = contract(solve_second, level - damping * second_y, 1, False)
    level = contract(solve_third, level - damping * second_z, 2, False)
    drift = mixed_of(jnp.pad(level - state, 1))
    back_third = contract(solve_third, cotangent, 2, True)
    back_second = contract(solve_second, back_third, 1, True)
    carried = contract(solve_first, back_second, 0, True)
    reaction = mixed_of(jnp.pad(correction * coefficient * carried, 1))
    total = cotangent + reaction
    upper_third = contract(solve_third, total, 2, True)
    upper_second = contract(solve_second, upper_third, 1, True)
    adjoint_start = contract(solve_first, upper_second, 0, True)
    scaled = time_step * coefficient * adjoint_start
    padded = jnp.pad(scaled, 1)
    parts = second_parts(padded)
    spread = mixed_of(padded) + parts[0] + parts[1] + parts[2]
    lines = second_parts(jnp.pad(adjoint_start, 1))[0] + second_parts(jnp.pad(upper_second, 1))[1]
    lines = lines + second_parts(jnp.pad(upper_third, 1))[2]
    adjoint = adjoint_start + spread - reaction - damping * lines
    sensitivity = volatility * (correction * carried * drift + time_step * adjoint_start * source)
    column = jnp.sum(sensitivity, axis=2)
    vega = jax.ops.segment_sum(column.reshape(-1), patch_index.reshape(-1).astype(jnp.int32),
                               num_segments=PATCHES)
    return adjoint, vega * vega_scale
```

```python
import functools
import jax
import jax.numpy as jnp
from jax import lax
from jax.experimental import pallas as pl
from jax.experimental.pallas import tpu as pltpu
from jax.sharding import PartitionSpec as P

PATCHES = 3072


time_step = 0.4
theta_weight = 0.5
frozen_coef = 0.2
correction = 0.5 * 0.4
vega_scale = 1.0 / 32.0
correlations = ((0, 1, 0.5), (0, 2, 0.3), (1, 2, -0.4))


def padded_2(cells, sides, width):
    for axis, dim in sides:
        count = lax.axis_size(axis)
        ends = count - 1
        head = lax.slice_in_dim(cells, 0, width, axis=dim)
        tail = lax.slice_in_dim(cells, cells.shape[dim] - width, cells.shape[dim], axis=dim)
        cells = jnp.concatenate(
            [
                lax.ppermute(tail, axis, [(i, (i + 1) % count) for i in range(ends)]),
                cells,
                lax.ppermute(head, axis, [((i + 1) % count, i) for i in range(ends)]),
            ],
            axis=dim,
        )
    return cells


def along_third(values, offset):
    if offset == 0:
        return values
    zero_layer = jnp.zeros_like(values[..., :1])
    if offset > 0:
        return jnp.concatenate([values[..., 1:], zero_layer], axis=-1)
    return jnp.concatenate([zero_layer, values[..., :-1]], axis=-1)


def shifted(padded, offsets):
    lead = padded.ndim - 3
    slices = [slice(None)] * lead
    for position in range(2):
        offset = offsets[position]
        length = padded.shape[lead + position]
        slices.append(slice(1 + offset, length - 1 + offset))
    slices.append(slice(None))
    return along_third(padded[tuple(slices)], offsets[2])


def second_parts(padded):
    centre = shifted(padded, [0, 0, 0])
    result = []
    for axis_number in range(3):
        upward = [0, 0, 0]
        upward[axis_number] = 1
        downward = [0, 0, 0]
        downward[axis_number] = -1
        result.append(shifted(padded, upward) + shifted(padded, downward) - 2.0 * centre)
    return tuple(result)


def cross_term(padded, first_axis, second_axis):

    def corner(sign_first, sign_second):
        offsets = [0, 0, 0]
        offsets[first_axis] = sign_first
        offsets[second_axis] = sign_second
        return shifted(padded, offsets)

    return 0.25 * (corner(1, 1) - corner(1, -1) - corner(-1, 1) + corner(-1, -1))


def mixed_of(padded):
    total = None
    for first_axis, second_axis, weight in correlations:
        term = weight * cross_term(padded, first_axis, second_axis)
        total = term if total is None else total + term
    return total


def contract(matrix, field, axis_number, transposed):
    letters = "xyz"
    source = letters[axis_number]
    matrix_form = source + "w" if transposed else "w" + source
    result_form = letters.replace(source, "w")
    return jnp.einsum(
        matrix_form + "," + letters + "->" + result_form,
        matrix,
        field,
        precision=lax.Precision.HIGHEST,
    )


def line_x(field, matrix, transposed):

    def solve_lines(pieces):
        solved = contract(matrix, pieces, 0, transposed)
        return lax.all_to_all(solved, "wide", split_axis=0, concat_axis=1, tiled=True)

    return solve_lines(lax.all_to_all(field, "wide", split_axis=1, concat_axis=0, tiled=True))


def line_y(field, matrix, transposed):

    def solve_lines(pieces):
        solved = contract(matrix, pieces, 1, transposed)
        return lax.all_to_all(solved, "narrow", split_axis=1, concat_axis=2, tiled=True)

    return solve_lines(lax.all_to_all(field, "narrow", split_axis=2, concat_axis=1, tiled=True))


def rimmed(stacked):
    return padded_2(stacked, (("wide", 1), ("narrow", 2)), 1)


def third_second(field):
    return along_third(field, 1) + along_third(field, -1) - 2.0 * field


def on_device_plain(state, volatility, cotangent, solve_first, solve_second, solve_third, patch_index):
    coefficient = 0.5 * volatility * volatility
    padded = rimmed(state[None])
    parts = second_parts(padded)
    second_x, second_y, second_z = (parts[0][0], parts[1][0], parts[2][0])
    source = mixed_of(padded)[0] + second_x + second_y + second_z
    start = state + time_step * coefficient * source
    damping = theta_weight * time_step * frozen_coef
    level = line_x(start - damping * second_x, solve_first, False)
    level = line_y(level - damping * second_y, solve_second, False)
    level = contract(solve_third, level - damping * second_z, 2, False)
    drift = mixed_of(rimmed((level - state)[None]))[0]
    back_third = contract(solve_third, cotangent, 2, True)
    back_second = line_y(back_third, solve_second, True)
    carried = line_x(back_second, solve_first, True)
    reaction = mixed_of(rimmed((correction * coefficient * carried)[None]))[0]
    total = cotangent + reaction
    upper_third = contract(solve_third, total, 2, True)
    upper_second = line_y(upper_third, solve_second, True)
    adjoint_start = line_x(upper_second, solve_first, True)
    scaled = time_step * coefficient * adjoint_start
    padded = rimmed(jnp.stack([scaled, adjoint_start, upper_second]))
    parts = second_parts(padded)
    spread = mixed_of(padded[0:1])[0] + parts[0][0] + parts[1][0] + parts[2][0]
    lines = parts[0][1] + parts[1][2] + third_second(upper_third)
    adjoint = adjoint_start + spread - reaction - damping * lines
    sensitivity = volatility * (correction * carried * drift + time_step * adjoint_start * source)
    column = jnp.sum(sensitivity, axis=2)
    partial_sums = jax.ops.segment_sum(
        column.reshape(-1), patch_index.reshape(-1), num_segments=PATCHES
    )
    vega = lax.psum_scatter(partial_sums, ("wide", "narrow"), scatter_dimension=0, tiled=True)
    return (adjoint, vega * vega_scale)


F32 = jnp.float32
BF16 = jnp.bfloat16
damping = 0.5 * 0.4 * 0.2
MIB = 1024 * 1024
PLANES = 8


def params(mib):
    return pltpu.CompilerParams(vmem_limit_bytes=mib * MIB)


def cost(flops, mib):
    return pl.CostEstimate(flops=int(flops), bytes_accessed=int(mib * MIB), transcendentals=0)


def halves(x):
    high = lax.reduce_precision(x, 8, 7)
    return high.astype(BF16), (x - high).astype(BF16)


def left_form(matrix):
    high, low = halves(matrix)
    return jnp.concatenate([high, high, low], axis=1)


def right_form(matrix):
    high, low = halves(matrix)
    return jnp.concatenate([high, high, low], axis=0)


def split(x):
    high = x.astype(BF16)
    return high, (x - high.astype(F32)).astype(BF16)


def left_product(matrix3, field):
    high, low = split(field)
    return jnp.dot(matrix3, jnp.concatenate([high, low, high], axis=0), preferred_element_type=F32)


def right_product(field, matrix3):
    high, low = split(field)
    return jnp.dot(jnp.concatenate([high, low, high], axis=1), matrix3, preferred_element_type=F32)


def y_pair(v, low_row, high_row):
    n = v.shape[0]
    row = lax.broadcasted_iota(jnp.int32, v.shape, 0)
    up = jnp.where(row == n - 1, high_row, pltpu.roll(v, n - 1, 0))
    down = jnp.where(row == 0, low_row, pltpu.roll(v, 1, 0))
    return up, down


def z_pair(v):
    n = v.shape[1]
    lane = lax.broadcasted_iota(jnp.int32, v.shape, 1)
    up = jnp.where(lane == n - 1, 0.0, pltpu.roll(v, n - 1, 1))
    down = jnp.where(lane == 0, 0.0, pltpu.roll(v, 1, 1))
    return up, down


def sweep(count, plane, rows, emit, full):
    v, p, rest, inner = {}, {}, {}, {}
    for k in range(-1, count + 1):
        centre = plane(k)
        y_up, y_down = y_pair(centre, *rows(k))
        z_up, z_down = z_pair(centre)
        e = y_up - y_down
        v[k] = centre
        p[k] = 0.125 * e + 0.075 * (z_up - z_down)
        if 0 <= k < count:
            e_up, e_down = z_pair(e)
            rest[k] = -0.1 * (e_up - e_down)
            if full:
                inner[k] = (y_up + y_down) + (z_up + z_down) - 4.0 * centre
        if k >= 1:
            mixed = (p[k] - p[k - 2]) + rest[k - 1]
            emit(k - 1, v[k - 1], v[k - 2], v[k], mixed, inner.get(k - 1))


def chunk_plane(ref, x):
    value = ref[:, x]
    return value.reshape(value.shape[0] * value.shape[1], value.shape[2])


def plane_specs(step_block, last, shape):
    tail = shape[1:]
    return [
        pl.BlockSpec((PLANES,) + tail, lambda s, i: (step_block(s, i), 0, 0)),
        pl.BlockSpec((1,) + tail, lambda s, i: (jnp.maximum(step_block(s, i) * PLANES - 1, 0), 0, 0)),
        pl.BlockSpec((1,) + tail, lambda s, i: (jnp.minimum(step_block(s, i) * PLANES + PLANES, last), 0, 0)),
    ]


def whole(shape):
    return pl.BlockSpec(shape, lambda s, i: (0,) * len(shape))


def pick_plane(k, count, block, main, before, after, low, high, blocks):
    if k < 0:
        return jnp.where(block == 0, low[0], before[0])
    if k >= count:
        return jnp.where(block == blocks - 1, high[0], after[0])
    return main[k]


def natural(s, i):
    return s


def rotated(per, n):
    def block(s, i):
        return lax.rem(i[0] + s // per, n) * per + lax.rem(s, per)

    return block


def piece_map(d, per):
    return lambda s: jnp.clip(s - d * per, 0, per - 1)


def forward_kernel(i, state, before, after, low, high, y_low, y_high, volatility, a_out, source_out, *, blocks):
    block = pl.program_id(0)

    def emit(k, v, prev, nxt, mixed, inner):
        second_x = prev + nxt - 2.0 * v
        source = mixed + second_x + inner
        sigma = volatility[k]
        a = v + (time_step * 0.5) * sigma * sigma * source - damping * second_x
        a_out[:, k] = a.reshape(a_out.shape[0], a_out.shape[2], a_out.shape[3])
        source_out[k] = time_step * sigma * source

    sweep(
        PLANES,
        lambda k: pick_plane(k, PLANES, block, state, before, after, low, high, blocks),
        lambda k: (y_low[pl.ds(block * PLANES + k + 1, 1), :], y_high[pl.ds(block * PLANES + k + 1, 1), :]),
        emit,
        True,
    )


def forward(index, state, volatility, low, high, y_low, y_high, wide):
    bx, by, bz = state.shape
    blocks = bx // PLANES
    return pl.pallas_call(
        functools.partial(forward_kernel, blocks=blocks),
        grid_spec=pltpu.PrefetchScalarGridSpec(
            num_scalar_prefetch=1,
            grid=(blocks,),
            in_specs=plane_specs(natural, bx - 1, state.shape)
            + [whole(low.shape), whole(high.shape), whole(y_low.shape), whole(y_high.shape)]
            + [pl.BlockSpec((PLANES, by, bz), lambda s, i: (s, 0, 0))],
            out_specs=[
                pl.BlockSpec((wide, PLANES, by // wide, bz), lambda s, i: (0, s, 0, 0)),
                pl.BlockSpec((PLANES, by, bz), lambda s, i: (s, 0, 0)),
            ],
        ),
        out_shape=[
            jax.ShapeDtypeStruct((wide, bx, by // wide, bz), F32),
            jax.ShapeDtypeStruct(state.shape, F32),
        ],
        compiler_params=params(32),
        cost_estimate=cost(5e9, 17),
        name="forward",
    )(index, state, state, state, low, high, y_low, y_high, volatility)


def frozen_kernel(i, state, before, after, low, high, q_low, q_high, third3, out, *, blocks):
    block = pl.program_id(0)

    def plane(k):
        v = pick_plane(k, PLANES, block, state, before, after, low, high, blocks)
        up, down = z_pair(v)
        return v + damping * right_product(up + down - 2.0 * v, third3[...])

    def emit(k, v, prev, nxt, mixed, inner):
        out[k] = mixed

    sweep(
        PLANES,
        plane,
        lambda k: (q_low[pl.ds(block * PLANES + k + 1, 1), :], q_high[pl.ds(block * PLANES + k + 1, 1), :]),
        emit,
        False,
    )


def frozen(index, state, low, high, q_low, q_high, third3):
    bx, by, bz = state.shape
    blocks = bx // PLANES
    return pl.pallas_call(
        functools.partial(frozen_kernel, blocks=blocks),
        grid_spec=pltpu.PrefetchScalarGridSpec(
            num_scalar_prefetch=1,
            grid=(blocks,),
            in_specs=plane_specs(natural, bx - 1, state.shape)
            + [whole(low.shape), whole(high.shape), whole(q_low.shape), whole(q_high.shape), whole(third3.shape)],
            out_specs=pl.BlockSpec((PLANES, by, bz), lambda s, i: (s, 0, 0)),
        ),
        out_shape=jax.ShapeDtypeStruct(state.shape, F32),
        compiler_params=params(32),
        cost_estimate=cost(5e9, 9),
        name="frozen",
    )(index, state, state, state, low, high, q_low, q_high, third3)


def first_kernel(*refs, count, lines, parts, length, halo):
    pieces, matrix3, out = refs[:count], refs[count], refs[count + 1]
    depth = pieces[0].shape[0] // lines
    rows = length + 2 * halo

    def pair(step, carry):
        y = step * 2
        field = jnp.concatenate(
            [
                jnp.concatenate([piece[pl.ds(y + t, depth, stride=lines), :] for piece in pieces], axis=0)
                for t in range(2)
            ],
            axis=1,
        )
        solved = left_product(matrix3[...], field)
        width = solved.shape[1] // 2
        for t in range(2):
            half = solved[:, t * width : (t + 1) * width]
            for part in range(parts):
                base = part * rows
                out[pl.ds((base + halo) * lines + y + t, length, stride=lines), :] = half[part * length : (part + 1) * length]
                if halo:
                    zero = jnp.zeros((1, width), F32)
                    before = half[part * length - 1 : part * length] if part > 0 else zero
                    after = half[(part + 1) * length : (part + 1) * length + 1] if part < parts - 1 else zero
                    out[pl.ds(base * lines + y + t, 1), :] = before
                    out[pl.ds((base + rows - 1) * lines + y + t, 1), :] = after
        return carry

    lax.fori_loop(0, lines // 2, pair, 0)


def first(pieces, matrix3, halo):
    wide = pieces[0].shape[0]
    lines, bz = pieces[0].shape[2:]
    length = sum(piece.shape[1] for piece in pieces)
    rows = length + 2 * halo
    flat = [piece.reshape(-1, bz) for piece in pieces]
    out = pl.pallas_call(
        functools.partial(first_kernel, count=len(flat), lines=lines, parts=wide, length=length, halo=halo),
        in_specs=[pl.BlockSpec(memory_space=pltpu.VMEM)] * (len(flat) + 1),
        out_specs=pl.BlockSpec(memory_space=pltpu.VMEM),
        out_shape=jax.ShapeDtypeStruct((wide * rows * lines, bz), F32),
        compiler_params=params(40),
        cost_estimate=cost(7e9, 10),
        name="first",
    )(*flat, matrix3)
    return out.reshape(wide, rows, lines, bz)


def second_kernel(*refs, count, chunked):
    pieces, second3, third3, outs = refs[:count], refs[count], refs[count + 1], refs[count + 2 :]
    per, by, bz = pieces[0].shape
    length = count * by
    field = jnp.concatenate([piece[x] for x in range(per) for piece in pieces], axis=0)
    field = right_product(field, third3[...])
    field = jnp.concatenate([field[x * length : (x + 1) * length] for x in range(per)], axis=1)
    solved = left_product(second3[...], field)
    for x in range(per):
        half = solved[:, x * bz : (x + 1) * bz]
        if chunked:
            for d in range(count):
                out = outs[d]
                out[:, x] = half[d * by : (d + 1) * by].reshape(out.shape[0], out.shape[2], bz)
        else:
            outs[0][x] = half


def second(pieces, second3, third3, wide):
    count = len(pieces)
    xs, by, bz = pieces[0].shape
    per = 2
    if wide:
        out_specs = [pl.BlockSpec((wide, per, by // wide, bz), lambda s: (0, s, 0, 0))] * count
        out_shape = [jax.ShapeDtypeStruct((wide, xs, by // wide, bz), F32)] * count
    else:
        out_specs = [pl.BlockSpec((per, count * by, bz), lambda s: (s, 0, 0))]
        out_shape = [jax.ShapeDtypeStruct((xs, count * by, bz), F32)]
    return pl.pallas_call(
        functools.partial(second_kernel, count=count, chunked=bool(wide)),
        grid=(xs // per,),
        in_specs=[pl.BlockSpec((per, by, bz), lambda s: (s, 0, 0))] * count
        + [pl.BlockSpec(second3.shape, lambda s: (0, 0)), pl.BlockSpec(third3.shape, lambda s: (0, 0))],
        out_specs=out_specs,
        out_shape=out_shape,
        compiler_params=params(40),
        cost_estimate=cost(9e9, 10),
        name="second",
    )(*pieces, second3, third3)


def piece_specs(xs, tail, per, n):
    return [pl.BlockSpec((PLANES,) + tail, lambda s, i, d=d: (jnp.clip(s - d * per, 0, per - 1), 0, 0)) for d in range(n)]


def chunk_piece_specs(wide, lines, bz, per, order):
    return [
        pl.BlockSpec((wide, PLANES, lines, bz), lambda s, i, d=d: (0, jnp.clip(s - d * per, 0, per - 1), 0, 0))
        for d in order
    ]


def store_piece(outs, step, per, k, value):
    for d, out in enumerate(outs):

        @pl.when(step // per == d)
        def _(out=out):
            out[k] = value


def select(values, turn):
    result = values[0]
    for d in range(1, len(values)):
        result = jnp.where(turn == d, values[d], result)
    return result


def lifted_kernel(i, solved, state, y_low, y_high, *outs, per, n):
    step = pl.program_id(0)
    block = rotated(per, n)(step, i)
    for k in range(PLANES):
        v = state[k]
        up, down = y_pair(v, y_low[pl.ds(block * PLANES + k + 1, 1), :], y_high[pl.ds(block * PLANES + k + 1, 1), :])
        store_piece(outs, step, per, k, chunk_plane(solved, k) - damping * (up + down - 2.0 * v))


def lifted(index, solved, state, y_low, y_high, n):
    bx, by, bz = state.shape
    xs = bx // n
    per = xs // PLANES
    wide, lines = solved.shape[0], solved.shape[2]
    block = rotated(per, n)
    return pl.pallas_call(
        functools.partial(lifted_kernel, per=per, n=n),
        grid_spec=pltpu.PrefetchScalarGridSpec(
            num_scalar_prefetch=1,
            grid=(n * per,),
            in_specs=[
                pl.BlockSpec((wide, PLANES, lines, bz), lambda s, i: (0, block(s, i), 0, 0)),
                pl.BlockSpec((PLANES, by, bz), lambda s, i: (block(s, i), 0, 0)),
                whole(y_low.shape),
                whole(y_high.shape),
            ],
            out_specs=piece_specs(xs, (by, bz), per, n),
        ),
        out_shape=[jax.ShapeDtypeStruct((xs, by, bz), F32)] * n,
        compiler_params=params(32),
        cost_estimate=cost(2e9, 13),
        name="lifted",
    )(index, solved, state, y_low, y_high)


def reaction_kernel(
    i, carried, carried_low, carried_high, vol, before, after, low, high, vol_low, vol_high, cotangent, *outs, per, n, blocks
):
    step = pl.program_id(0)
    block = rotated(per, n)(step, i)

    def plane(k):
        sigma = pick_plane(k, PLANES, block, vol, before, after, low, high, blocks)
        return (0.5 * correction) * sigma * sigma * chunk_plane(carried, block * PLANES + k + 1)

    def rows(k):
        at = pl.ds(block * PLANES + k + 1, 1)
        s_low, s_high = vol_low[at, :], vol_high[at, :]
        return (
            (0.5 * correction) * s_low * s_low * carried_low[at, :],
            (0.5 * correction) * s_high * s_high * carried_high[at, :],
        )

    def emit(k, v, prev, nxt, mixed, inner):
        store_piece(outs, step, per, k, cotangent[k] + mixed)

    sweep(PLANES, plane, rows, emit, False)


def react(index, carried, carried_low, carried_high, vol, low, high, vol_low, vol_high, cotangent, n):
    bx, by, bz = vol.shape
    xs = bx // n
    per = xs // PLANES
    block = rotated(per, n)
    return pl.pallas_call(
        functools.partial(reaction_kernel, per=per, n=n, blocks=bx // PLANES),
        grid_spec=pltpu.PrefetchScalarGridSpec(
            num_scalar_prefetch=1,
            grid=(n * per,),
            in_specs=[whole(carried.shape), whole(carried_low.shape), whole(carried_high.shape)]
            + plane_specs(block, bx - 1, vol.shape)
            + [whole(low.shape), whole(high.shape), whole(vol_low.shape), whole(vol_high.shape)]
            + [pl.BlockSpec((PLANES, by, bz), lambda s, i: (block(s, i), 0, 0))],
            out_specs=piece_specs(xs, (by, bz), per, n),
        ),
        out_shape=[jax.ShapeDtypeStruct((xs, by, bz), F32)] * n,
        compiler_params=params(40),
        cost_estimate=cost(4e9, 17),
        name="reaction",
    )(index, carried, carried_low, carried_high, vol, vol, vol, low, high, vol_low, vol_high, cotangent)


def lines_kernel(i, *refs, per, n):
    totals, uppers = refs[:n], refs[n : 2 * n]
    cotangent, upper_low, upper_high, third3, out = refs[2 * n :]
    step = pl.program_id(0)
    turn = step // per
    block = rotated(per, n)(step, i)
    for k in range(PLANES):
        total = select([ref[k] for ref in totals], turn)
        upper = select([chunk_plane(ref, k) for ref in uppers], turn)
        at = pl.ds(block * PLANES + k, 1)
        up, down = y_pair(upper, upper_low[at, :], upper_high[at, :])
        third = right_product(total, third3[...])
        z_up, z_down = z_pair(third)
        lines = (up + down - 2.0 * upper) + (z_up + z_down - 2.0 * third)
        out[k] = cotangent[k] - total - damping * lines


def gather_lines(index, totals, uppers, cotangent, upper_low, upper_high, third3):
    n = len(totals)
    bx, by, bz = cotangent.shape
    xs = bx // n
    per = xs // PLANES
    wide, lines = uppers[0].shape[0], uppers[0].shape[2]
    block = rotated(per, n)
    order = [(n - e) % n for e in range(n)]
    return pl.pallas_call(
        functools.partial(lines_kernel, per=per, n=n),
        grid_spec=pltpu.PrefetchScalarGridSpec(
            num_scalar_prefetch=1,
            grid=(n * per,),
            in_specs=piece_specs(xs, (by, bz), per, n)
            + chunk_piece_specs(wide, lines, bz, per, range(n))
            + [pl.BlockSpec((PLANES, by, bz), lambda s, i: (block(s, i), 0, 0))]
            + [whole(upper_low.shape), whole(upper_high.shape), whole(third3.shape)],
            out_specs=pl.BlockSpec((PLANES, by, bz), lambda s, i: (block(s, i), 0, 0)),
        ),
        out_shape=jax.ShapeDtypeStruct(cotangent.shape, F32),
        compiler_params=params(40),
        cost_estimate=cost(5e9, 17),
        name="lines",
    )(index, *totals, *[uppers[order[d]] for d in range(n)], cotangent, upper_low, upper_high, third3)


def mixed_kernel(i, field, low, high, *refs, n):
    outs, scratch = refs[:n], refs[n]
    count = field.shape[0]
    by = outs[0].shape[1]

    def emit(k, v, prev, nxt, mixed, inner):
        scratch[...] = mixed
        for d, out in enumerate(outs):
            start = pl.multiple_of(lax.rem(i[0] + d, n) * by, by)
            out[k] = scratch[pl.ds(start, by), :]

    zero = jnp.zeros((1, field.shape[2]), F32)
    sweep(
        count,
        lambda k: low[0] if k < 0 else high[0] if k >= count else field[k],
        lambda k: (zero, zero),
        emit,
        False,
    )


def mix(index, field, low, high, n):
    xs, ny, bz = field.shape
    by = ny // n
    return pl.pallas_call(
        functools.partial(mixed_kernel, n=n),
        grid_spec=pltpu.PrefetchScalarGridSpec(
            num_scalar_prefetch=1,
            grid=(1,),
            in_specs=[whole(field.shape), whole(low.shape), whole(high.shape)],
            out_specs=[whole((xs, by, bz))] * n,
            scratch_shapes=[pltpu.VMEM((ny, bz), F32)],
        ),
        out_shape=[jax.ShapeDtypeStruct((xs, by, bz), F32)] * n,
        compiler_params=params(40),
        cost_estimate=cost(4e9, 9),
        name="mixed",
    )(index, field, low, high)


def patch_sums(out, step, planes, patch, patch_t, groups):
    @pl.when(step == 0)
    def _():
        out[...] = jnp.zeros_like(out)

    acc = None
    for k, value in enumerate(planes):
        column = jnp.sum(value, axis=1, keepdims=True)
        number = patch[pl.ds(k, 1), :]
        coarse = lax.broadcasted_iota(jnp.int32, (groups, number.shape[1]), 0) == lax.shift_right_logical(number, 7)
        number_t = patch_t[k]
        lane = lax.broadcasted_iota(jnp.int32, (number_t.shape[0], 128), 1)
        fine = jnp.where(lane == lax.bitwise_and(number_t, 127), column, 0.0)
        high, low = split(fine)
        term = jnp.dot(
            jnp.where(coarse, 1.0, 0.0).astype(BF16), jnp.concatenate([high, low], axis=1), preferred_element_type=F32
        )
        acc = term if acc is None else acc + term
    out[...] += acc


def drift_kernel(i, *refs, per, n, groups):
    drifts = refs[:n]
    frozen_part, carried, vol, patch, patch_t, out = refs[n:]
    step = pl.program_id(0)
    turn = step // per
    block = rotated(per, n)(step, i)
    planes = []
    for k in range(PLANES):
        drift = select([ref[k] for ref in drifts], turn) - frozen_part[k]
        planes.append(correction * vol[k] * chunk_plane(carried, block * PLANES + k + 1) * drift)
    patch_sums(out, step, planes, patch, patch_t, groups)


def drift_sums(index, drifts, frozen_part, carried, vol, patch, patch_t, groups):
    n = len(drifts)
    bx, by, bz = vol.shape
    xs = bx // n
    per = xs // PLANES
    block = rotated(per, n)
    order = [(n - e) % n for e in range(n)]
    main = pl.BlockSpec((PLANES, by, bz), lambda s, i: (block(s, i), 0, 0))
    return pl.pallas_call(
        functools.partial(drift_kernel, per=per, n=n, groups=groups),
        grid_spec=pltpu.PrefetchScalarGridSpec(
            num_scalar_prefetch=1,
            grid=(n * per,),
            in_specs=piece_specs(xs, (by, bz), per, n)
            + [main, whole(carried.shape), main]
            + [pl.BlockSpec((PLANES, by), lambda s, i: (block(s, i), 0))]
            + [pl.BlockSpec((PLANES, by, 1), lambda s, i: (block(s, i), 0, 0))],
            out_specs=whole((groups, 256)),
        ),
        out_shape=jax.ShapeDtypeStruct((groups, 256), F32),
        compiler_params=params(40),
        cost_estimate=cost(4e9, 17),
        name="drift",
    )(index, *[drifts[order[d]] for d in range(n)], frozen_part, carried, vol, patch, patch_t)


def source_kernel(i, adjoint_start, source, patch, patch_t, given, out, *, groups):
    step = pl.program_id(0)
    planes = [source[k] * chunk_plane(adjoint_start, step * PLANES + k + 1) for k in range(PLANES)]
    patch_sums(out, step, planes, patch, patch_t, groups)

    @pl.when(step == pl.num_programs(0) - 1)
    def _():
        out[...] += given[...]


def source_sums(index, adjoint_start, source, patch, patch_t, given):
    bx, by, bz = source.shape
    groups = given.shape[0]
    return pl.pallas_call(
        functools.partial(source_kernel, groups=groups),
        grid_spec=pltpu.PrefetchScalarGridSpec(
            num_scalar_prefetch=1,
            grid=(bx // PLANES,),
            in_specs=[whole(adjoint_start.shape), pl.BlockSpec((PLANES, by, bz), lambda s, i: (s, 0, 0))]
            + [pl.BlockSpec((PLANES, by), lambda s, i: (s, 0))]
            + [pl.BlockSpec((PLANES, by, 1), lambda s, i: (s, 0, 0)), whole(given.shape)],
            out_specs=whole(given.shape),
        ),
        out_shape=jax.ShapeDtypeStruct(given.shape, F32),
        compiler_params=params(40),
        cost_estimate=cost(3e9, 9),
        name="source",
    )(index, adjoint_start, source, patch, patch_t, given)


def adjoint_kernel(
    i, start, start_low, start_high, vol, before, after, low, high, vol_low, vol_high, tail, out, *, blocks
):
    block = pl.program_id(0)
    raw = {}

    def plane(k):
        sigma = pick_plane(k, PLANES, block, vol, before, after, low, high, blocks)
        raw[k] = chunk_plane(start, block * PLANES + k + 1)
        return (0.5 * time_step) * sigma * sigma * raw[k]

    def rows(k):
        at = pl.ds(block * PLANES + k + 1, 1)
        s_low, s_high = vol_low[at, :], vol_high[at, :]
        return (
            (0.5 * time_step) * s_low * s_low * start_low[at, :],
            (0.5 * time_step) * s_high * s_high * start_high[at, :],
        )

    def emit(k, v, prev, nxt, mixed, inner):
        spread = mixed + (prev + nxt - 2.0 * v) + inner
        lines = raw[k - 1] + raw[k + 1] - 2.0 * raw[k]
        out[k] = raw[k] + spread + tail[k] - damping * lines

    sweep(PLANES, plane, rows, emit, True)


def finish(index, start, start_low, start_high, vol, low, high, vol_low, vol_high, tail):
    bx, by, bz = vol.shape
    return pl.pallas_call(
        functools.partial(adjoint_kernel, blocks=bx // PLANES),
        grid_spec=pltpu.PrefetchScalarGridSpec(
            num_scalar_prefetch=1,
            grid=(bx // PLANES,),
            in_specs=[whole(start.shape), whole(start_low.shape), whole(start_high.shape)]
            + plane_specs(natural, bx - 1, vol.shape)
            + [whole(low.shape), whole(high.shape), whole(vol_low.shape), whole(vol_high.shape)]
            + [pl.BlockSpec((PLANES, by, bz), lambda s, i: (s, 0, 0))],
            out_specs=pl.BlockSpec((PLANES, by, bz), lambda s, i: (s, 0, 0)),
        ),
        out_shape=jax.ShapeDtypeStruct(vol.shape, F32),
        compiler_params=params(40),
        cost_estimate=cost(5e9, 17),
        name="adjoint",
    )(index, start, start_low, start_high, vol, vol, vol, low, high, vol_low, vol_high, tail)


def neighbours(low_edge, high_edge, axis):
    count = lax.axis_size(axis)
    up = [(k, k + 1) for k in range(count - 1)]
    down = [(k + 1, k) for k in range(count - 1)]
    return lax.ppermute(high_edge, axis, up), lax.ppermute(low_edge, axis, down)


def scatter_pieces(pieces, order=(2, 1, 3)):
    n = len(pieces)
    result = [pieces[0]] + [None] * (n - 1)
    for d in sorted(range(1, n), key=lambda d: -min(d, n - d)):
        result[d] = lax.ppermute(pieces[d], "narrow", [(k, (k + d) % n) for k in range(n)])
    return result


def across(piece):
    return lax.all_to_all(piece, "wide", split_axis=0, concat_axis=0, tiled=True)


def y_edges(chunks):
    return neighbours(chunks[0, :, 0, :], chunks[-1, :, -1, :], "narrow")


def on_device_kernels(state, volatility, cotangent, solve_first, solve_second, solve_third, patch_index):
    n, wide = lax.axis_size("narrow"), lax.axis_size("wide")
    here = lax.axis_index("narrow")
    index = here.astype(jnp.int32).reshape(1)
    bx, by, bz = state.shape
    xs = bx // n
    groups = PATCHES // 128

    ahead = (here + jnp.arange(n)) % n
    back = (here - jnp.arange(n)) % n

    cot_pieces = [lax.dynamic_slice_in_dim(cotangent, ahead[d] * xs, xs, 0) for d in range(n)]
    cot_lines = scatter_pieces(cot_pieces)

    both_low, both_high = neighbours(
        jnp.stack([state[0], volatility[0]]), jnp.stack([state[-1], volatility[-1]]), "wide"
    )
    both = jnp.stack([state[:, :: by - 1], volatility[:, :: by - 1]])
    both = jnp.concatenate([both_low[:, None, :: by - 1], both, both_high[:, None, :: by - 1]], axis=1)
    y_low, y_high = neighbours(both[:, :, 0], both[:, :, 1], "narrow")
    state_x = (both_low[0:1], both_high[0:1])
    vol_x = (both_low[1:2], both_high[1:2])
    state_y = (y_low[0], y_high[0])
    vol_y = (y_low[1], y_high[1])

    second_t = solve_second.T.reshape(n, by, n, by)
    second_t3 = left_form(second_t[ahead][:, :, back].reshape(n * by, n * by))
    second_n = solve_second.reshape(n * by, n, by)
    second_n3 = left_form(second_n[:, back].reshape(n * by, n * by))
    third_t3 = right_form(solve_third)
    third_n3 = right_form(solve_third.T)
    first_n3 = left_form(solve_first)
    first_t = solve_first.T.reshape(wide * bx, wide, n, xs)
    first_t3 = left_form(first_t[:, :, back].transpose(0, 2, 1, 3).reshape(wide * bx, wide * bx))

    a, source = forward(index, state, volatility, *state_x, *state_y, wide)
    solved = across(first([across(a)], first_n3, 0))

    back_second = scatter_pieces(second(cot_lines, second_t3, third_t3, wide))
    carried = across(first([across(piece) for piece in back_second], first_t3, 1))

    level = second(scatter_pieces(lifted(index, solved, state, *state_y, n)), second_n3, third_n3, 0)[0]
    count = n * wide
    joint = ("wide", "narrow")
    level_low = lax.ppermute(level[-1:], joint, [(k, k + 1) for k in range(count - 1)])
    level_high = lax.ppermute(level[:1], joint, [(k + 1, k) for k in range(count - 1)])
    drift_pieces = mix(index, level, level_low, level_high, n)

    def frozen_rows(rows):
        padded = jnp.pad(rows, ((0, 0), (1, 1)))
        curved = padded[:, 2:] + padded[:, :-2] - 2.0 * rows
        return rows + damping * jnp.dot(curved, solve_third.T, precision=lax.Precision.HIGHEST)

    frozen_part = frozen(index, state, *state_x, frozen_rows(state_y[0]), frozen_rows(state_y[1]), third_n3)

    carried_y = y_edges(carried)
    totals = react(index, carried, *carried_y, volatility, *vol_x, *vol_y, cotangent, n)
    uppers = scatter_pieces(second(scatter_pieces(totals), second_t3, third_t3, wide))
    start = across(first([across(piece) for piece in uppers], first_t3, 1))

    drifts = scatter_pieces(drift_pieces)
    order = (here - jnp.arange(n)) % n
    edge_low = jnp.stack([piece[0, :, 0] for piece in uppers])[order].reshape(bx, bz)
    edge_high = jnp.stack([piece[-1, :, -1] for piece in uppers])[order].reshape(bx, bz)
    upper_y = neighbours(edge_low, edge_high, "narrow")
    tail = gather_lines(index, totals, uppers, cotangent, *upper_y, third_t3)

    patch_t = patch_index[:, :, None]
    sums = drift_sums(index, drifts, frozen_part, carried, volatility, patch_index, patch_t, groups)
    sums = source_sums(index, start, source, patch_index, patch_t, sums)
    sums = (sums[:, :128] + sums[:, 128:]).reshape(count, PATCHES // count)
    shares = lax.all_to_all(sums, joint, split_axis=0, concat_axis=0, tiled=True)
    vega = jnp.sum(shares, axis=0)

    start_y = y_edges(start)
    adjoint = finish(index, start, *start_y, volatility, *vol_x, *vol_y, tail)
    return (adjoint, vega * vega_scale)


def on_device(*args):
    n, wide = lax.axis_size("narrow"), lax.axis_size("wide")
    bx, by, bz = args[0].shape
    aligned = bx % (n * PLANES) == 0 and by % 128 == 0 and by % (wide * 8) == 0 and bz == 128
    aligned = aligned and PATCHES % (n * wide) == 0 and by // wide % 2 == 0
    return on_device_kernels(*args) if aligned else on_device_plain(*args)


def solution(mesh):
    placed = (
        P("wide", "narrow", None),
        P("wide", "narrow", None),
        P("wide", "narrow", None),
        P(),
        P(),
        P(),
        P("wide", "narrow"),
    )
    return jax.shard_map(
        on_device,
        mesh=mesh,
        in_specs=placed,
        out_specs=(P("wide", "narrow", None), P(("wide", "narrow"))),
        check_vma=False,
    )
```

```python
import functools
import jax
import jax.numpy as jnp
from jax import lax
from jax.experimental import pallas as pl
from jax.experimental.pallas import tpu as pltpu
from jax.sharding import PartitionSpec as P

PATCHES = 3072


time_step = 0.4
theta_weight = 0.5
frozen_coef = 0.2
correction = 0.5 * 0.4
vega_scale = 1.0 / 32.0
correlations = ((0, 1, 0.5), (0, 2, 0.3), (1, 2, -0.4))


def padded_2(cells, sides, width):
    for axis, dim in sides:
        count = lax.axis_size(axis)
        ends = count - 1
        head = lax.slice_in_dim(cells, 0, width, axis=dim)
        tail = lax.slice_in_dim(cells, cells.shape[dim] - width, cells.shape[dim], axis=dim)
        cells = jnp.concatenate(
            [
                lax.ppermute(tail, axis, [(i, (i + 1) % count) for i in range(ends)]),
                cells,
                lax.ppermute(head, axis, [((i + 1) % count, i) for i in range(ends)]),
            ],
            axis=dim,
        )
    return cells


def along_third(values, offset):
    if offset == 0:
        return values
    zero_layer = jnp.zeros_like(values[..., :1])
    if offset > 0:
        return jnp.concatenate([values[..., 1:], zero_layer], axis=-1)
    return jnp.concatenate([zero_layer, values[..., :-1]], axis=-1)


def shifted(padded, offsets):
    lead = padded.ndim - 3
    slices = [slice(None)] * lead
    for position in range(2):
        offset = offsets[position]
        length = padded.shape[lead + position]
        slices.append(slice(1 + offset, length - 1 + offset))
    slices.append(slice(None))
    return along_third(padded[tuple(slices)], offsets[2])


def second_parts(padded):
    centre = shifted(padded, [0, 0, 0])
    result = []
    for axis_number in range(3):
        upward = [0, 0, 0]
        upward[axis_number] = 1
        downward = [0, 0, 0]
        downward[axis_number] = -1
        result.append(shifted(padded, upward) + shifted(padded, downward) - 2.0 * centre)
    return tuple(result)


def cross_term(padded, first_axis, second_axis):

    def corner(sign_first, sign_second):
        offsets = [0, 0, 0]
        offsets[first_axis] = sign_first
        offsets[second_axis] = sign_second
        return shifted(padded, offsets)

    return 0.25 * (corner(1, 1) - corner(1, -1) - corner(-1, 1) + corner(-1, -1))


def mixed_of(padded):
    total = None
    for first_axis, second_axis, weight in correlations:
        term = weight * cross_term(padded, first_axis, second_axis)
        total = term if total is None else total + term
    return total


def contract(matrix, field, axis_number, transposed):
    letters = "xyz"
    source = letters[axis_number]
    matrix_form = source + "w" if transposed else "w" + source
    result_form = letters.replace(source, "w")
    return jnp.einsum(
        matrix_form + "," + letters + "->" + result_form,
        matrix,
        field,
        precision=lax.Precision.HIGHEST,
    )


def line_x(field, matrix, transposed):

    def solve_lines(pieces):
        solved = contract(matrix, pieces, 0, transposed)
        return lax.all_to_all(solved, "wide", split_axis=0, concat_axis=1, tiled=True)

    return solve_lines(lax.all_to_all(field, "wide", split_axis=1, concat_axis=0, tiled=True))


def line_y(field, matrix, transposed):

    def solve_lines(pieces):
        solved = contract(matrix, pieces, 1, transposed)
        return lax.all_to_all(solved, "narrow", split_axis=1, concat_axis=2, tiled=True)

    return solve_lines(lax.all_to_all(field, "narrow", split_axis=2, concat_axis=1, tiled=True))


def rimmed(stacked):
    return padded_2(stacked, (("wide", 1), ("narrow", 2)), 1)


def third_second(field):
    return along_third(field, 1) + along_third(field, -1) - 2.0 * field


def on_device_plain(state, volatility, cotangent, solve_first, solve_second, solve_third, patch_index):
    coefficient = 0.5 * volatility * volatility
    padded = rimmed(state[None])
    parts = second_parts(padded)
    second_x, second_y, second_z = (parts[0][0], parts[1][0], parts[2][0])
    source = mixed_of(padded)[0] + second_x + second_y + second_z
    start = state + time_step * coefficient * source
    damping = theta_weight * time_step * frozen_coef
    level = line_x(start - damping * second_x, solve_first, False)
    level = line_y(level - damping * second_y, solve_second, False)
    level = contract(solve_third, level - damping * second_z, 2, False)
    drift = mixed_of(rimmed((level - state)[None]))[0]
    back_third = contract(solve_third, cotangent, 2, True)
    back_second = line_y(back_third, solve_second, True)
    carried = line_x(back_second, solve_first, True)
    reaction = mixed_of(rimmed((correction * coefficient * carried)[None]))[0]
    total = cotangent + reaction
    upper_third = contract(solve_third, total, 2, True)
    upper_second = line_y(upper_third, solve_second, True)
    adjoint_start = line_x(upper_second, solve_first, True)
    scaled = time_step * coefficient * adjoint_start
    padded = rimmed(jnp.stack([scaled, adjoint_start, upper_second]))
    parts = second_parts(padded)
    spread = mixed_of(padded[0:1])[0] + parts[0][0] + parts[1][0] + parts[2][0]
    lines = parts[0][1] + parts[1][2] + third_second(upper_third)
    adjoint = adjoint_start + spread - reaction - damping * lines
    sensitivity = volatility * (correction * carried * drift + time_step * adjoint_start * source)
    column = jnp.sum(sensitivity, axis=2)
    partial_sums = jax.ops.segment_sum(
        column.reshape(-1), patch_index.reshape(-1), num_segments=PATCHES
    )
    vega = lax.psum_scatter(partial_sums, ("wide", "narrow"), scatter_dimension=0, tiled=True)
    return (adjoint, vega * vega_scale)


F32 = jnp.float32
BF16 = jnp.bfloat16
damping = 0.5 * 0.4 * 0.2
MIB = 1024 * 1024
PLANES = 8


def params(mib):
    return pltpu.CompilerParams(vmem_limit_bytes=60 * MIB)


def cost(flops, mib):
    return pl.CostEstimate(flops=int(flops / 50), bytes_accessed=int(mib * MIB / 50), transcendentals=0)


def halves(x):
    high = lax.reduce_precision(x, 8, 7)
    return high.astype(BF16), (x - high).astype(BF16)


def left_form(matrix):
    high, low = halves(matrix)
    return jnp.concatenate([high, high, low], axis=1)


def right_form(matrix):
    high, low = halves(matrix)
    return jnp.concatenate([high, high, low], axis=0)


def split(x):
    high = x.astype(BF16)
    return high, (x - high.astype(F32)).astype(BF16)


def left_product(matrix3, field):
    high, low = split(field)
    return jnp.dot(matrix3, jnp.concatenate([high, low, high], axis=0), preferred_element_type=F32)


def right_product(field, matrix3):
    high, low = split(field)
    return jnp.dot(jnp.concatenate([high, low, high], axis=1), matrix3, preferred_element_type=F32)


def y_pair(v, low_row, high_row):
    n = v.shape[0]
    row = lax.broadcasted_iota(jnp.int32, v.shape, 0)
    up = jnp.where(row == n - 1, high_row, pltpu.roll(v, n - 1, 0))
    down = jnp.where(row == 0, low_row, pltpu.roll(v, 1, 0))
    return up, down


def z_pair(v):
    n = v.shape[1]
    lane = lax.broadcasted_iota(jnp.int32, v.shape, 1)
    up = jnp.where(lane == n - 1, 0.0, pltpu.roll(v, n - 1, 1))
    down = jnp.where(lane == 0, 0.0, pltpu.roll(v, 1, 1))
    return up, down


def sweep(count, plane, rows, emit, full):
    v, p, rest, inner = {}, {}, {}, {}
    for k in range(-1, count + 1):
        centre = plane(k)
        y_up, y_down = y_pair(centre, *rows(k))
        z_up, z_down = z_pair(centre)
        e = y_up - y_down
        v[k] = centre
        p[k] = 0.125 * e + 0.075 * (z_up - z_down)
        if 0 <= k < count:
            e_up, e_down = z_pair(e)
            rest[k] = -0.1 * (e_up - e_down)
            if full:
                inner[k] = (y_up + y_down) + (z_up + z_down) - 4.0 * centre
        if k >= 1:
            mixed = (p[k] - p[k - 2]) + rest[k - 1]
            emit(k - 1, v[k - 1], v[k - 2], v[k], mixed, inner.get(k - 1))


def chunk_plane(ref, x):
    value = ref[:, x]
    return value.reshape(value.shape[0] * value.shape[1], value.shape[2])


def plane_specs(step_block, last, shape):
    tail = shape[1:]
    return [
        pl.BlockSpec((PLANES,) + tail, lambda s, i: (step_block(s, i), 0, 0)),
        pl.BlockSpec((1,) + tail, lambda s, i: (jnp.maximum(step_block(s, i) * PLANES - 1, 0), 0, 0)),
        pl.BlockSpec((1,) + tail, lambda s, i: (jnp.minimum(step_block(s, i) * PLANES + PLANES, last), 0, 0)),
    ]


def whole(shape):
    return pl.BlockSpec(shape, lambda s, i: (0,) * len(shape))


def pick_plane(k, count, block, main, before, after, low, high, blocks):
    if k < 0:
        return jnp.where(block == 0, low[0], before[0])
    if k >= count:
        return jnp.where(block == blocks - 1, high[0], after[0])
    return main[k]


def natural(s, i):
    return s


def rotated(per, n):
    def block(s, i):
        return lax.rem(i[0] + s // per, n) * per + lax.rem(s, per)

    return block


def piece_map(d, per):
    return lambda s: jnp.clip(s - d * per, 0, per - 1)


def forward_kernel(i, state, before, after, low, high, y_low, y_high, volatility, a_out, source_out, *, blocks):
    block = pl.program_id(0)

    def emit(k, v, prev, nxt, mixed, inner):
        second_x = prev + nxt - 2.0 * v
        source = mixed + second_x + inner
        sigma = volatility[k]
        a = v + (time_step * 0.5) * sigma * sigma * source - damping * second_x
        a_out[:, k] = a.reshape(a_out.shape[0], a_out.shape[2], a_out.shape[3])
        source_out[k] = time_step * sigma * source

    sweep(
        PLANES,
        lambda k: pick_plane(k, PLANES, block, state, before, after, low, high, blocks),
        lambda k: (y_low[pl.ds(block * PLANES + k + 1, 1), :], y_high[pl.ds(block * PLANES + k + 1, 1), :]),
        emit,
        True,
    )


def forward(index, state, volatility, low, high, y_low, y_high, wide):
    bx, by, bz = state.shape
    blocks = bx // PLANES
    return pl.pallas_call(
        functools.partial(forward_kernel, blocks=blocks),
        grid_spec=pltpu.PrefetchScalarGridSpec(
            num_scalar_prefetch=1,
            grid=(blocks,),
            in_specs=plane_specs(natural, bx - 1, state.shape)
            + [whole(low.shape), whole(high.shape), whole(y_low.shape), whole(y_high.shape)]
            + [pl.BlockSpec((PLANES, by, bz), lambda s, i: (s, 0, 0))],
            out_specs=[
                pl.BlockSpec((wide, PLANES, by // wide, bz), lambda s, i: (0, s, 0, 0)),
                pl.BlockSpec((PLANES, by, bz), lambda s, i: (s, 0, 0)),
            ],
        ),
        out_shape=[
            jax.ShapeDtypeStruct((wide, bx, by // wide, bz), F32),
            jax.ShapeDtypeStruct(state.shape, F32),
        ],
        compiler_params=params(32),
        cost_estimate=cost(5e9, 17),
        name="forward",
    )(index, state, state, state, low, high, y_low, y_high, volatility)


def first_kernel(*refs, count, lines, parts, length, halo):
    pieces, matrix3, out = refs[:count], refs[count], refs[count + 1]
    depth = pieces[0].shape[0] // lines
    rows = length + 2 * halo

    def pair(step, carry):
        y = step * 2
        field = jnp.concatenate(
            [
                jnp.concatenate([piece[pl.ds(y + t, depth, stride=lines), :] for piece in pieces], axis=0)
                for t in range(2)
            ],
            axis=1,
        )
        solved = left_product(matrix3[...], field)
        width = solved.shape[1] // 2
        for t in range(2):
            half = solved[:, t * width : (t + 1) * width]
            for part in range(parts):
                base = part * rows
                out[pl.ds((base + halo) * lines + y + t, length, stride=lines), :] = half[part * length : (part + 1) * length]
                if halo:
                    zero = jnp.zeros((1, width), F32)
                    before = half[part * length - 1 : part * length] if part > 0 else zero
                    after = half[(part + 1) * length : (part + 1) * length + 1] if part < parts - 1 else zero
                    out[pl.ds(base * lines + y + t, 1), :] = before
                    out[pl.ds((base + rows - 1) * lines + y + t, 1), :] = after
        return carry

    lax.fori_loop(0, lines // 2, pair, 0)


def first(pieces, matrix3, halo):
    wide = pieces[0].shape[0]
    lines, bz = pieces[0].shape[2:]
    length = sum(piece.shape[1] for piece in pieces)
    rows = length + 2 * halo
    flat = [piece.reshape(-1, bz) for piece in pieces]
    out = pl.pallas_call(
        functools.partial(first_kernel, count=len(flat), lines=lines, parts=wide, length=length, halo=halo),
        in_specs=[pl.BlockSpec(memory_space=pltpu.VMEM)] * (len(flat) + 1),
        out_specs=pl.BlockSpec(memory_space=pltpu.VMEM),
        out_shape=jax.ShapeDtypeStruct((wide * rows * lines, bz), F32),
        compiler_params=params(40),
        cost_estimate=cost(7e9, 10),
        name="first",
    )(*flat, matrix3)
    return out.reshape(wide, rows, lines, bz)


def second_kernel(*refs, count, chunked):
    pieces, second3, third3, outs = refs[:count], refs[count], refs[count + 1], refs[count + 2 :]
    per, by, bz = pieces[0].shape
    length = count * by
    field = jnp.concatenate([piece[x] for x in range(per) for piece in pieces], axis=0)
    field = right_product(field, third3[...])
    field = jnp.concatenate([field[x * length : (x + 1) * length] for x in range(per)], axis=1)
    solved = left_product(second3[...], field)
    for x in range(per):
        half = solved[:, x * bz : (x + 1) * bz]
        if chunked:
            for d in range(count):
                out = outs[d]
                out[:, x] = half[d * by : (d + 1) * by].reshape(out.shape[0], out.shape[2], bz)
        else:
            outs[0][x] = half


def second(pieces, second3, third3, wide):
    count = len(pieces)
    xs, by, bz = pieces[0].shape
    per = 2
    if wide:
        out_specs = [pl.BlockSpec((wide, per, by // wide, bz), lambda s: (0, s, 0, 0))] * count
        out_shape = [jax.ShapeDtypeStruct((wide, xs, by // wide, bz), F32)] * count
    else:
        out_specs = [pl.BlockSpec((per, count * by, bz), lambda s: (s, 0, 0))]
        out_shape = [jax.ShapeDtypeStruct((xs, count * by, bz), F32)]
    return pl.pallas_call(
        functools.partial(second_kernel, count=count, chunked=bool(wide)),
        grid=(xs // per,),
        in_specs=[pl.BlockSpec((per, by, bz), lambda s: (s, 0, 0))] * count
        + [pl.BlockSpec(second3.shape, lambda s: (0, 0)), pl.BlockSpec(third3.shape, lambda s: (0, 0))],
        out_specs=out_specs,
        out_shape=out_shape,
        compiler_params=params(40),
        cost_estimate=cost(9e9, 10),
        name="second",
    )(*pieces, second3, third3)


def piece_specs(size, tail, per, n):
    return [pl.BlockSpec((size,) + tail, lambda s, i, d=d: (jnp.clip(s - d * per, 0, per - 1), 0, 0)) for d in range(n)]


def chunk_piece_specs(wide, lines, bz, per, order):
    return [
        pl.BlockSpec((wide, PLANES, lines, bz), lambda s, i, d=d: (0, jnp.clip(s - d * per, 0, per - 1), 0, 0))
        for d in order
    ]


def store_piece(outs, turn, kept):
    for d, out in enumerate(outs):

        @pl.when(turn == d)
        def _(out=out):
            out[...] = kept[...]


def select(values, turn):
    result = values[0]
    for d in range(1, len(values)):
        result = jnp.where(turn == d, values[d], result)
    return result


def lifted_kernel(i, solved, state, low, high, y_low, y_high, *refs, per, n, size, xs):
    outs, kept = refs[:n], refs[n]
    step = pl.program_id(0)
    bx = state.shape[0]
    base = lax.rem(i[0] + step // per, n) * xs + lax.rem(step, per) * size
    for k in range(size):
        row = base + k
        v = state[jnp.clip(row - 1, 0, bx - 1)]
        v = jnp.where(row == 0, low[0], jnp.where(row == bx + 1, high[0], v))
        up, down = y_pair(v, y_low[pl.ds(row, 1), :], y_high[pl.ds(row, 1), :])
        kept[k] = chunk_plane(solved, row) - damping * (up + down - 2.0 * v)
    store_piece(outs, step // per, kept)


def lifted(index, solved, state, low, high, y_low, y_high, n):
    bx, by, bz = state.shape
    xs = bx // n
    size = next(k for k in range(9, 0, -1) if (xs + 2) % k == 0)
    per = (xs + 2) // size
    return pl.pallas_call(
        functools.partial(lifted_kernel, per=per, n=n, size=size, xs=xs),
        grid_spec=pltpu.PrefetchScalarGridSpec(
            num_scalar_prefetch=1,
            grid=(n * per,),
            in_specs=[whole(v.shape) for v in (solved, state, low, high, y_low, y_high)],
            out_specs=piece_specs(size, (by, bz), per, n),
            scratch_shapes=[pltpu.VMEM((size, by, bz), F32)],
        ),
        out_shape=[jax.ShapeDtypeStruct((xs + 2, by, bz), F32)] * n,
        compiler_params=params(32),
        cost_estimate=cost(2e9, 13),
        name="lifted",
    )(index, solved, state, low, high, y_low, y_high)


def reaction_kernel(
    i, carried, carried_low, carried_high, vol, before, after, low, high, vol_low, vol_high, cotangent, *refs, per, n, blocks
):
    outs, kept = refs[:n], refs[n]
    step = pl.program_id(0)
    block = rotated(per, n)(step, i)

    def plane(k):
        sigma = pick_plane(k, PLANES, block, vol, before, after, low, high, blocks)
        return (0.5 * correction) * sigma * sigma * chunk_plane(carried, block * PLANES + k + 1)

    def rows(k):
        at = pl.ds(block * PLANES + k + 1, 1)
        s_low, s_high = vol_low[at, :], vol_high[at, :]
        return (
            (0.5 * correction) * s_low * s_low * carried_low[at, :],
            (0.5 * correction) * s_high * s_high * carried_high[at, :],
        )

    def emit(k, v, prev, nxt, mixed, inner):
        kept[k] = cotangent[k] + mixed

    sweep(PLANES, plane, rows, emit, False)
    store_piece(outs, step // per, kept)


def react(index, carried, carried_low, carried_high, vol, low, high, vol_low, vol_high, cotangent, n):
    bx, by, bz = vol.shape
    xs = bx // n
    per = xs // PLANES
    block = rotated(per, n)
    return pl.pallas_call(
        functools.partial(reaction_kernel, per=per, n=n, blocks=bx // PLANES),
        grid_spec=pltpu.PrefetchScalarGridSpec(
            num_scalar_prefetch=1,
            grid=(n * per,),
            in_specs=[whole(carried.shape), whole(carried_low.shape), whole(carried_high.shape)]
            + plane_specs(block, bx - 1, vol.shape)
            + [whole(low.shape), whole(high.shape), whole(vol_low.shape), whole(vol_high.shape)]
            + [pl.BlockSpec((PLANES, by, bz), lambda s, i: (block(s, i), 0, 0))],
            out_specs=piece_specs(PLANES, (by, bz), per, n),
            scratch_shapes=[pltpu.VMEM((PLANES, by, bz), F32)],
        ),
        out_shape=[jax.ShapeDtypeStruct((xs, by, bz), F32)] * n,
        compiler_params=params(40),
        cost_estimate=cost(4e9, 17),
        name="reaction",
    )(index, carried, carried_low, carried_high, vol, vol, vol, low, high, vol_low, vol_high, cotangent)


def lines_kernel(i, *refs, per, n):
    totals, uppers = refs[:n], refs[n : 2 * n]
    cotangent, upper_low, upper_high, third3, out = refs[2 * n :]
    step = pl.program_id(0)
    turn = step // per
    block = rotated(per, n)(step, i)
    for k in range(PLANES):
        total = select([ref[k] for ref in totals], turn)
        upper = select([chunk_plane(ref, k) for ref in uppers], turn)
        at = pl.ds(block * PLANES + k, 1)
        up, down = y_pair(upper, upper_low[at, :], upper_high[at, :])
        third = right_product(total, third3[...])
        z_up, z_down = z_pair(third)
        lines = (up + down - 2.0 * upper) + (z_up + z_down - 2.0 * third)
        out[k] = cotangent[k] - total - damping * lines


def gather_lines(index, totals, uppers, cotangent, upper_low, upper_high, third3):
    n = len(totals)
    bx, by, bz = cotangent.shape
    xs = bx // n
    per = xs // PLANES
    wide, lines = uppers[0].shape[0], uppers[0].shape[2]
    block = rotated(per, n)
    order = [(n - e) % n for e in range(n)]
    return pl.pallas_call(
        functools.partial(lines_kernel, per=per, n=n),
        grid_spec=pltpu.PrefetchScalarGridSpec(
            num_scalar_prefetch=1,
            grid=(n * per,),
            in_specs=piece_specs(PLANES, (by, bz), per, n)
            + chunk_piece_specs(wide, lines, bz, per, range(n))
            + [pl.BlockSpec((PLANES, by, bz), lambda s, i: (block(s, i), 0, 0))]
            + [whole(upper_low.shape), whole(upper_high.shape), whole(third3.shape)],
            out_specs=pl.BlockSpec((PLANES, by, bz), lambda s, i: (block(s, i), 0, 0)),
        ),
        out_shape=jax.ShapeDtypeStruct(cotangent.shape, F32),
        compiler_params=params(40),
        cost_estimate=cost(5e9, 17),
        name="lines",
    )(index, *totals, *[uppers[order[d]] for d in range(n)], cotangent, upper_low, upper_high, third3)


def mixed_kernel(i, field, *refs, n):
    outs, scratch = refs[:n], refs[n]
    by = outs[0].shape[1]

    def emit(k, v, prev, nxt, mixed, inner):
        scratch[...] = mixed
        for d, out in enumerate(outs):
            start = pl.multiple_of(lax.rem(i[0] + d, n) * by, by)
            out[k] = scratch[pl.ds(start, by), :]

    zero = jnp.zeros((1, field.shape[2]), F32)
    sweep(field.shape[0] - 2, lambda k: field[k + 1], lambda k: (zero, zero), emit, False)


def mix(index, field, n):
    rows, ny, bz = field.shape
    xs, by = rows - 2, ny // n
    return pl.pallas_call(
        functools.partial(mixed_kernel, n=n),
        grid_spec=pltpu.PrefetchScalarGridSpec(
            num_scalar_prefetch=1,
            grid=(1,),
            in_specs=[whole(field.shape)],
            out_specs=[whole((xs, by, bz))] * n,
            scratch_shapes=[pltpu.VMEM((ny, bz), F32)],
        ),
        out_shape=[jax.ShapeDtypeStruct((xs, by, bz), F32)] * n,
        compiler_params=params(40),
        cost_estimate=cost(4e9, 9),
        name="mixed",
    )(index, field)


def patch_sums(out, step, planes, patch, patch_t, groups):
    @pl.when(step == 0)
    def _():
        out[...] = jnp.zeros_like(out)

    acc = None
    ones = jnp.ones((planes[0].shape[1], 128), BF16)
    for k, value in enumerate(planes):
        value_high, value_low = split(value)
        column = jnp.dot(value_high, ones, preferred_element_type=F32) + jnp.dot(
            value_low, ones, preferred_element_type=F32
        )
        number = patch[pl.ds(k, 1), :]
        coarse = lax.broadcasted_iota(jnp.int32, (groups, number.shape[1]), 0) == lax.shift_right_logical(number, 7)
        number_t = patch_t[k]
        lane = lax.broadcasted_iota(jnp.int32, (number_t.shape[0], 128), 1)
        fine = jnp.where(lane == lax.bitwise_and(number_t, 127), column, 0.0)
        high, low = split(fine)
        term = jnp.dot(
            jnp.where(coarse, 1.0, 0.0).astype(BF16), jnp.concatenate([high, low], axis=1), preferred_element_type=F32
        )
        acc = term if acc is None else acc + term
    out[...] += acc


def frozen_kernel(
    i, state, before, after, low, high, q_low, q_high, third3, vol, carried, patch, patch_t, weight, out, *, blocks, groups
):
    block = pl.program_id(0)
    planes = []

    def plane(k):
        v = pick_plane(k, PLANES, block, state, before, after, low, high, blocks)
        up, down = z_pair(v)
        return v + damping * right_product(up + down - 2.0 * v, third3[...])

    def emit(k, v, prev, nxt, mixed, inner):
        w = correction * vol[k] * chunk_plane(carried, block * PLANES + k + 1)
        weight[k] = w
        planes.append(-w * mixed)

    sweep(
        PLANES,
        plane,
        lambda k: (q_low[pl.ds(block * PLANES + k + 1, 1), :], q_high[pl.ds(block * PLANES + k + 1, 1), :]),
        emit,
        False,
    )
    patch_sums(out, block, planes, patch, patch_t, groups)


def frozen(index, state, low, high, q_low, q_high, third3, vol, carried, patch, patch_t, groups):
    bx, by, bz = state.shape
    blocks = bx // PLANES
    main = pl.BlockSpec((PLANES, by, bz), lambda s, i: (s, 0, 0))
    return pl.pallas_call(
        functools.partial(frozen_kernel, blocks=blocks, groups=groups),
        grid_spec=pltpu.PrefetchScalarGridSpec(
            num_scalar_prefetch=1,
            grid=(blocks,),
            in_specs=plane_specs(natural, bx - 1, state.shape)
            + [whole(low.shape), whole(high.shape), whole(q_low.shape), whole(q_high.shape), whole(third3.shape)]
            + [main, whole(carried.shape)]
            + [pl.BlockSpec((PLANES, by), lambda s, i: (s, 0))]
            + [pl.BlockSpec((PLANES, by, 1), lambda s, i: (s, 0, 0))],
            out_specs=[main, whole((groups, 256))],
        ),
        out_shape=[jax.ShapeDtypeStruct(state.shape, F32), jax.ShapeDtypeStruct((groups, 256), F32)],
        compiler_params=params(32),
        cost_estimate=cost(5e9, 17),
        name="frozen",
    )(index, state, state, state, low, high, q_low, q_high, third3, vol, carried, patch, patch_t)


def column_kernel(i, *refs, per, n, groups):
    drifts = refs[:n]
    weight, source, start, patch, patch_t, given, out = refs[n:]
    step = pl.program_id(0)
    turn = step // per
    block = rotated(per, n)(step, i)
    planes = [
        weight[k] * select([ref[k] for ref in drifts], turn)
        + source[k] * chunk_plane(start, block * PLANES + k + 1)
        for k in range(PLANES)
    ]
    patch_sums(out, step, planes, patch, patch_t, groups)

    @pl.when(step == pl.num_programs(0) - 1)
    def _():
        out[...] += given[...]


def column_sums(index, drifts, weight, source, start, patch, patch_t, given):
    n = len(drifts)
    bx, by, bz = source.shape
    xs = bx // n
    per = xs // PLANES
    groups = given.shape[0]
    block = rotated(per, n)
    order = [(n - e) % n for e in range(n)]
    main = pl.BlockSpec((PLANES, by, bz), lambda s, i: (block(s, i), 0, 0))
    return pl.pallas_call(
        functools.partial(column_kernel, per=per, n=n, groups=groups),
        grid_spec=pltpu.PrefetchScalarGridSpec(
            num_scalar_prefetch=1,
            grid=(n * per,),
            in_specs=piece_specs(PLANES, (by, bz), per, n)
            + [main, main, whole(start.shape)]
            + [pl.BlockSpec((PLANES, by), lambda s, i: (block(s, i), 0))]
            + [pl.BlockSpec((PLANES, by, 1), lambda s, i: (block(s, i), 0, 0)), whole(given.shape)],
            out_specs=whole(given.shape),
        ),
        out_shape=jax.ShapeDtypeStruct(given.shape, F32),
        compiler_params=params(40),
        cost_estimate=cost(4e9, 17),
        name="column",
    )(index, *[drifts[order[d]] for d in range(n)], weight, source, start, patch, patch_t, given)


def adjoint_kernel(
    i, start, start_low, start_high, vol, before, after, low, high, vol_low, vol_high, tail, out, *, blocks
):
    block = pl.program_id(0)
    raw = {}

    def plane(k):
        sigma = pick_plane(k, PLANES, block, vol, before, after, low, high, blocks)
        raw[k] = chunk_plane(start, block * PLANES + k + 1)
        return (0.5 * time_step) * sigma * sigma * raw[k]

    def rows(k):
        at = pl.ds(block * PLANES + k + 1, 1)
        s_low, s_high = vol_low[at, :], vol_high[at, :]
        return (
            (0.5 * time_step) * s_low * s_low * start_low[at, :],
            (0.5 * time_step) * s_high * s_high * start_high[at, :],
        )

    def emit(k, v, prev, nxt, mixed, inner):
        spread = mixed + (prev + nxt - 2.0 * v) + inner
        lines = raw[k - 1] + raw[k + 1] - 2.0 * raw[k]
        out[k] = raw[k] + spread + tail[k] - damping * lines

    sweep(PLANES, plane, rows, emit, True)


def finish(index, start, start_low, start_high, vol, low, high, vol_low, vol_high, tail):
    bx, by, bz = vol.shape
    return pl.pallas_call(
        functools.partial(adjoint_kernel, blocks=bx // PLANES),
        grid_spec=pltpu.PrefetchScalarGridSpec(
            num_scalar_prefetch=1,
            grid=(bx // PLANES,),
            in_specs=[whole(start.shape), whole(start_low.shape), whole(start_high.shape)]
            + plane_specs(natural, bx - 1, vol.shape)
            + [whole(low.shape), whole(high.shape), whole(vol_low.shape), whole(vol_high.shape)]
            + [pl.BlockSpec((PLANES, by, bz), lambda s, i: (s, 0, 0))],
            out_specs=pl.BlockSpec((PLANES, by, bz), lambda s, i: (s, 0, 0)),
        ),
        out_shape=jax.ShapeDtypeStruct(vol.shape, F32),
        compiler_params=params(40),
        cost_estimate=cost(5e9, 17),
        name="adjoint",
    )(index, start, start_low, start_high, vol, vol, vol, low, high, vol_low, vol_high, tail)


def neighbours(low_edge, high_edge, axis):
    count = lax.axis_size(axis)
    up = [(k, k + 1) for k in range(count - 1)]
    down = [(k + 1, k) for k in range(count - 1)]
    return lax.ppermute(high_edge, axis, up), lax.ppermute(low_edge, axis, down)


def far_and_near(n):
    return [n // 2] if n > 1 else [], [d for d in range(1, n) if d != n // 2]


def send(pieces, chosen, *earlier):
    n = len(pieces)
    result = list(pieces)
    for d in chosen:
        piece = after(pieces[d], *earlier) if earlier else pieces[d]
        result[d] = lax.ppermute(piece, "narrow", [(k, (k + d) % n) for k in range(n)])
    return result


def pick(pieces, chosen):
    return [pieces[d] for d in chosen]


def after(value, *earlier):
    return lax.optimization_barrier((value, earlier))[0]


def across(piece):
    return lax.all_to_all(piece, "wide", split_axis=0, concat_axis=0, tiled=True)


def cross_both(pieces, before, between, near, far):
    lines = list(pieces)
    met = send(pieces, near)
    for d in near:
        lines[d] = met[d]
    chunks = [across(pieces[0])] + [None] * (len(pieces) - 1)
    met, chunks[0], waiting = lax.optimization_barrier((pick(lines, near), chunks[0], pick(pieces, far)))
    for d, value in zip(near, met):
        lines[d] = value
    rest = list(pieces)
    for d, value in zip(far, waiting):
        rest[d] = value
    arrived = send(rest, far)
    last = chunks[0]
    for d in near:
        chunks[d] = last = across(after(lines[d], last, *before))
    gone = pick(arrived, far)
    for d in far:
        lines[d] = arrived[d]
        chunks[d] = across(after(arrived[d], last, *between))
    return lines, chunks, gone


def y_edges(chunks):
    return neighbours(chunks[0, :, 0, :], chunks[-1, :, -1, :], "narrow")


def on_device_kernels(state, volatility, cotangent, solve_first, solve_second, solve_third, patch_index):
    n, wide = lax.axis_size("narrow"), lax.axis_size("wide")
    here = lax.axis_index("narrow")
    index = here.astype(jnp.int32).reshape(1)
    bx, by, bz = state.shape
    xs = bx // n
    groups = PATCHES // 128

    ahead = (here + jnp.arange(n)) % n
    back = (here - jnp.arange(n)) % n

    far, near = far_and_near(n)
    every = range(n)

    cot_pieces = [lax.dynamic_slice_in_dim(cotangent, ahead[d] * xs, xs, 0) for d in range(n)]
    early, late = near[:1], near[1:]
    cot_lines = send(cot_pieces, near)
    edge_state, edge_volatility = after((state, volatility), cot_pieces)

    both_low, both_high = neighbours(
        jnp.stack([edge_state[0], edge_volatility[0]]), jnp.stack([edge_state[-1], edge_volatility[-1]]), "wide"
    )
    both = jnp.stack([edge_state[:, :: by - 1], edge_volatility[:, :: by - 1]])
    both = jnp.concatenate([both_low[:, None, :: by - 1], both, both_high[:, None, :: by - 1]], axis=1)
    y_low, y_high = neighbours(both[:, :, 0], both[:, :, 1], "narrow")
    state_x = (both_low[0:1], both_high[0:1])
    vol_x = (both_low[1:2], both_high[1:2])
    state_y = (y_low[0], y_high[0])
    vol_y = (y_low[1], y_high[1])

    second_t = solve_second.T.reshape(n, by, n, by)
    second_t3 = left_form(second_t[ahead][:, :, back].reshape(n * by, n * by))
    second_n = solve_second.reshape(n * by, n, by)
    second_n3 = left_form(second_n[:, back].reshape(n * by, n * by))
    third_t3 = right_form(solve_third)
    third_n3 = right_form(solve_third.T)
    first_n3 = left_form(solve_first)
    first_t = solve_first.T.reshape(wide * bx, wide, n, xs)
    first_t3 = left_form(first_t[:, :, back].transpose(0, 2, 1, 3).reshape(wide * bx, wide * bx))

    state = after(state, *pick(cot_lines, early))
    a, source = forward(index, state, volatility, *state_x, *state_y, wide)
    a = after(a, *pick(cot_lines, late))
    cot_lines = send(cot_lines, far, *pick(cot_lines, near))
    back = second(cot_lines, second_t3, third_t3, wide)
    forward_lines = first([after(across(a), *back)], first_n3, 1)
    solved = across(forward_lines)

    lifted_pieces = lifted(index, solved, state, *state_x, *state_y, n)
    back, carried_chunks, gone = cross_both(back, (solved,), lifted_pieces, near, far)
    carried_lines = first(carried_chunks, first_t3, 1)
    level_lines = send(lifted_pieces, late, gone)
    carried = across(after(carried_lines, *pick(level_lines, late)))

    level_lines = send(level_lines, far, *pick(level_lines, late))
    carried = after(carried, *pick(level_lines, far))
    carried_y = y_edges(carried)
    level_lines = send(level_lines, early, *carried_y)
    totals = react(index, carried, *carried_y, volatility, *vol_x, *vol_y, cotangent, n)
    total_lines = send(totals, far + near)

    level = second(after(level_lines, totals), second_n3, third_n3, 0)[0]
    drift_pieces = mix(index, level, n)

    def frozen_rows(rows):
        padded = jnp.pad(rows, ((0, 0), (1, 1)))
        curved = padded[:, 2:] + padded[:, :-2] - 2.0 * rows
        return rows + damping * jnp.dot(curved, solve_third.T, precision=lax.Precision.HIGHEST)

    patch_t = patch_index[:, :, None]
    weight, sums = frozen(
        index,
        after(state, *drift_pieces),
        *state_x,
        frozen_rows(state_y[0]),
        frozen_rows(state_y[1]),
        third_n3,
        volatility,
        carried,
        patch_index,
        patch_t,
        groups,
    )

    total_lines = after(total_lines, drift_pieces, sums)
    drifts = send(drift_pieces, early, *total_lines)
    uppers = after(second(total_lines, second_t3, third_t3, wide), *pick(drifts, early))
    uppers, start_chunks, gone = cross_both(uppers, (), (), near, far)
    start_lines = first(start_chunks, first_t3, 1)
    drifts = send(drifts, late, gone)
    start = across(after(start_lines, *pick(drifts, late)))

    order = (here - jnp.arange(n)) % n
    edge_low = jnp.stack([piece[0, :, 0] for piece in uppers])[order].reshape(bx, bz)
    edge_high = jnp.stack([piece[-1, :, -1] for piece in uppers])[order].reshape(bx, bz)
    upper_y = neighbours(edge_low, edge_high, "narrow")
    drifts = send(drifts, far, *pick(drifts, late), *upper_y)
    tail = gather_lines(index, totals, uppers, cotangent, *upper_y, third_t3)

    start = after(start, tail)
    start_y = y_edges(start)
    start = after(start, *start_y)
    sums = column_sums(index, drifts, weight, source, start, patch_index, patch_t, sums)
    count, joint = n * wide, ("wide", "narrow")
    sums = (sums[:, :128] + sums[:, 128:]).reshape(count, PATCHES // count)
    shares = lax.all_to_all(sums, joint, split_axis=0, concat_axis=0, tiled=True)
    vega = jnp.sum(shares, axis=0)

    adjoint = finish(index, start, *start_y, volatility, *vol_x, *vol_y, tail)
    return (adjoint, vega * vega_scale)


def on_device(*args):
    n, wide = lax.axis_size("narrow"), lax.axis_size("wide")
    bx, by, bz = args[0].shape
    aligned = bx % (n * PLANES) == 0 and by % 128 == 0 and by % (wide * 8) == 0 and bz == 128
    aligned = aligned and PATCHES % (n * wide) == 0 and by // wide % 2 == 0
    return on_device_kernels(*args) if aligned else on_device_plain(*args)


def solution(mesh):
    placed = (
        P("wide", "narrow", None),
        P("wide", "narrow", None),
        P("wide", "narrow", None),
        P(),
        P(),
        P(),
        P("wide", "narrow"),
    )
    return jax.shard_map(
        on_device,
        mesh=mesh,
        in_specs=placed,
        out_specs=(P("wide", "narrow", None), P(("wide", "narrow"))),
        check_vma=False,
    )
```

```python
import functools
import jax
import jax.numpy as jnp
from jax import lax
from jax.experimental import pallas as pl
from jax.experimental.layout import Layout, with_layout_constraint
from jax.experimental.pallas import tpu as pltpu
from jax.sharding import PartitionSpec as P

PATCHES = 3072


time_step = 0.4
theta_weight = 0.5
frozen_coef = 0.2
correction = 0.5 * 0.4
vega_scale = 1.0 / 32.0
correlations = ((0, 1, 0.5), (0, 2, 0.3), (1, 2, -0.4))


def padded_2(cells, sides, width):
    for axis, dim in sides:
        count = lax.axis_size(axis)
        ends = count - 1
        head = lax.slice_in_dim(cells, 0, width, axis=dim)
        tail = lax.slice_in_dim(cells, cells.shape[dim] - width, cells.shape[dim], axis=dim)
        cells = jnp.concatenate(
            [
                lax.ppermute(tail, axis, [(i, (i + 1) % count) for i in range(ends)]),
                cells,
                lax.ppermute(head, axis, [((i + 1) % count, i) for i in range(ends)]),
            ],
            axis=dim,
        )
    return cells


def along_third(values, offset):
    if offset == 0:
        return values
    zero_layer = jnp.zeros_like(values[..., :1])
    if offset > 0:
        return jnp.concatenate([values[..., 1:], zero_layer], axis=-1)
    return jnp.concatenate([zero_layer, values[..., :-1]], axis=-1)


def shifted(padded, offsets):
    lead = padded.ndim - 3
    slices = [slice(None)] * lead
    for position in range(2):
        offset = offsets[position]
        length = padded.shape[lead + position]
        slices.append(slice(1 + offset, length - 1 + offset))
    slices.append(slice(None))
    return along_third(padded[tuple(slices)], offsets[2])


def second_parts(padded):
    centre = shifted(padded, [0, 0, 0])
    result = []
    for axis_number in range(3):
        upward = [0, 0, 0]
        upward[axis_number] = 1
        downward = [0, 0, 0]
        downward[axis_number] = -1
        result.append(shifted(padded, upward) + shifted(padded, downward) - 2.0 * centre)
    return tuple(result)


def cross_term(padded, first_axis, second_axis):

    def corner(sign_first, sign_second):
        offsets = [0, 0, 0]
        offsets[first_axis] = sign_first
        offsets[second_axis] = sign_second
        return shifted(padded, offsets)

    return 0.25 * (corner(1, 1) - corner(1, -1) - corner(-1, 1) + corner(-1, -1))


def mixed_of(padded):
    total = None
    for first_axis, second_axis, weight in correlations:
        term = weight * cross_term(padded, first_axis, second_axis)
        total = term if total is None else total + term
    return total


def contract(matrix, field, axis_number, transposed):
    letters = "xyz"
    source = letters[axis_number]
    matrix_form = source + "w" if transposed else "w" + source
    result_form = letters.replace(source, "w")
    return jnp.einsum(
        matrix_form + "," + letters + "->" + result_form,
        matrix,
        field,
        precision=lax.Precision.HIGHEST,
    )


def line_x(field, matrix, transposed):

    def solve_lines(pieces):
        solved = contract(matrix, pieces, 0, transposed)
        return lax.all_to_all(solved, "wide", split_axis=0, concat_axis=1, tiled=True)

    return solve_lines(lax.all_to_all(field, "wide", split_axis=1, concat_axis=0, tiled=True))


def line_y(field, matrix, transposed):

    def solve_lines(pieces):
        solved = contract(matrix, pieces, 1, transposed)
        return lax.all_to_all(solved, "narrow", split_axis=1, concat_axis=2, tiled=True)

    return solve_lines(lax.all_to_all(field, "narrow", split_axis=2, concat_axis=1, tiled=True))


def rimmed(stacked):
    return padded_2(stacked, (("wide", 1), ("narrow", 2)), 1)


def third_second(field):
    return along_third(field, 1) + along_third(field, -1) - 2.0 * field


def on_device_plain(state, volatility, cotangent, solve_first, solve_second, solve_third, patch_index):
    coefficient = 0.5 * volatility * volatility
    padded = rimmed(state[None])
    parts = second_parts(padded)
    second_x, second_y, second_z = (parts[0][0], parts[1][0], parts[2][0])
    source = mixed_of(padded)[0] + second_x + second_y + second_z
    start = state + time_step * coefficient * source
    damping = theta_weight * time_step * frozen_coef
    level = line_x(start - damping * second_x, solve_first, False)
    level = line_y(level - damping * second_y, solve_second, False)
    level = contract(solve_third, level - damping * second_z, 2, False)
    drift = mixed_of(rimmed((level - state)[None]))[0]
    back_third = contract(solve_third, cotangent, 2, True)
    back_second = line_y(back_third, solve_second, True)
    carried = line_x(back_second, solve_first, True)
    reaction = mixed_of(rimmed((correction * coefficient * carried)[None]))[0]
    total = cotangent + reaction
    upper_third = contract(solve_third, total, 2, True)
    upper_second = line_y(upper_third, solve_second, True)
    adjoint_start = line_x(upper_second, solve_first, True)
    scaled = time_step * coefficient * adjoint_start
    padded = rimmed(jnp.stack([scaled, adjoint_start, upper_second]))
    parts = second_parts(padded)
    spread = mixed_of(padded[0:1])[0] + parts[0][0] + parts[1][0] + parts[2][0]
    lines = parts[0][1] + parts[1][2] + third_second(upper_third)
    adjoint = adjoint_start + spread - reaction - damping * lines
    sensitivity = volatility * (correction * carried * drift + time_step * adjoint_start * source)
    column = jnp.sum(sensitivity, axis=2)
    partial_sums = jax.ops.segment_sum(
        column.reshape(-1), patch_index.reshape(-1), num_segments=PATCHES
    )
    vega = lax.psum_scatter(partial_sums, ("wide", "narrow"), scatter_dimension=0, tiled=True)
    return (adjoint, vega * vega_scale)


F32 = jnp.float32
BF16 = jnp.bfloat16
damping = 0.5 * 0.4 * 0.2
MIB = 1024 * 1024
PLANES = 8


def params(mib):
    return pltpu.CompilerParams(vmem_limit_bytes=60 * MIB)


def cost(flops, mib):
    return pl.CostEstimate(flops=int(flops / 50), bytes_accessed=int(mib * MIB / 50), transcendentals=0)


def halves(x):
    high = lax.reduce_precision(x, 8, 7)
    return high.astype(BF16), (x - high).astype(BF16)


def left_form(matrix):
    high, low = halves(matrix)
    return jnp.concatenate([high, high, low], axis=1)


def right_form(matrix):
    high, low = halves(matrix)
    return jnp.concatenate([high, high, low], axis=0)


def split(x):
    high = x.astype(BF16)
    return high, (x - high.astype(F32)).astype(BF16)


def left_product(matrix3, field):
    high, low = split(field)
    return jnp.dot(matrix3, jnp.concatenate([high, low, high], axis=0), preferred_element_type=F32)


def right_product(field, matrix3):
    high, low = split(field)
    return jnp.dot(jnp.concatenate([high, low, high], axis=1), matrix3, preferred_element_type=F32)


def y_pair(v, low_row, high_row):
    n = v.shape[0]
    row = lax.broadcasted_iota(jnp.int32, (8, v.shape[1]), 0)
    up, down = pltpu.roll(v, n - 1, 0), pltpu.roll(v, 1, 0)
    up = jnp.concatenate([up[: n - 8], jnp.where(row == 7, high_row, up[n - 8 :])], axis=0)
    down = jnp.concatenate([jnp.where(row == 0, low_row, down[:8]), down[8:]], axis=0)
    return up, down


def z_pair(v):
    n = v.shape[1]
    lane = lax.broadcasted_iota(jnp.int32, v.shape, 1)
    up = jnp.where(lane == n - 1, 0.0, pltpu.roll(v, n - 1, 1))
    down = jnp.where(lane == 0, 0.0, pltpu.roll(v, 1, 1))
    return up, down


def sweep(count, plane, rows, emit, full):
    v, p, rest, inner = {}, {}, {}, {}
    for k in range(-1, count + 1):
        centre = plane(k)
        y_up, y_down = y_pair(centre, *rows(k))
        z_up, z_down = z_pair(centre)
        e = y_up - y_down
        v[k] = centre
        p[k] = 0.125 * e + 0.075 * (z_up - z_down)
        if 0 <= k < count:
            e_up, e_down = z_pair(e)
            rest[k] = -0.1 * (e_up - e_down)
            if full:
                inner[k] = (y_up + y_down) + (z_up + z_down) - 4.0 * centre
        if k >= 1:
            mixed = (p[k] - p[k - 2]) + rest[k - 1]
            emit(k - 1, v[k - 1], v[k - 2], v[k], mixed, inner.get(k - 1))


def chunk_plane(ref, x):
    value = ref[:, x]
    return value.reshape(value.shape[0] * value.shape[1], value.shape[2])


def plane_specs(step_block, last, shape):
    tail = shape[1:]
    return [
        pl.BlockSpec((PLANES,) + tail, lambda s, i: (step_block(s, i), 0, 0)),
        pl.BlockSpec((1,) + tail, lambda s, i: (jnp.maximum(step_block(s, i) * PLANES - 1, 0), 0, 0)),
        pl.BlockSpec((1,) + tail, lambda s, i: (jnp.minimum(step_block(s, i) * PLANES + PLANES, last), 0, 0)),
    ]


def whole(shape):
    return pl.BlockSpec(shape, lambda s, i: (0,) * len(shape))


def pick_plane(k, count, block, main, before, after, low, high, blocks):
    if k < 0:
        return jnp.where(block == 0, low[0], before[0])
    if k >= count:
        return jnp.where(block == blocks - 1, high[0], after[0])
    return main[k]


def natural(s, i):
    return s


def rotated(per, n):
    def block(s, i):
        return lax.rem(i[0] + s // per, n) * per + lax.rem(s, per)

    return block


def piece_map(d, per):
    return lambda s: jnp.clip(s - d * per, 0, per - 1)


def forward_kernel(i, state, before, after, low, high, y_low, y_high, volatility, a_out, source_out, *, blocks):
    block = pl.program_id(0)

    def emit(k, v, prev, nxt, mixed, inner):
        second_x = prev + nxt - 2.0 * v
        source = mixed + second_x + inner
        sigma = volatility[k]
        a = v + (time_step * 0.5) * sigma * sigma * source - damping * second_x
        a_out[:, k] = a.reshape(a_out.shape[0], a_out.shape[2], a_out.shape[3])
        source_out[k] = time_step * sigma * source

    sweep(
        PLANES,
        lambda k: pick_plane(k, PLANES, block, state, before, after, low, high, blocks),
        lambda k: (y_low[pl.ds(block * PLANES + k + 1, 1), :], y_high[pl.ds(block * PLANES + k + 1, 1), :]),
        emit,
        True,
    )


def forward(index, state, volatility, low, high, y_low, y_high, wide):
    bx, by, bz = state.shape
    blocks = bx // PLANES
    return pl.pallas_call(
        functools.partial(forward_kernel, blocks=blocks),
        grid_spec=pltpu.PrefetchScalarGridSpec(
            num_scalar_prefetch=1,
            grid=(blocks,),
            in_specs=plane_specs(natural, bx - 1, state.shape)
            + [whole(low.shape), whole(high.shape), whole(y_low.shape), whole(y_high.shape)]
            + [pl.BlockSpec((PLANES, by, bz), lambda s, i: (s, 0, 0))],
            out_specs=[
                pl.BlockSpec((wide, PLANES, by // wide, bz), lambda s, i: (0, s, 0, 0)),
                pl.BlockSpec((PLANES, by, bz), lambda s, i: (s, 0, 0)),
            ],
        ),
        out_shape=[
            jax.ShapeDtypeStruct((wide, bx, by // wide, bz), F32),
            jax.ShapeDtypeStruct(state.shape, F32),
        ],
        compiler_params=params(32),
        cost_estimate=cost(5e9, 17),
        name="forward",
    )(index, state, state, state, low, high, y_low, y_high, volatility)


def first_kernel(*refs, count, lines, parts, length, halo):
    pieces, matrix3, out = refs[:count], refs[count], refs[count + 1]
    rows = length + 2 * halo

    def pair(step, carry):
        y = step * 2
        field = jnp.concatenate(
            [
                jnp.concatenate(
                    [piece[pl.ds(y + t, piece.shape[0] // lines, stride=lines), :] for piece in pieces], axis=0
                )
                for t in range(2)
            ],
            axis=1,
        )
        solved = left_product(matrix3[...], field)
        width = solved.shape[1] // 2
        for t in range(2):
            half = solved[:, t * width : (t + 1) * width]
            for part in range(parts):
                base = part * rows
                out[pl.ds((base + halo) * lines + y + t, length, stride=lines), :] = half[part * length : (part + 1) * length]
                if halo:
                    zero = jnp.zeros((1, width), F32)
                    before = half[part * length - 1 : part * length] if part > 0 else zero
                    after = half[(part + 1) * length : (part + 1) * length + 1] if part < parts - 1 else zero
                    out[pl.ds(base * lines + y + t, 1), :] = before
                    out[pl.ds((base + rows - 1) * lines + y + t, 1), :] = after
        return carry

    lax.fori_loop(0, lines // 2, pair, 0)


def first(pieces, matrix3, halo):
    wide = pieces[0].shape[0]
    lines, bz = pieces[0].shape[2:]
    length = sum(piece.shape[1] for piece in pieces)
    rows = length + 2 * halo
    flat = [piece.reshape(-1, bz) for piece in pieces]
    out = pl.pallas_call(
        functools.partial(first_kernel, count=len(flat), lines=lines, parts=wide, length=length, halo=halo),
        in_specs=[pl.BlockSpec(memory_space=pltpu.VMEM)] * (len(flat) + 1),
        out_specs=pl.BlockSpec(memory_space=pltpu.VMEM),
        out_shape=jax.ShapeDtypeStruct((wide * rows * lines, bz), F32),
        compiler_params=params(40),
        cost_estimate=cost(7e9, 10),
        name="first",
    )(*flat, matrix3)
    return out.reshape(wide, rows, lines, bz)


def second_kernel(*refs, count, chunked):
    pieces, second3, third3, outs = refs[:count], refs[count], refs[count + 1], refs[count + 2 :]
    per, by, bz = pieces[0].shape
    length = count * by
    field = jnp.concatenate([piece[x] for x in range(per) for piece in pieces], axis=0)
    field = right_product(field, third3[...])
    field = jnp.concatenate([field[x * length : (x + 1) * length] for x in range(per)], axis=1)
    solved = left_product(second3[...], field)
    for x in range(per):
        half = solved[:, x * bz : (x + 1) * bz]
        if chunked:
            for d in range(count):
                out = outs[d]
                out[:, x] = half[d * by : (d + 1) * by].reshape(out.shape[0], out.shape[2], bz)
        else:
            outs[0][x] = half


def second(pieces, second3, third3, wide):
    count = len(pieces)
    xs, by, bz = pieces[0].shape
    per = 2
    if wide:
        out_specs = [pl.BlockSpec((wide, per, by // wide, bz), lambda s: (0, s, 0, 0))] * count
        out_shape = [jax.ShapeDtypeStruct((wide, xs, by // wide, bz), F32)] * count
    else:
        out_specs = [pl.BlockSpec((per, count * by, bz), lambda s: (s, 0, 0))]
        out_shape = [jax.ShapeDtypeStruct((xs, count * by, bz), F32)]
    return pl.pallas_call(
        functools.partial(second_kernel, count=count, chunked=bool(wide)),
        grid=(xs // per,),
        in_specs=[pl.BlockSpec((per, by, bz), lambda s: (s, 0, 0))] * count
        + [pl.BlockSpec(second3.shape, lambda s: (0, 0)), pl.BlockSpec(third3.shape, lambda s: (0, 0))],
        out_specs=out_specs,
        out_shape=out_shape,
        compiler_params=params(40),
        cost_estimate=cost(9e9, 10),
        name="second",
    )(*pieces, second3, third3)


def piece_specs(size, tail, per, n):
    return [pl.BlockSpec((size,) + tail, lambda s, i, d=d: (jnp.clip(s - d * per, 0, per - 1), 0, 0)) for d in range(n)]


def chunk_piece_specs(wide, lines, bz, per, order):
    return [
        pl.BlockSpec((wide, PLANES, lines, bz), lambda s, i, d=d: (0, jnp.clip(s - d * per, 0, per - 1), 0, 0))
        for d in order
    ]


def store_piece(outs, turn, kept):
    for d, out in enumerate(outs):

        @pl.when(turn == d)
        def _(out=out):
            out[...] = kept[...]


def select(values, turn):
    result = values[0]
    for d in range(1, len(values)):
        result = jnp.where(turn == d, values[d], result)
    return result


def lifted_kernel(i, solved, state, low, high, y_low, y_high, *refs, per, n, size, xs):
    outs, kept = refs[:n], refs[n]
    step = pl.program_id(0)
    bx = state.shape[0]
    base = lax.rem(i[0] + step // per, n) * xs + lax.rem(step, per) * size
    for k in range(size):
        row = base + k
        v = state[jnp.clip(row - 1, 0, bx - 1)]
        v = jnp.where(row == 0, low[0], jnp.where(row == bx + 1, high[0], v))
        up, down = y_pair(v, y_low[pl.ds(row, 1), :], y_high[pl.ds(row, 1), :])
        kept[k] = chunk_plane(solved, row) - damping * (up + down - 2.0 * v)
    store_piece(outs, step // per, kept)


def lifted(index, solved, state, low, high, y_low, y_high, n):
    bx, by, bz = state.shape
    xs = bx // n
    size = next(k for k in range(9, 0, -1) if (xs + 2) % k == 0)
    per = (xs + 2) // size
    return pl.pallas_call(
        functools.partial(lifted_kernel, per=per, n=n, size=size, xs=xs),
        grid_spec=pltpu.PrefetchScalarGridSpec(
            num_scalar_prefetch=1,
            grid=(n * per,),
            in_specs=[whole(v.shape) for v in (solved, state, low, high, y_low, y_high)],
            out_specs=piece_specs(size, (by, bz), per, n),
            scratch_shapes=[pltpu.VMEM((size, by, bz), F32)],
        ),
        out_shape=[jax.ShapeDtypeStruct((xs + 2, by, bz), F32)] * n,
        compiler_params=params(32),
        cost_estimate=cost(2e9, 13),
        name="lifted",
    )(index, solved, state, low, high, y_low, y_high)


def reaction_kernel(
    i, carried, carried_low, carried_high, vol, before, after, low, high, vol_low, vol_high, cotangent, *refs, per, n, blocks
):
    outs, kept = refs[:n], refs[n]
    step = pl.program_id(0)
    block = rotated(per, n)(step, i)

    def plane(k):
        sigma = pick_plane(k, PLANES, block, vol, before, after, low, high, blocks)
        return (0.5 * correction) * sigma * sigma * chunk_plane(carried, block * PLANES + k + 1)

    def rows(k):
        at = pl.ds(block * PLANES + k + 1, 1)
        s_low, s_high = vol_low[at, :], vol_high[at, :]
        return (
            (0.5 * correction) * s_low * s_low * carried_low[at, :],
            (0.5 * correction) * s_high * s_high * carried_high[at, :],
        )

    def emit(k, v, prev, nxt, mixed, inner):
        kept[k] = cotangent[k] + mixed

    sweep(PLANES, plane, rows, emit, False)
    store_piece(outs, step // per, kept)


def react(index, carried, carried_low, carried_high, vol, low, high, vol_low, vol_high, cotangent, n):
    bx, by, bz = vol.shape
    xs = bx // n
    per = xs // PLANES
    block = rotated(per, n)
    return pl.pallas_call(
        functools.partial(reaction_kernel, per=per, n=n, blocks=bx // PLANES),
        grid_spec=pltpu.PrefetchScalarGridSpec(
            num_scalar_prefetch=1,
            grid=(n * per,),
            in_specs=[whole(carried.shape), whole(carried_low.shape), whole(carried_high.shape)]
            + plane_specs(block, bx - 1, vol.shape)
            + [whole(low.shape), whole(high.shape), whole(vol_low.shape), whole(vol_high.shape)]
            + [pl.BlockSpec((PLANES, by, bz), lambda s, i: (block(s, i), 0, 0))],
            out_specs=piece_specs(PLANES, (by, bz), per, n),
            scratch_shapes=[pltpu.VMEM((PLANES, by, bz), F32)],
        ),
        out_shape=[jax.ShapeDtypeStruct((xs, by, bz), F32)] * n,
        compiler_params=params(40),
        cost_estimate=cost(4e9, 17),
        name="reaction",
    )(index, carried, carried_low, carried_high, vol, vol, vol, low, high, vol_low, vol_high, cotangent)


def lines_kernel(i, *refs, per, n):
    totals, uppers = refs[:n], refs[n : 2 * n]
    cotangent, upper_low, upper_high, third3, out = refs[2 * n :]
    step = pl.program_id(0)
    turn = step // per
    block = rotated(per, n)(step, i)
    for k in range(PLANES):
        total = select([ref[k] for ref in totals], turn)
        upper = select([chunk_plane(ref, k) for ref in uppers], turn)
        at = pl.ds(block * PLANES + k, 1)
        up, down = y_pair(upper, upper_low[at, :], upper_high[at, :])
        third = right_product(total, third3[...])
        z_up, z_down = z_pair(third)
        lines = (up + down - 2.0 * upper) + (z_up + z_down - 2.0 * third)
        out[k] = cotangent[k] - total - damping * lines


def gather_lines(index, totals, uppers, cotangent, upper_low, upper_high, third3):
    n = len(totals)
    bx, by, bz = cotangent.shape
    xs = bx // n
    per = xs // PLANES
    wide, lines = uppers[0].shape[0], uppers[0].shape[2]
    block = rotated(per, n)
    order = [(n - e) % n for e in range(n)]
    return pl.pallas_call(
        functools.partial(lines_kernel, per=per, n=n),
        grid_spec=pltpu.PrefetchScalarGridSpec(
            num_scalar_prefetch=1,
            grid=(n * per,),
            in_specs=piece_specs(PLANES, (by, bz), per, n)
            + chunk_piece_specs(wide, lines, bz, per, range(n))
            + [pl.BlockSpec((PLANES, by, bz), lambda s, i: (block(s, i), 0, 0))]
            + [whole(upper_low.shape), whole(upper_high.shape), whole(third3.shape)],
            out_specs=pl.BlockSpec((PLANES, by, bz), lambda s, i: (block(s, i), 0, 0)),
        ),
        out_shape=jax.ShapeDtypeStruct(cotangent.shape, F32),
        compiler_params=params(40),
        cost_estimate=cost(5e9, 17),
        name="lines",
    )(index, *totals, *[uppers[order[d]] for d in range(n)], cotangent, upper_low, upper_high, third3)


def mixed_kernel(i, field, *refs, n):
    outs, scratch = refs[:n], refs[n]
    by = outs[0].shape[1]

    def emit(k, v, prev, nxt, mixed, inner):
        scratch[...] = mixed
        for d, out in enumerate(outs):
            start = pl.multiple_of(lax.rem(i[0] + d, n) * by, by)
            out[k] = scratch[pl.ds(start, by), :]

    zero = jnp.zeros((1, field.shape[2]), F32)
    sweep(field.shape[0] - 2, lambda k: field[k + 1], lambda k: (zero, zero), emit, False)


def mix(index, field, n):
    rows, ny, bz = field.shape
    xs, by = rows - 2, ny // n
    return pl.pallas_call(
        functools.partial(mixed_kernel, n=n),
        grid_spec=pltpu.PrefetchScalarGridSpec(
            num_scalar_prefetch=1,
            grid=(1,),
            in_specs=[whole(field.shape)],
            out_specs=[whole((xs, by, bz))] * n,
            scratch_shapes=[pltpu.VMEM((ny, bz), F32)],
        ),
        out_shape=[jax.ShapeDtypeStruct((xs, by, bz), F32)] * n,
        compiler_params=params(40),
        cost_estimate=cost(4e9, 9),
        name="mixed",
    )(index, field)


def patch_sums(out, step, planes, patch, patch_t, groups):
    @pl.when(step == 0)
    def _():
        out[...] = jnp.zeros_like(out)

    count, (by, bz) = len(planes), planes[0].shape
    value_high, value_low = split(jnp.concatenate(planes, axis=0))
    ones = jnp.ones((2 * bz, 128), BF16)
    column = jnp.dot(jnp.concatenate([value_high, value_low], axis=1), ones, preferred_element_type=F32)
    number = jnp.concatenate([patch[pl.ds(k, 1), :] for k in range(count)], axis=1)
    coarse = lax.broadcasted_iota(jnp.int32, (groups, count * by), 0) == lax.shift_right_logical(number, 7)
    number_t = patch_t[...].reshape(count * by, 1)
    lane = lax.broadcasted_iota(jnp.int32, (count * by, 128), 1)
    high, low = split(jnp.where(lane == lax.bitwise_and(number_t, 127), column, 0.0))
    out[...] += jnp.dot(
        jnp.where(coarse, 1.0, 0.0).astype(BF16), jnp.concatenate([high, low], axis=1), preferred_element_type=F32
    )


def frozen_kernel(
    i, state, before, after, low, high, q_low, q_high, third3, vol, carried, patch, patch_t, weight, out, *, blocks, groups
):
    block = pl.program_id(0)
    planes = []

    def plane(k):
        v = pick_plane(k, PLANES, block, state, before, after, low, high, blocks)
        up, down = z_pair(v)
        return v + damping * right_product(up + down - 2.0 * v, third3[...])

    def emit(k, v, prev, nxt, mixed, inner):
        w = correction * vol[k] * chunk_plane(carried, block * PLANES + k + 1)
        weight[k] = w
        planes.append(-w * mixed)

    sweep(
        PLANES,
        plane,
        lambda k: (q_low[pl.ds(block * PLANES + k + 1, 1), :], q_high[pl.ds(block * PLANES + k + 1, 1), :]),
        emit,
        False,
    )
    patch_sums(out, block, planes, patch, patch_t, groups)


def frozen(index, state, low, high, q_low, q_high, third3, vol, carried, patch, patch_t, groups):
    bx, by, bz = state.shape
    blocks = bx // PLANES
    main = pl.BlockSpec((PLANES, by, bz), lambda s, i: (s, 0, 0))
    return pl.pallas_call(
        functools.partial(frozen_kernel, blocks=blocks, groups=groups),
        grid_spec=pltpu.PrefetchScalarGridSpec(
            num_scalar_prefetch=1,
            grid=(blocks,),
            in_specs=plane_specs(natural, bx - 1, state.shape)
            + [whole(low.shape), whole(high.shape), whole(q_low.shape), whole(q_high.shape), whole(third3.shape)]
            + [main, whole(carried.shape)]
            + [pl.BlockSpec((PLANES, by), lambda s, i: (s, 0))]
            + [pl.BlockSpec((PLANES, by, 1), lambda s, i: (s, 0, 0))],
            out_specs=[main, whole((groups, 256))],
        ),
        out_shape=[jax.ShapeDtypeStruct(state.shape, F32), jax.ShapeDtypeStruct((groups, 256), F32)],
        compiler_params=params(32),
        cost_estimate=cost(5e9, 17),
        name="frozen",
    )(index, state, state, state, low, high, q_low, q_high, third3, vol, carried, patch, patch_t)


def column_kernel(i, *refs, per, n, groups):
    drifts = refs[:n]
    weight, source, start, patch, patch_t, given, out = refs[n:]
    step = pl.program_id(0)
    turn = step // per
    block = rotated(per, n)(step, i)
    planes = [
        weight[k] * select([ref[k] for ref in drifts], turn)
        + source[k] * chunk_plane(start, block * PLANES + k + 1)
        for k in range(PLANES)
    ]
    patch_sums(out, step, planes, patch, patch_t, groups)

    @pl.when(step == pl.num_programs(0) - 1)
    def _():
        out[...] += given[...]


def column_sums(index, drifts, weight, source, start, patch, patch_t, given):
    n = len(drifts)
    bx, by, bz = source.shape
    xs = bx // n
    per = xs // PLANES
    groups = given.shape[0]
    block = rotated(per, n)
    order = [(n - e) % n for e in range(n)]
    main = pl.BlockSpec((PLANES, by, bz), lambda s, i: (block(s, i), 0, 0))
    return pl.pallas_call(
        functools.partial(column_kernel, per=per, n=n, groups=groups),
        grid_spec=pltpu.PrefetchScalarGridSpec(
            num_scalar_prefetch=1,
            grid=(n * per,),
            in_specs=piece_specs(PLANES, (by, bz), per, n)
            + [main, main, whole(start.shape)]
            + [pl.BlockSpec((PLANES, by), lambda s, i: (block(s, i), 0))]
            + [pl.BlockSpec((PLANES, by, 1), lambda s, i: (block(s, i), 0, 0)), whole(given.shape)],
            out_specs=whole(given.shape),
        ),
        out_shape=jax.ShapeDtypeStruct(given.shape, F32),
        compiler_params=params(40),
        cost_estimate=cost(4e9, 17),
        name="column",
    )(index, *[drifts[order[d]] for d in range(n)], weight, source, start, patch, patch_t, given)


def adjoint_kernel(
    i, start, start_low, start_high, vol, before, after, low, high, vol_low, vol_high, tail, out, *, blocks
):
    block = pl.program_id(0)
    raw = {}

    def plane(k):
        sigma = pick_plane(k, PLANES, block, vol, before, after, low, high, blocks)
        raw[k] = chunk_plane(start, block * PLANES + k + 1)
        return (0.5 * time_step) * sigma * sigma * raw[k]

    def rows(k):
        at = pl.ds(block * PLANES + k + 1, 1)
        s_low, s_high = vol_low[at, :], vol_high[at, :]
        return (
            (0.5 * time_step) * s_low * s_low * start_low[at, :],
            (0.5 * time_step) * s_high * s_high * start_high[at, :],
        )

    def emit(k, v, prev, nxt, mixed, inner):
        spread = mixed + (prev + nxt - 2.0 * v) + inner
        lines = raw[k - 1] + raw[k + 1] - 2.0 * raw[k]
        out[k] = raw[k] + spread + tail[k] - damping * lines

    sweep(PLANES, plane, rows, emit, True)


def finish(index, start, start_low, start_high, vol, low, high, vol_low, vol_high, tail):
    bx, by, bz = vol.shape
    return pl.pallas_call(
        functools.partial(adjoint_kernel, blocks=bx // PLANES),
        grid_spec=pltpu.PrefetchScalarGridSpec(
            num_scalar_prefetch=1,
            grid=(bx // PLANES,),
            in_specs=[whole(start.shape), whole(start_low.shape), whole(start_high.shape)]
            + plane_specs(natural, bx - 1, vol.shape)
            + [whole(low.shape), whole(high.shape), whole(vol_low.shape), whole(vol_high.shape)]
            + [pl.BlockSpec((PLANES, by, bz), lambda s, i: (s, 0, 0))],
            out_specs=pl.BlockSpec((PLANES, by, bz), lambda s, i: (s, 0, 0)),
        ),
        out_shape=jax.ShapeDtypeStruct(vol.shape, F32),
        compiler_params=params(40),
        cost_estimate=cost(5e9, 17),
        name="adjoint",
    )(index, start, start_low, start_high, vol, vol, vol, low, high, vol_low, vol_high, tail)


def neighbours(low_edge, high_edge, axis):
    count = lax.axis_size(axis)
    up = [(k, k + 1) for k in range(count - 1)]
    down = [(k + 1, k) for k in range(count - 1)]
    return lax.ppermute(high_edge, axis, up), lax.ppermute(low_edge, axis, down)


def far_and_near(n):
    return [n // 2] if n > 1 else [], [d for d in range(1, n) if d != n // 2]


def send(pieces, chosen, *earlier):
    n = len(pieces)
    result = list(pieces)
    for d in chosen:
        piece = after(pieces[d], *earlier) if earlier else pieces[d]
        result[d] = lax.ppermute(piece, "narrow", [(k, (k + d) % n) for k in range(n)])
    return result


def pick(pieces, chosen):
    return [pieces[d] for d in chosen]


def after(value, *earlier):
    return lax.optimization_barrier((value, earlier))[0]


def across(piece):
    return lax.all_to_all(piece, "wide", split_axis=0, concat_axis=0, tiled=True)


def row_major(value):
    return with_layout_constraint(value, Layout(major_to_minor=tuple(range(value.ndim))))


def cross_both(pieces, before, between, near, far):
    pieces = [row_major(piece) for piece in pieces]
    lines = send(pieces, near)
    lines = send(lines, far, *pick(lines, near))
    lines = [row_major(line) for line in lines]
    block = jnp.concatenate(pick(lines, [0] + near), axis=1)
    chunks = [across(after(block, *before) if before else block)]
    for d in far:
        chunks.append(across(after(lines[d], chunks[-1], *between)))
    return lines, chunks, pick(lines, far)


def y_edges(chunks):
    return neighbours(chunks[0, :, 0, :], chunks[-1, :, -1, :], "narrow")


def on_device_kernels(state, volatility, cotangent, solve_first, solve_second, solve_third, patch_index):
    n, wide = lax.axis_size("narrow"), lax.axis_size("wide")
    here = lax.axis_index("narrow")
    index = here.astype(jnp.int32).reshape(1)
    bx, by, bz = state.shape
    xs = bx // n
    groups = PATCHES // 128

    ahead = (here + jnp.arange(n)) % n
    back = (here - jnp.arange(n)) % n

    far, near = far_and_near(n)
    every = range(n)

    cot_pieces = [lax.dynamic_slice_in_dim(cotangent, ahead[d] * xs, xs, 0) for d in range(n)]
    early, late = near[:1], near[1:]
    both_low, both_high = neighbours(
        jnp.stack([state[0], volatility[0]]), jnp.stack([state[-1], volatility[-1]]), "wide"
    )
    both = jnp.stack([state[:, :: by - 1], volatility[:, :: by - 1]])
    both = jnp.concatenate([both_low[:, None, :: by - 1], both, both_high[:, None, :: by - 1]], axis=1)
    y_low, y_high = neighbours(both[:, :, 0], both[:, :, 1], "narrow")
    state_x = (both_low[0:1], both_high[0:1])
    vol_x = (both_low[1:2], both_high[1:2])
    state_y = (y_low[0], y_high[0])
    vol_y = (y_low[1], y_high[1])
    cot_lines = send(cot_pieces, near, y_low, y_high)

    second_t = solve_second.T.reshape(n, by, n, by)
    second_t3 = left_form(second_t[ahead][:, :, back].reshape(n * by, n * by))
    second_n = solve_second.reshape(n * by, n, by)
    second_n3 = left_form(second_n[:, back].reshape(n * by, n * by))
    third_t3 = right_form(solve_third)
    third_n3 = right_form(solve_third.T)
    first_n3 = left_form(solve_first)
    first_t = solve_first.T.reshape(wide * bx, wide, n, xs)
    first_t = first_t[:, :, back]
    groups_of = [[0] + near] + [[d] for d in far]
    first_t3 = left_form(
        jnp.concatenate([first_t[:, :, jnp.array(g)].reshape(wide * bx, -1) for g in groups_of], axis=1)
    )

    a, source = forward(index, state, volatility, *state_x, *state_y, wide)
    a = after(a, *pick(cot_lines, early))
    cot_lines = send(cot_lines, far, *pick(cot_lines, near))
    forward_lines = after(first([across(a)], first_n3, 1), *pick(cot_lines, far), second_t3, third_t3)
    back = second(after(cot_lines, forward_lines), second_t3, third_t3, wide)
    solved = across(forward_lines)

    lifted_pieces = lifted(index, solved, state, *state_x, *state_y, n)
    back, carried_chunks, gone = cross_both(back, (solved,), lifted_pieces, near, far)
    carried_lines = first(carried_chunks, first_t3, 1)
    level_lines = send(lifted_pieces, late, gone)
    carried = across(after(carried_lines, *pick(level_lines, late)))

    level_lines = send(level_lines, far, *pick(level_lines, late))
    carried = after(carried, *pick(level_lines, far))
    carried_y = y_edges(carried)
    level_lines = send(level_lines, early, *carried_y)
    totals = react(index, carried, *carried_y, volatility, *vol_x, *vol_y, cotangent, n)
    total_lines = send(totals, far + near)

    level = second(after(level_lines, totals), second_n3, third_n3, 0)[0]
    drift_pieces = mix(index, level, n)

    def frozen_rows(rows):
        padded = jnp.pad(rows, ((0, 0), (1, 1)))
        curved = padded[:, 2:] + padded[:, :-2] - 2.0 * rows
        return rows + damping * jnp.dot(curved, solve_third.T, precision=lax.Precision.HIGHEST)

    patch_t = patch_index[:, :, None]
    weight, sums = frozen(
        index,
        after(state, *drift_pieces),
        *state_x,
        frozen_rows(state_y[0]),
        frozen_rows(state_y[1]),
        third_n3,
        volatility,
        carried,
        patch_index,
        patch_t,
        groups,
    )

    total_lines = after(total_lines, drift_pieces, sums)
    drifts = send(drift_pieces, early, *total_lines)
    uppers = after(second(total_lines, second_t3, third_t3, wide), *pick(drifts, early))
    uppers, start_chunks, gone = cross_both(uppers, (), (), near, far)
    start_lines = first(start_chunks, first_t3, 1)
    drifts = send(drifts, late, gone)
    start = across(after(start_lines, *pick(drifts, late)))

    order = (here - jnp.arange(n)) % n
    edge_low = jnp.stack([piece[0, :, 0] for piece in uppers])[order].reshape(bx, bz)
    edge_high = jnp.stack([piece[-1, :, -1] for piece in uppers])[order].reshape(bx, bz)
    upper_y = neighbours(edge_low, edge_high, "narrow")
    drifts = send(drifts, far, *pick(drifts, late), *upper_y)
    tail = gather_lines(index, totals, uppers, cotangent, *upper_y, third_t3)

    start = after(start, tail)
    start_y = y_edges(start)
    start = after(start, *start_y)
    sums = column_sums(index, drifts, weight, source, start, patch_index, patch_t, sums)
    count, joint = n * wide, ("wide", "narrow")
    sums = (sums[:, :128] + sums[:, 128:]).reshape(count, PATCHES // count)
    shares = lax.all_to_all(sums, joint, split_axis=0, concat_axis=0, tiled=True)
    vega = jnp.sum(shares, axis=0)

    adjoint = finish(index, start, *start_y, volatility, *vol_x, *vol_y, tail)
    return (adjoint, vega * vega_scale)


def on_device(*args):
    n, wide = lax.axis_size("narrow"), lax.axis_size("wide")
    bx, by, bz = args[0].shape
    aligned = bx % (n * PLANES) == 0 and by % 128 == 0 and by % (wide * 8) == 0 and bz == 128
    aligned = aligned and PATCHES % (n * wide) == 0 and by // wide % 2 == 0
    return on_device_kernels(*args) if aligned else on_device_plain(*args)


def solution(mesh):
    placed = (
        P("wide", "narrow", None),
        P("wide", "narrow", None),
        P("wide", "narrow", None),
        P(),
        P(),
        P(),
        P("wide", "narrow"),
    )
    return jax.shard_map(
        on_device,
        mesh=mesh,
        in_specs=placed,
        out_specs=(P("wide", "narrow", None), P(("wide", "narrow"))),
        check_vma=False,
    )
```

```python
import functools
import jax
import jax.numpy as jnp
from jax import lax
from jax.experimental import pallas as pl
from jax.experimental.layout import Layout, with_layout_constraint
from jax.experimental.pallas import tpu as pltpu
from jax.sharding import PartitionSpec as P

PATCHES = 3072


time_step = 0.4
theta_weight = 0.5
frozen_coef = 0.2
correction = 0.5 * 0.4
vega_scale = 1.0 / 32.0
correlations = ((0, 1, 0.5), (0, 2, 0.3), (1, 2, -0.4))


def padded_2(cells, sides, width):
    for axis, dim in sides:
        count = lax.axis_size(axis)
        ends = count - 1
        head = lax.slice_in_dim(cells, 0, width, axis=dim)
        tail = lax.slice_in_dim(cells, cells.shape[dim] - width, cells.shape[dim], axis=dim)
        cells = jnp.concatenate(
            [
                lax.ppermute(tail, axis, [(i, (i + 1) % count) for i in range(ends)]),
                cells,
                lax.ppermute(head, axis, [((i + 1) % count, i) for i in range(ends)]),
            ],
            axis=dim,
        )
    return cells


def along_third(values, offset):
    if offset == 0:
        return values
    zero_layer = jnp.zeros_like(values[..., :1])
    if offset > 0:
        return jnp.concatenate([values[..., 1:], zero_layer], axis=-1)
    return jnp.concatenate([zero_layer, values[..., :-1]], axis=-1)


def shifted(padded, offsets):
    lead = padded.ndim - 3
    slices = [slice(None)] * lead
    for position in range(2):
        offset = offsets[position]
        length = padded.shape[lead + position]
        slices.append(slice(1 + offset, length - 1 + offset))
    slices.append(slice(None))
    return along_third(padded[tuple(slices)], offsets[2])


def second_parts(padded):
    centre = shifted(padded, [0, 0, 0])
    result = []
    for axis_number in range(3):
        upward = [0, 0, 0]
        upward[axis_number] = 1
        downward = [0, 0, 0]
        downward[axis_number] = -1
        result.append(shifted(padded, upward) + shifted(padded, downward) - 2.0 * centre)
    return tuple(result)


def cross_term(padded, first_axis, second_axis):

    def corner(sign_first, sign_second):
        offsets = [0, 0, 0]
        offsets[first_axis] = sign_first
        offsets[second_axis] = sign_second
        return shifted(padded, offsets)

    return 0.25 * (corner(1, 1) - corner(1, -1) - corner(-1, 1) + corner(-1, -1))


def mixed_of(padded):
    total = None
    for first_axis, second_axis, weight in correlations:
        term = weight * cross_term(padded, first_axis, second_axis)
        total = term if total is None else total + term
    return total


def contract(matrix, field, axis_number, transposed):
    letters = "xyz"
    source = letters[axis_number]
    matrix_form = source + "w" if transposed else "w" + source
    result_form = letters.replace(source, "w")
    return jnp.einsum(
        matrix_form + "," + letters + "->" + result_form,
        matrix,
        field,
        precision=lax.Precision.HIGHEST,
    )


def line_x(field, matrix, transposed):

    def solve_lines(pieces):
        solved = contract(matrix, pieces, 0, transposed)
        return lax.all_to_all(solved, "wide", split_axis=0, concat_axis=1, tiled=True)

    return solve_lines(lax.all_to_all(field, "wide", split_axis=1, concat_axis=0, tiled=True))


def line_y(field, matrix, transposed):

    def solve_lines(pieces):
        solved = contract(matrix, pieces, 1, transposed)
        return lax.all_to_all(solved, "narrow", split_axis=1, concat_axis=2, tiled=True)

    return solve_lines(lax.all_to_all(field, "narrow", split_axis=2, concat_axis=1, tiled=True))


def rimmed(stacked):
    return padded_2(stacked, (("wide", 1), ("narrow", 2)), 1)


def third_second(field):
    return along_third(field, 1) + along_third(field, -1) - 2.0 * field


def on_device_plain(state, volatility, cotangent, solve_first, solve_second, solve_third, patch_index):
    coefficient = 0.5 * volatility * volatility
    padded = rimmed(state[None])
    parts = second_parts(padded)
    second_x, second_y, second_z = (parts[0][0], parts[1][0], parts[2][0])
    source = mixed_of(padded)[0] + second_x + second_y + second_z
    start = state + time_step * coefficient * source
    damping = theta_weight * time_step * frozen_coef
    level = line_x(start - damping * second_x, solve_first, False)
    level = line_y(level - damping * second_y, solve_second, False)
    level = contract(solve_third, level - damping * second_z, 2, False)
    drift = mixed_of(rimmed((level - state)[None]))[0]
    back_third = contract(solve_third, cotangent, 2, True)
    back_second = line_y(back_third, solve_second, True)
    carried = line_x(back_second, solve_first, True)
    reaction = mixed_of(rimmed((correction * coefficient * carried)[None]))[0]
    total = cotangent + reaction
    upper_third = contract(solve_third, total, 2, True)
    upper_second = line_y(upper_third, solve_second, True)
    adjoint_start = line_x(upper_second, solve_first, True)
    scaled = time_step * coefficient * adjoint_start
    padded = rimmed(jnp.stack([scaled, adjoint_start, upper_second]))
    parts = second_parts(padded)
    spread = mixed_of(padded[0:1])[0] + parts[0][0] + parts[1][0] + parts[2][0]
    lines = parts[0][1] + parts[1][2] + third_second(upper_third)
    adjoint = adjoint_start + spread - reaction - damping * lines
    sensitivity = volatility * (correction * carried * drift + time_step * adjoint_start * source)
    column = jnp.sum(sensitivity, axis=2)
    partial_sums = jax.ops.segment_sum(
        column.reshape(-1), patch_index.reshape(-1), num_segments=PATCHES
    )
    vega = lax.psum_scatter(partial_sums, ("wide", "narrow"), scatter_dimension=0, tiled=True)
    return (adjoint, vega * vega_scale)


F32 = jnp.float32
BF16 = jnp.bfloat16
damping = 0.5 * 0.4 * 0.2
MIB = 1024 * 1024
PLANES = 8


def params(mib):
    return pltpu.CompilerParams(vmem_limit_bytes=60 * MIB)


def cost(flops, mib):
    return pl.CostEstimate(flops=int(flops / 50), bytes_accessed=int(mib * MIB / 50), transcendentals=0)


def halves(x):
    high = lax.reduce_precision(x, 8, 7)
    return high.astype(BF16), (x - high).astype(BF16)


def left_form(matrix):
    high, low = halves(matrix)
    return jnp.concatenate([high, high, low], axis=1)


def right_form(matrix):
    high, low = halves(matrix)
    return jnp.concatenate([high, high, low], axis=0)


def split(x):
    high = x.astype(BF16)
    return high, (x - high.astype(F32)).astype(BF16)


def left_product(matrix3, field):
    high, low = split(field)
    return jnp.dot(matrix3, jnp.concatenate([high, low, high], axis=0), preferred_element_type=F32)


def right_product(field, matrix3):
    high, low = split(field)
    return jnp.dot(jnp.concatenate([high, low, high], axis=1), matrix3, preferred_element_type=F32)


def y_pair(v, low_row, high_row):
    n = v.shape[0]
    row = lax.broadcasted_iota(jnp.int32, (8, v.shape[1]), 0)
    up, down = pltpu.roll(v, n - 1, 0), pltpu.roll(v, 1, 0)
    up = jnp.concatenate([up[: n - 8], jnp.where(row == 7, high_row, up[n - 8 :])], axis=0)
    down = jnp.concatenate([jnp.where(row == 0, low_row, down[:8]), down[8:]], axis=0)
    return up, down


def z_pair(v):
    n = v.shape[1]
    lane = lax.broadcasted_iota(jnp.int32, v.shape, 1)
    up = jnp.where(lane == n - 1, 0.0, pltpu.roll(v, n - 1, 1))
    down = jnp.where(lane == 0, 0.0, pltpu.roll(v, 1, 1))
    return up, down


def sweep(count, plane, rows, emit, full):
    v, p, rest, inner = {}, {}, {}, {}
    for k in range(-1, count + 1):
        centre = plane(k)
        y_up, y_down = y_pair(centre, *rows(k))
        z_up, z_down = z_pair(centre)
        e = y_up - y_down
        v[k] = centre
        p[k] = 0.125 * e + 0.075 * (z_up - z_down)
        if 0 <= k < count:
            e_up, e_down = z_pair(e)
            rest[k] = -0.1 * (e_up - e_down)
            if full:
                inner[k] = (y_up + y_down) + (z_up + z_down) - 4.0 * centre
        if k >= 1:
            mixed = (p[k] - p[k - 2]) + rest[k - 1]
            emit(k - 1, v[k - 1], v[k - 2], v[k], mixed, inner.get(k - 1))


def chunk_plane(ref, x):
    value = ref[:, x]
    return value.reshape(value.shape[0] * value.shape[1], value.shape[2])


def plane_specs(step_block, last, shape):
    tail = shape[1:]
    return [
        pl.BlockSpec((PLANES,) + tail, lambda s, i: (step_block(s, i), 0, 0)),
        pl.BlockSpec((1,) + tail, lambda s, i: (jnp.maximum(step_block(s, i) * PLANES - 1, 0), 0, 0)),
        pl.BlockSpec((1,) + tail, lambda s, i: (jnp.minimum(step_block(s, i) * PLANES + PLANES, last), 0, 0)),
    ]


def whole(shape):
    return pl.BlockSpec(shape, lambda s, i: (0,) * len(shape))


def pick_plane(k, count, block, main, before, after, low, high, blocks):
    if k < 0:
        return jnp.where(block == 0, low[0], before[0])
    if k >= count:
        return jnp.where(block == blocks - 1, high[0], after[0])
    return main[k]


def natural(s, i):
    return s


def rotated(per, n):
    def block(s, i):
        return lax.rem(i[0] + s // per, n) * per + lax.rem(s, per)

    return block


def piece_map(d, per):
    return lambda s: jnp.clip(s - d * per, 0, per - 1)


def forward_kernel(i, state, before, after, low, high, y_low, y_high, volatility, a_out, source_out, *, blocks):
    block = pl.program_id(0)

    def emit(k, v, prev, nxt, mixed, inner):
        second_x = prev + nxt - 2.0 * v
        source = mixed + second_x + inner
        sigma = volatility[k]
        a = v + (time_step * 0.5) * sigma * sigma * source - damping * second_x
        a_out[:, k] = a.reshape(a_out.shape[0], a_out.shape[2], a_out.shape[3])
        source_out[k] = time_step * sigma * source

    sweep(
        PLANES,
        lambda k: pick_plane(k, PLANES, block, state, before, after, low, high, blocks),
        lambda k: (y_low[pl.ds(block * PLANES + k + 1, 1), :], y_high[pl.ds(block * PLANES + k + 1, 1), :]),
        emit,
        True,
    )


def forward(index, state, volatility, low, high, y_low, y_high, wide):
    bx, by, bz = state.shape
    blocks = bx // PLANES
    return pl.pallas_call(
        functools.partial(forward_kernel, blocks=blocks),
        grid_spec=pltpu.PrefetchScalarGridSpec(
            num_scalar_prefetch=1,
            grid=(blocks,),
            in_specs=plane_specs(natural, bx - 1, state.shape)
            + [whole(low.shape), whole(high.shape), whole(y_low.shape), whole(y_high.shape)]
            + [pl.BlockSpec((PLANES, by, bz), lambda s, i: (s, 0, 0))],
            out_specs=[
                pl.BlockSpec((wide, PLANES, by // wide, bz), lambda s, i: (0, s, 0, 0)),
                pl.BlockSpec((PLANES, by, bz), lambda s, i: (s, 0, 0)),
            ],
        ),
        out_shape=[
            jax.ShapeDtypeStruct((wide, bx, by // wide, bz), F32),
            jax.ShapeDtypeStruct(state.shape, F32),
        ],
        compiler_params=params(32),
        cost_estimate=cost(5e9, 17),
        name="forward",
    )(index, state, state, state, low, high, y_low, y_high, volatility)


def first_kernel(*refs, count, lines, parts, length, halo):
    pieces, matrix3, out = refs[:count], refs[count], refs[count + 1]
    pieces = [piece.reshape(piece.shape[0] * lines, piece.shape[2]) for piece in pieces]
    out = out.reshape(out.shape[0] * lines, out.shape[2])
    rows = length + 2 * halo

    def pair(step, carry):
        y = step * 2
        field = jnp.concatenate(
            [
                jnp.concatenate(
                    [piece[pl.ds(y + t, piece.shape[0] // lines, stride=lines), :] for piece in pieces], axis=0
                )
                for t in range(2)
            ],
            axis=1,
        )
        solved = left_product(matrix3[...], field)
        width = solved.shape[1] // 2
        for t in range(2):
            half = solved[:, t * width : (t + 1) * width]
            for part in range(parts):
                base = part * rows
                out[pl.ds((base + halo) * lines + y + t, length, stride=lines), :] = half[part * length : (part + 1) * length]
                if halo:
                    zero = jnp.zeros((1, width), F32)
                    before = half[part * length - 1 : part * length] if part > 0 else zero
                    after = half[(part + 1) * length : (part + 1) * length + 1] if part < parts - 1 else zero
                    out[pl.ds(base * lines + y + t, 1), :] = before
                    out[pl.ds((base + rows - 1) * lines + y + t, 1), :] = after
        return carry

    lax.fori_loop(0, lines // 2, pair, 0)


def first(pieces, matrix3, halo):
    wide = pieces[0].shape[0]
    lines, bz = pieces[0].shape[2:]
    length = sum(piece.shape[1] for piece in pieces)
    rows = length + 2 * halo
    flat = [piece.reshape(-1, lines, bz) for piece in pieces]
    block = 8
    out = pl.pallas_call(
        functools.partial(first_kernel, count=len(flat), lines=block, parts=wide, length=length, halo=halo),
        grid=(lines // block,),
        in_specs=[pl.BlockSpec((piece.shape[0], block, bz), lambda s: (0, s, 0)) for piece in flat]
        + [pl.BlockSpec(matrix3.shape, lambda s: (0, 0))],
        out_specs=pl.BlockSpec((wide * rows, block, bz), lambda s: (0, s, 0)),
        out_shape=jax.ShapeDtypeStruct((wide * rows, lines, bz), F32),
        compiler_params=params(40),
        cost_estimate=cost(7e9, 10),
        name="first",
    )(*flat, matrix3)
    return out.reshape(wide, rows, lines, bz)


def second_kernel(*refs, count, chunked):
    pieces, second3, third3, outs = refs[:count], refs[count], refs[count + 1], refs[count + 2 :]
    per, by, bz = pieces[0].shape
    length = count * by
    field = jnp.concatenate([piece[x] for x in range(per) for piece in pieces], axis=0)
    field = right_product(field, third3[...])
    field = jnp.concatenate([field[x * length : (x + 1) * length] for x in range(per)], axis=1)
    solved = left_product(second3[...], field)
    for x in range(per):
        half = solved[:, x * bz : (x + 1) * bz]
        if chunked:
            for d in range(count):
                out = outs[d]
                out[:, x] = half[d * by : (d + 1) * by].reshape(out.shape[0], out.shape[2], bz)
        else:
            outs[0][x] = half


def second(pieces, second3, third3, wide):
    count = len(pieces)
    xs, by, bz = pieces[0].shape
    per = 2
    if wide:
        out_specs = [pl.BlockSpec((wide, per, by // wide, bz), lambda s: (0, s, 0, 0))] * count
        out_shape = [jax.ShapeDtypeStruct((wide, xs, by // wide, bz), F32)] * count
    else:
        out_specs = [pl.BlockSpec((per, count * by, bz), lambda s: (s, 0, 0))]
        out_shape = [jax.ShapeDtypeStruct((xs, count * by, bz), F32)]
    return pl.pallas_call(
        functools.partial(second_kernel, count=count, chunked=bool(wide)),
        grid=(xs // per,),
        in_specs=[pl.BlockSpec((per, by, bz), lambda s: (s, 0, 0))] * count
        + [pl.BlockSpec(second3.shape, lambda s: (0, 0)), pl.BlockSpec(third3.shape, lambda s: (0, 0))],
        out_specs=out_specs,
        out_shape=out_shape,
        compiler_params=params(40),
        cost_estimate=cost(9e9, 10),
        name="second",
    )(*pieces, second3, third3)


def piece_specs(size, tail, per, n):
    return [pl.BlockSpec((size,) + tail, lambda s, i, d=d: (jnp.clip(s - d * per, 0, per - 1), 0, 0)) for d in range(n)]


def chunk_piece_specs(wide, lines, bz, per, order):
    return [
        pl.BlockSpec((wide, PLANES, lines, bz), lambda s, i, d=d: (0, jnp.clip(s - d * per, 0, per - 1), 0, 0))
        for d in order
    ]


def store_piece(outs, turn, kept):
    for d, out in enumerate(outs):

        @pl.when(turn == d)
        def _(out=out):
            out[...] = kept[...]


def select(values, turn):
    result = values[0]
    for d in range(1, len(values)):
        result = jnp.where(turn == d, values[d], result)
    return result


def lifted_kernel(i, solved, state, low, high, y_low, y_high, *refs, per, n, size, xs):
    outs, kept = refs[:n], refs[n]
    step = pl.program_id(0)
    bx = state.shape[0]
    base = lax.rem(i[0] + step // per, n) * xs + lax.rem(step, per) * size
    for k in range(size):
        row = base + k
        v = state[jnp.clip(row - 1, 0, bx - 1)]
        v = jnp.where(row == 0, low[0], jnp.where(row == bx + 1, high[0], v))
        up, down = y_pair(v, y_low[pl.ds(row, 1), :], y_high[pl.ds(row, 1), :])
        kept[k] = chunk_plane(solved, row) - damping * (up + down - 2.0 * v)
    store_piece(outs, step // per, kept)


def lifted(index, solved, state, low, high, y_low, y_high, n):
    bx, by, bz = state.shape
    xs = bx // n
    size = next(k for k in range(9, 0, -1) if (xs + 2) % k == 0)
    per = (xs + 2) // size
    return pl.pallas_call(
        functools.partial(lifted_kernel, per=per, n=n, size=size, xs=xs),
        grid_spec=pltpu.PrefetchScalarGridSpec(
            num_scalar_prefetch=1,
            grid=(n * per,),
            in_specs=[whole(v.shape) for v in (solved, state, low, high, y_low, y_high)],
            out_specs=piece_specs(size, (by, bz), per, n),
            scratch_shapes=[pltpu.VMEM((size, by, bz), F32)],
        ),
        out_shape=[jax.ShapeDtypeStruct((xs + 2, by, bz), F32)] * n,
        compiler_params=params(32),
        cost_estimate=cost(2e9, 13),
        name="lifted",
    )(index, solved, state, low, high, y_low, y_high)


def reaction_kernel(
    i, carried, carried_low, carried_high, vol, before, after, low, high, vol_low, vol_high, cotangent, *refs, per, n, blocks
):
    outs, kept = refs[:n], refs[n]
    step = pl.program_id(0)
    block = rotated(per, n)(step, i)

    def plane(k):
        sigma = pick_plane(k, PLANES, block, vol, before, after, low, high, blocks)
        return (0.5 * correction) * sigma * sigma * chunk_plane(carried, block * PLANES + k + 1)

    def rows(k):
        at = pl.ds(block * PLANES + k + 1, 1)
        s_low, s_high = vol_low[at, :], vol_high[at, :]
        return (
            (0.5 * correction) * s_low * s_low * carried_low[at, :],
            (0.5 * correction) * s_high * s_high * carried_high[at, :],
        )

    def emit(k, v, prev, nxt, mixed, inner):
        kept[k] = cotangent[k] + mixed

    sweep(PLANES, plane, rows, emit, False)
    store_piece(outs, step // per, kept)


def react(index, carried, carried_low, carried_high, vol, low, high, vol_low, vol_high, cotangent, n):
    bx, by, bz = vol.shape
    xs = bx // n
    per = xs // PLANES
    block = rotated(per, n)
    return pl.pallas_call(
        functools.partial(reaction_kernel, per=per, n=n, blocks=bx // PLANES),
        grid_spec=pltpu.PrefetchScalarGridSpec(
            num_scalar_prefetch=1,
            grid=(n * per,),
            in_specs=[whole(carried.shape), whole(carried_low.shape), whole(carried_high.shape)]
            + plane_specs(block, bx - 1, vol.shape)
            + [whole(low.shape), whole(high.shape), whole(vol_low.shape), whole(vol_high.shape)]
            + [pl.BlockSpec((PLANES, by, bz), lambda s, i: (block(s, i), 0, 0))],
            out_specs=piece_specs(PLANES, (by, bz), per, n),
            scratch_shapes=[pltpu.VMEM((PLANES, by, bz), F32)],
        ),
        out_shape=[jax.ShapeDtypeStruct((xs, by, bz), F32)] * n,
        compiler_params=params(40),
        cost_estimate=cost(4e9, 17),
        name="reaction",
    )(index, carried, carried_low, carried_high, vol, vol, vol, low, high, vol_low, vol_high, cotangent)


def lines_kernel(i, *refs, per, n):
    totals, uppers = refs[:n], refs[n : 2 * n]
    cotangent, upper_low, upper_high, third3, out = refs[2 * n :]
    step = pl.program_id(0)
    turn = step // per
    block = rotated(per, n)(step, i)
    for k in range(PLANES):
        total = select([ref[k] for ref in totals], turn)
        upper = select([chunk_plane(ref, k) for ref in uppers], turn)
        at = pl.ds(block * PLANES + k, 1)
        up, down = y_pair(upper, upper_low[at, :], upper_high[at, :])
        third = right_product(total, third3[...])
        z_up, z_down = z_pair(third)
        lines = (up + down - 2.0 * upper) + (z_up + z_down - 2.0 * third)
        out[k] = cotangent[k] - total - damping * lines


def gather_lines(index, totals, uppers, cotangent, upper_low, upper_high, third3):
    n = len(totals)
    bx, by, bz = cotangent.shape
    xs = bx // n
    per = xs // PLANES
    wide, lines = uppers[0].shape[0], uppers[0].shape[2]
    block = rotated(per, n)
    order = [(n - e) % n for e in range(n)]
    return pl.pallas_call(
        functools.partial(lines_kernel, per=per, n=n),
        grid_spec=pltpu.PrefetchScalarGridSpec(
            num_scalar_prefetch=1,
            grid=(n * per,),
            in_specs=piece_specs(PLANES, (by, bz), per, n)
            + chunk_piece_specs(wide, lines, bz, per, range(n))
            + [pl.BlockSpec((PLANES, by, bz), lambda s, i: (block(s, i), 0, 0))]
            + [whole(upper_low.shape), whole(upper_high.shape), whole(third3.shape)],
            out_specs=pl.BlockSpec((PLANES, by, bz), lambda s, i: (block(s, i), 0, 0)),
        ),
        out_shape=jax.ShapeDtypeStruct(cotangent.shape, F32),
        compiler_params=params(40),
        cost_estimate=cost(5e9, 17),
        name="lines",
    )(index, *totals, *[uppers[order[d]] for d in range(n)], cotangent, upper_low, upper_high, third3)


def mixed_kernel(i, field, *refs, n):
    outs, scratch = refs[:n], refs[n]
    by = outs[0].shape[1]

    def emit(k, v, prev, nxt, mixed, inner):
        scratch[...] = mixed
        for d, out in enumerate(outs):
            start = pl.multiple_of(lax.rem(i[0] + d, n) * by, by)
            out[k] = scratch[pl.ds(start, by), :]

    zero = jnp.zeros((1, field.shape[2]), F32)
    sweep(field.shape[0] - 2, lambda k: field[k + 1], lambda k: (zero, zero), emit, False)


def mix(index, field, n):
    rows, ny, bz = field.shape
    xs, by = rows - 2, ny // n
    return pl.pallas_call(
        functools.partial(mixed_kernel, n=n),
        grid_spec=pltpu.PrefetchScalarGridSpec(
            num_scalar_prefetch=1,
            grid=(1,),
            in_specs=[whole(field.shape)],
            out_specs=[whole((xs, by, bz))] * n,
            scratch_shapes=[pltpu.VMEM((ny, bz), F32)],
        ),
        out_shape=[jax.ShapeDtypeStruct((xs, by, bz), F32)] * n,
        compiler_params=params(40),
        cost_estimate=cost(4e9, 9),
        name="mixed",
    )(index, field)


def patch_sums(out, step, planes, patch, patch_t, groups):
    @pl.when(step == 0)
    def _():
        out[...] = jnp.zeros_like(out)

    count, (by, bz) = len(planes), planes[0].shape
    value_high, value_low = split(jnp.concatenate(planes, axis=0))
    ones = jnp.ones((2 * bz, 128), BF16)
    column = jnp.dot(jnp.concatenate([value_high, value_low], axis=1), ones, preferred_element_type=F32)
    number = jnp.concatenate([patch[pl.ds(k, 1), :] for k in range(count)], axis=1)
    coarse = lax.broadcasted_iota(jnp.int32, (groups, count * by), 0) == lax.shift_right_logical(number, 7)
    number_t = patch_t[...].reshape(count * by, 1)
    lane = lax.broadcasted_iota(jnp.int32, (count * by, 128), 1)
    high, low = split(jnp.where(lane == lax.bitwise_and(number_t, 127), column, 0.0))
    out[...] += jnp.dot(
        jnp.where(coarse, 1.0, 0.0).astype(BF16), jnp.concatenate([high, low], axis=1), preferred_element_type=F32
    )


def frozen_kernel(
    i, state, before, after, low, high, q_low, q_high, third3, vol, carried, patch, patch_t, weight, out, *, blocks, groups
):
    block = pl.program_id(0)
    planes = []

    def plane(k):
        v = pick_plane(k, PLANES, block, state, before, after, low, high, blocks)
        up, down = z_pair(v)
        return v + damping * right_product(up + down - 2.0 * v, third3[...])

    def emit(k, v, prev, nxt, mixed, inner):
        w = correction * vol[k] * chunk_plane(carried, block * PLANES + k + 1)
        weight[k] = w
        planes.append(-w * mixed)

    sweep(
        PLANES,
        plane,
        lambda k: (q_low[pl.ds(block * PLANES + k + 1, 1), :], q_high[pl.ds(block * PLANES + k + 1, 1), :]),
        emit,
        False,
    )
    patch_sums(out, block, planes, patch, patch_t, groups)


def frozen(index, state, low, high, q_low, q_high, third3, vol, carried, patch, patch_t, groups):
    bx, by, bz = state.shape
    blocks = bx // PLANES
    main = pl.BlockSpec((PLANES, by, bz), lambda s, i: (s, 0, 0))
    return pl.pallas_call(
        functools.partial(frozen_kernel, blocks=blocks, groups=groups),
        grid_spec=pltpu.PrefetchScalarGridSpec(
            num_scalar_prefetch=1,
            grid=(blocks,),
            in_specs=plane_specs(natural, bx - 1, state.shape)
            + [whole(low.shape), whole(high.shape), whole(q_low.shape), whole(q_high.shape), whole(third3.shape)]
            + [main, whole(carried.shape)]
            + [pl.BlockSpec((PLANES, by), lambda s, i: (s, 0))]
            + [pl.BlockSpec((PLANES, by, 1), lambda s, i: (s, 0, 0))],
            out_specs=[main, whole((groups, 256))],
        ),
        out_shape=[jax.ShapeDtypeStruct(state.shape, F32), jax.ShapeDtypeStruct((groups, 256), F32)],
        compiler_params=params(32),
        cost_estimate=cost(5e9, 17),
        name="frozen",
    )(index, state, state, state, low, high, q_low, q_high, third3, vol, carried, patch, patch_t)


def column_kernel(i, *refs, per, n, groups):
    drifts = refs[:n]
    weight, source, start, patch, patch_t, given, out = refs[n:]
    step = pl.program_id(0)
    turn = step // per
    block = rotated(per, n)(step, i)
    planes = [
        weight[k] * select([ref[k] for ref in drifts], turn)
        + source[k] * chunk_plane(start, block * PLANES + k + 1)
        for k in range(PLANES)
    ]
    patch_sums(out, step, planes, patch, patch_t, groups)

    @pl.when(step == pl.num_programs(0) - 1)
    def _():
        out[...] += given[...]


def column_sums(index, drifts, weight, source, start, patch, patch_t, given):
    n = len(drifts)
    bx, by, bz = source.shape
    xs = bx // n
    per = xs // PLANES
    groups = given.shape[0]
    block = rotated(per, n)
    order = [(n - e) % n for e in range(n)]
    main = pl.BlockSpec((PLANES, by, bz), lambda s, i: (block(s, i), 0, 0))
    return pl.pallas_call(
        functools.partial(column_kernel, per=per, n=n, groups=groups),
        grid_spec=pltpu.PrefetchScalarGridSpec(
            num_scalar_prefetch=1,
            grid=(n * per,),
            in_specs=piece_specs(PLANES, (by, bz), per, n)
            + [main, main, whole(start.shape)]
            + [pl.BlockSpec((PLANES, by), lambda s, i: (block(s, i), 0))]
            + [pl.BlockSpec((PLANES, by, 1), lambda s, i: (block(s, i), 0, 0)), whole(given.shape)],
            out_specs=whole(given.shape),
        ),
        out_shape=jax.ShapeDtypeStruct(given.shape, F32),
        compiler_params=params(40),
        cost_estimate=cost(4e9, 17),
        name="column",
    )(index, *[drifts[order[d]] for d in range(n)], weight, source, start, patch, patch_t, given)


def adjoint_kernel(
    i, start, start_low, start_high, vol, before, after, low, high, vol_low, vol_high, tail, out, *, blocks
):
    block = pl.program_id(0)
    raw = {}

    def plane(k):
        sigma = pick_plane(k, PLANES, block, vol, before, after, low, high, blocks)
        raw[k] = chunk_plane(start, block * PLANES + k + 1)
        return (0.5 * time_step) * sigma * sigma * raw[k]

    def rows(k):
        at = pl.ds(block * PLANES + k + 1, 1)
        s_low, s_high = vol_low[at, :], vol_high[at, :]
        return (
            (0.5 * time_step) * s_low * s_low * start_low[at, :],
            (0.5 * time_step) * s_high * s_high * start_high[at, :],
        )

    def emit(k, v, prev, nxt, mixed, inner):
        spread = mixed + (prev + nxt - 2.0 * v) + inner
        lines = raw[k - 1] + raw[k + 1] - 2.0 * raw[k]
        out[k] = raw[k] + spread + tail[k] - damping * lines

    sweep(PLANES, plane, rows, emit, True)


def finish(index, start, start_low, start_high, vol, low, high, vol_low, vol_high, tail):
    bx, by, bz = vol.shape
    return pl.pallas_call(
        functools.partial(adjoint_kernel, blocks=bx // PLANES),
        grid_spec=pltpu.PrefetchScalarGridSpec(
            num_scalar_prefetch=1,
            grid=(bx // PLANES,),
            in_specs=[whole(start.shape), whole(start_low.shape), whole(start_high.shape)]
            + plane_specs(natural, bx - 1, vol.shape)
            + [whole(low.shape), whole(high.shape), whole(vol_low.shape), whole(vol_high.shape)]
            + [pl.BlockSpec((PLANES, by, bz), lambda s, i: (s, 0, 0))],
            out_specs=pl.BlockSpec((PLANES, by, bz), lambda s, i: (s, 0, 0)),
        ),
        out_shape=jax.ShapeDtypeStruct(vol.shape, F32),
        compiler_params=params(40),
        cost_estimate=cost(5e9, 17),
        name="adjoint",
    )(index, start, start_low, start_high, vol, vol, vol, low, high, vol_low, vol_high, tail)


def neighbours(low_edge, high_edge, axis):
    count = lax.axis_size(axis)
    up = [(k, k + 1) for k in range(count - 1)]
    down = [(k + 1, k) for k in range(count - 1)]
    return lax.ppermute(high_edge, axis, up), lax.ppermute(low_edge, axis, down)


def far_and_near(n):
    return [n // 2] if n > 1 else [], [d for d in range(1, n) if d != n // 2]


def send(pieces, chosen, *earlier):
    n = len(pieces)
    result = list(pieces)
    for d in chosen:
        piece = after(pieces[d], *earlier) if earlier else pieces[d]
        result[d] = lax.ppermute(piece, "narrow", [(k, (k + d) % n) for k in range(n)])
    return result


def pick(pieces, chosen):
    return [pieces[d] for d in chosen]


def after(value, *earlier):
    return lax.optimization_barrier((value, earlier))[0]


def across(piece):
    return lax.all_to_all(piece, "wide", split_axis=0, concat_axis=0, tiled=True)


def row_major(value):
    return with_layout_constraint(value, Layout(major_to_minor=tuple(range(value.ndim))))


def cross_both(pieces, before, between, near, far):
    pieces = [row_major(piece) for piece in pieces]
    lines = send(pieces, near)
    lines = send(lines, far, *pick(lines, near))
    lines = [row_major(line) for line in lines]
    block = jnp.concatenate(pick(lines, [0] + near), axis=1)
    chunks = [across(after(block, *before) if before else block)]
    for d in far:
        chunks.append(across(after(lines[d], chunks[-1], *between)))
    return lines, chunks, pick(lines, far)


def y_edges(chunks):
    return neighbours(chunks[0, :, 0, :], chunks[-1, :, -1, :], "narrow")


def on_device_kernels(state, volatility, cotangent, solve_first, solve_second, solve_third, patch_index):
    n, wide = lax.axis_size("narrow"), lax.axis_size("wide")
    here = lax.axis_index("narrow")
    index = here.astype(jnp.int32).reshape(1)
    bx, by, bz = state.shape
    xs = bx // n
    groups = PATCHES // 128

    ahead = (here + jnp.arange(n)) % n
    back = (here - jnp.arange(n)) % n

    far, near = far_and_near(n)
    every = range(n)

    cot_pieces = [lax.dynamic_slice_in_dim(cotangent, ahead[d] * xs, xs, 0) for d in range(n)]
    early, late = near[:1], near[1:]
    both_low, both_high = neighbours(
        jnp.stack([state[0], volatility[0]]), jnp.stack([state[-1], volatility[-1]]), "wide"
    )
    both = jnp.stack([state[:, :: by - 1], volatility[:, :: by - 1]])
    both = jnp.concatenate([both_low[:, None, :: by - 1], both, both_high[:, None, :: by - 1]], axis=1)
    y_low, y_high = neighbours(both[:, :, 0], both[:, :, 1], "narrow")
    state_x = (both_low[0:1], both_high[0:1])
    vol_x = (both_low[1:2], both_high[1:2])
    state_y = (y_low[0], y_high[0])
    vol_y = (y_low[1], y_high[1])
    cot_lines = send(cot_pieces, near, y_low, y_high)

    second_t = solve_second.T.reshape(n, by, n, by)
    second_t3 = left_form(second_t[ahead][:, :, back].reshape(n * by, n * by))
    second_n = solve_second.reshape(n * by, n, by)
    second_n3 = left_form(second_n[:, back].reshape(n * by, n * by))
    third_t3 = right_form(solve_third)
    third_n3 = right_form(solve_third.T)
    first_n3 = left_form(solve_first)
    first_t = solve_first.T.reshape(wide * bx, wide, n, xs)
    first_t = first_t[:, :, back]
    groups_of = [[0] + near] + [[d] for d in far]
    first_t3 = left_form(
        jnp.concatenate([first_t[:, :, jnp.array(g)].reshape(wide * bx, -1) for g in groups_of], axis=1)
    )

    a, source = forward(index, state, volatility, *state_x, *state_y, wide)
    a = after(a, *pick(cot_lines, early))
    cot_lines = send(cot_lines, far, *pick(cot_lines, near))
    forward_lines = after(first([across(a)], first_n3, 1), *pick(cot_lines, far), second_t3, third_t3)
    back = second(after(cot_lines, forward_lines), second_t3, third_t3, wide)
    solved = across(forward_lines)

    lifted_pieces = lifted(index, solved, state, *state_x, *state_y, n)
    back, carried_chunks, gone = cross_both(back, (solved,), lifted_pieces, near, far)
    carried_lines = first(carried_chunks, first_t3, 1)
    level_lines = send(lifted_pieces, late, gone)
    carried = across(after(carried_lines, *pick(level_lines, late)))

    level_lines = send(level_lines, far, *pick(level_lines, late))
    carried = after(carried, *pick(level_lines, far))
    carried_y = y_edges(carried)
    level_lines = send(level_lines, early, *carried_y)
    totals = react(index, carried, *carried_y, volatility, *vol_x, *vol_y, cotangent, n)
    total_lines = send(totals, near)
    total_lines = send(total_lines, far, *pick(total_lines, near))

    level = second(after(level_lines, totals), second_n3, third_n3, 0)[0]
    drift_pieces = mix(index, level, n)

    def frozen_rows(rows):
        padded = jnp.pad(rows, ((0, 0), (1, 1)))
        curved = padded[:, 2:] + padded[:, :-2] - 2.0 * rows
        return rows + damping * jnp.dot(curved, solve_third.T, precision=lax.Precision.HIGHEST)

    patch_t = patch_index[:, :, None]
    weight, sums = frozen(
        index,
        after(state, *drift_pieces),
        *state_x,
        frozen_rows(state_y[0]),
        frozen_rows(state_y[1]),
        third_n3,
        volatility,
        carried,
        patch_index,
        patch_t,
        groups,
    )

    total_lines = after(total_lines, drift_pieces, sums)
    drifts = send(drift_pieces, early, *total_lines)
    uppers = after(second(total_lines, second_t3, third_t3, wide), *pick(drifts, early))
    uppers, start_chunks, gone = cross_both(uppers, (), (), near, far)
    start_lines = first(start_chunks, first_t3, 1)
    drifts = send(drifts, late, gone)
    start = across(after(start_lines, *pick(drifts, late)))

    order = (here - jnp.arange(n)) % n
    edge_low = jnp.stack([piece[0, :, 0] for piece in uppers])[order].reshape(bx, bz)
    edge_high = jnp.stack([piece[-1, :, -1] for piece in uppers])[order].reshape(bx, bz)
    upper_y = neighbours(edge_low, edge_high, "narrow")
    drifts = send(drifts, far, *pick(drifts, late), *upper_y)
    tail = gather_lines(index, totals, uppers, cotangent, *upper_y, third_t3)

    start = after(start, tail)
    start_y = y_edges(start)
    start = after(start, *start_y)
    sums = column_sums(index, drifts, weight, source, start, patch_index, patch_t, sums)
    count, joint = n * wide, ("wide", "narrow")
    sums = (sums[:, :128] + sums[:, 128:]).reshape(count, PATCHES // count)
    shares = lax.all_to_all(sums, joint, split_axis=0, concat_axis=0, tiled=True)
    vega = jnp.sum(shares, axis=0)

    adjoint = finish(index, start, *start_y, volatility, *vol_x, *vol_y, tail)
    return (adjoint, vega * vega_scale)


def on_device(*args):
    n, wide = lax.axis_size("narrow"), lax.axis_size("wide")
    bx, by, bz = args[0].shape
    aligned = bx % (n * PLANES) == 0 and by % 128 == 0 and by % (wide * 8) == 0 and bz == 128
    aligned = aligned and PATCHES % (n * wide) == 0 and by // wide % 2 == 0
    return on_device_kernels(*args) if aligned else on_device_plain(*args)


def solution(mesh):
    placed = (
        P("wide", "narrow", None),
        P("wide", "narrow", None),
        P("wide", "narrow", None),
        P(),
        P(),
        P(),
        P("wide", "narrow"),
    )
    return jax.shard_map(
        on_device,
        mesh=mesh,
        in_specs=placed,
        out_specs=(P("wide", "narrow", None), P(("wide", "narrow"))),
        check_vma=False,
    )
```

```python
import functools
import jax
import jax.numpy as jnp
from jax import lax
from jax.experimental import pallas as pl
from jax.experimental.layout import Layout, with_layout_constraint
from jax.experimental.pallas import tpu as pltpu
from jax.sharding import PartitionSpec as P

PATCHES = 3072


time_step = 0.4
theta_weight = 0.5
frozen_coef = 0.2
correction = 0.5 * 0.4
vega_scale = 1.0 / 32.0
correlations = ((0, 1, 0.5), (0, 2, 0.3), (1, 2, -0.4))


def padded_2(cells, sides, width):
    for axis, dim in sides:
        count = lax.axis_size(axis)
        ends = count - 1
        head = lax.slice_in_dim(cells, 0, width, axis=dim)
        tail = lax.slice_in_dim(cells, cells.shape[dim] - width, cells.shape[dim], axis=dim)
        cells = jnp.concatenate(
            [
                lax.ppermute(tail, axis, [(i, (i + 1) % count) for i in range(ends)]),
                cells,
                lax.ppermute(head, axis, [((i + 1) % count, i) for i in range(ends)]),
            ],
            axis=dim,
        )
    return cells


def along_third(values, offset):
    if offset == 0:
        return values
    zero_layer = jnp.zeros_like(values[..., :1])
    if offset > 0:
        return jnp.concatenate([values[..., 1:], zero_layer], axis=-1)
    return jnp.concatenate([zero_layer, values[..., :-1]], axis=-1)


def shifted(padded, offsets):
    lead = padded.ndim - 3
    slices = [slice(None)] * lead
    for position in range(2):
        offset = offsets[position]
        length = padded.shape[lead + position]
        slices.append(slice(1 + offset, length - 1 + offset))
    slices.append(slice(None))
    return along_third(padded[tuple(slices)], offsets[2])


def second_parts(padded):
    centre = shifted(padded, [0, 0, 0])
    result = []
    for axis_number in range(3):
        upward = [0, 0, 0]
        upward[axis_number] = 1
        downward = [0, 0, 0]
        downward[axis_number] = -1
        result.append(shifted(padded, upward) + shifted(padded, downward) - 2.0 * centre)
    return tuple(result)


def cross_term(padded, first_axis, second_axis):

    def corner(sign_first, sign_second):
        offsets = [0, 0, 0]
        offsets[first_axis] = sign_first
        offsets[second_axis] = sign_second
        return shifted(padded, offsets)

    return 0.25 * (corner(1, 1) - corner(1, -1) - corner(-1, 1) + corner(-1, -1))


def mixed_of(padded):
    total = None
    for first_axis, second_axis, weight in correlations:
        term = weight * cross_term(padded, first_axis, second_axis)
        total = term if total is None else total + term
    return total


def contract(matrix, field, axis_number, transposed):
    letters = "xyz"
    source = letters[axis_number]
    matrix_form = source + "w" if transposed else "w" + source
    result_form = letters.replace(source, "w")
    return jnp.einsum(
        matrix_form + "," + letters + "->" + result_form,
        matrix,
        field,
        precision=lax.Precision.HIGHEST,
    )


def line_x(field, matrix, transposed):

    def solve_lines(pieces):
        solved = contract(matrix, pieces, 0, transposed)
        return lax.all_to_all(solved, "wide", split_axis=0, concat_axis=1, tiled=True)

    return solve_lines(lax.all_to_all(field, "wide", split_axis=1, concat_axis=0, tiled=True))


def line_y(field, matrix, transposed):

    def solve_lines(pieces):
        solved = contract(matrix, pieces, 1, transposed)
        return lax.all_to_all(solved, "narrow", split_axis=1, concat_axis=2, tiled=True)

    return solve_lines(lax.all_to_all(field, "narrow", split_axis=2, concat_axis=1, tiled=True))


def rimmed(stacked):
    return padded_2(stacked, (("wide", 1), ("narrow", 2)), 1)


def third_second(field):
    return along_third(field, 1) + along_third(field, -1) - 2.0 * field


def on_device_plain(state, volatility, cotangent, solve_first, solve_second, solve_third, patch_index):
    coefficient = 0.5 * volatility * volatility
    padded = rimmed(state[None])
    parts = second_parts(padded)
    second_x, second_y, second_z = (parts[0][0], parts[1][0], parts[2][0])
    source = mixed_of(padded)[0] + second_x + second_y + second_z
    start = state + time_step * coefficient * source
    damping = theta_weight * time_step * frozen_coef
    level = line_x(start - damping * second_x, solve_first, False)
    level = line_y(level - damping * second_y, solve_second, False)
    level = contract(solve_third, level - damping * second_z, 2, False)
    drift = mixed_of(rimmed((level - state)[None]))[0]
    back_third = contract(solve_third, cotangent, 2, True)
    back_second = line_y(back_third, solve_second, True)
    carried = line_x(back_second, solve_first, True)
    reaction = mixed_of(rimmed((correction * coefficient * carried)[None]))[0]
    total = cotangent + reaction
    upper_third = contract(solve_third, total, 2, True)
    upper_second = line_y(upper_third, solve_second, True)
    adjoint_start = line_x(upper_second, solve_first, True)
    scaled = time_step * coefficient * adjoint_start
    padded = rimmed(jnp.stack([scaled, adjoint_start, upper_second]))
    parts = second_parts(padded)
    spread = mixed_of(padded[0:1])[0] + parts[0][0] + parts[1][0] + parts[2][0]
    lines = parts[0][1] + parts[1][2] + third_second(upper_third)
    adjoint = adjoint_start + spread - reaction - damping * lines
    sensitivity = volatility * (correction * carried * drift + time_step * adjoint_start * source)
    column = jnp.sum(sensitivity, axis=2)
    partial_sums = jax.ops.segment_sum(
        column.reshape(-1), patch_index.reshape(-1), num_segments=PATCHES
    )
    vega = lax.psum_scatter(partial_sums, ("wide", "narrow"), scatter_dimension=0, tiled=True)
    return (adjoint, vega * vega_scale)


F32 = jnp.float32
BF16 = jnp.bfloat16
damping = 0.5 * 0.4 * 0.2
MIB = 1024 * 1024
PLANES = 8


def params(mib):
    return pltpu.CompilerParams(vmem_limit_bytes=60 * MIB)


def cost(flops, mib):
    return pl.CostEstimate(flops=int(flops / 50), bytes_accessed=int(mib * MIB / 50), transcendentals=0)


def halves(x):
    high = lax.reduce_precision(x, 8, 7)
    return high.astype(BF16), (x - high).astype(BF16)


def left_form(matrix):
    high, low = halves(matrix)
    return jnp.concatenate([high, high, low], axis=1)


def right_form(matrix):
    high, low = halves(matrix)
    return jnp.concatenate([high, high, low], axis=0)


def split(x):
    high = x.astype(BF16)
    return high, (x - high.astype(F32)).astype(BF16)


def left_product(matrix3, field):
    high, low = split(field)
    return jnp.dot(matrix3, jnp.concatenate([high, low, high], axis=0), preferred_element_type=F32)


def right_product(field, matrix3):
    high, low = split(field)
    return jnp.dot(jnp.concatenate([high, low, high], axis=1), matrix3, preferred_element_type=F32)


def y_pair(v, low_row, high_row):
    n = v.shape[0]
    row = lax.broadcasted_iota(jnp.int32, (8, v.shape[1]), 0)
    up, down = pltpu.roll(v, n - 1, 0), pltpu.roll(v, 1, 0)
    up = jnp.concatenate([up[: n - 8], jnp.where(row == 7, high_row, up[n - 8 :])], axis=0)
    down = jnp.concatenate([jnp.where(row == 0, low_row, down[:8]), down[8:]], axis=0)
    return up, down


def z_pair(v):
    n = v.shape[1]
    lane = lax.broadcasted_iota(jnp.int32, v.shape, 1)
    up = jnp.where(lane == n - 1, 0.0, pltpu.roll(v, n - 1, 1))
    down = jnp.where(lane == 0, 0.0, pltpu.roll(v, 1, 1))
    return up, down


def sweep(count, plane, rows, emit, full):
    v, p, rest, inner = {}, {}, {}, {}
    for k in range(-1, count + 1):
        centre = plane(k)
        y_up, y_down = y_pair(centre, *rows(k))
        z_up, z_down = z_pair(centre)
        e = y_up - y_down
        v[k] = centre
        p[k] = 0.125 * e + 0.075 * (z_up - z_down)
        if 0 <= k < count:
            e_up, e_down = z_pair(e)
            rest[k] = -0.1 * (e_up - e_down)
            if full:
                inner[k] = (y_up + y_down) + (z_up + z_down) - 4.0 * centre
        if k >= 1:
            mixed = (p[k] - p[k - 2]) + rest[k - 1]
            emit(k - 1, v[k - 1], v[k - 2], v[k], mixed, inner.get(k - 1))


def chunk_plane(ref, x):
    value = ref[:, x]
    return value.reshape(value.shape[0] * value.shape[1], value.shape[2])


def plane_specs(step_block, last, shape):
    tail = shape[1:]
    return [
        pl.BlockSpec((PLANES,) + tail, lambda s, i: (step_block(s, i), 0, 0)),
        pl.BlockSpec((1,) + tail, lambda s, i: (jnp.maximum(step_block(s, i) * PLANES - 1, 0), 0, 0)),
        pl.BlockSpec((1,) + tail, lambda s, i: (jnp.minimum(step_block(s, i) * PLANES + PLANES, last), 0, 0)),
    ]


def whole(shape):
    return pl.BlockSpec(shape, lambda s, i: (0,) * len(shape))


def pick_plane(k, count, block, main, before, after, low, high, blocks):
    if k < 0:
        return jnp.where(block == 0, low[0], before[0])
    if k >= count:
        return jnp.where(block == blocks - 1, high[0], after[0])
    return main[k]


def natural(s, i):
    return s


def rotated(per, n):
    def block(s, i):
        return lax.rem(i[0] + s // per, n) * per + lax.rem(s, per)

    return block


def piece_map(d, per):
    return lambda s: jnp.clip(s - d * per, 0, per - 1)


def forward_kernel(i, state, before, after, low, high, y_low, y_high, volatility, a_out, source_out, *, blocks):
    block = pl.program_id(0)

    def emit(k, v, prev, nxt, mixed, inner):
        second_x = prev + nxt - 2.0 * v
        source = mixed + second_x + inner
        sigma = volatility[k]
        a = v + (time_step * 0.5) * sigma * sigma * source - damping * second_x
        a_out[:, k] = a.reshape(a_out.shape[0], a_out.shape[2], a_out.shape[3])
        source_out[k] = time_step * sigma * source

    sweep(
        PLANES,
        lambda k: pick_plane(k, PLANES, block, state, before, after, low, high, blocks),
        lambda k: (y_low[pl.ds(block * PLANES + k + 1, 1), :], y_high[pl.ds(block * PLANES + k + 1, 1), :]),
        emit,
        True,
    )


def forward(index, state, volatility, low, high, y_low, y_high, wide):
    bx, by, bz = state.shape
    blocks = bx // PLANES
    return pl.pallas_call(
        functools.partial(forward_kernel, blocks=blocks),
        grid_spec=pltpu.PrefetchScalarGridSpec(
            num_scalar_prefetch=1,
            grid=(blocks,),
            in_specs=plane_specs(natural, bx - 1, state.shape)
            + [whole(low.shape), whole(high.shape), whole(y_low.shape), whole(y_high.shape)]
            + [pl.BlockSpec((PLANES, by, bz), lambda s, i: (s, 0, 0))],
            out_specs=[
                pl.BlockSpec((wide, PLANES, by // wide, bz), lambda s, i: (0, s, 0, 0)),
                pl.BlockSpec((PLANES, by, bz), lambda s, i: (s, 0, 0)),
            ],
        ),
        out_shape=[
            jax.ShapeDtypeStruct((wide, bx, by // wide, bz), F32),
            jax.ShapeDtypeStruct(state.shape, F32),
        ],
        compiler_params=params(32),
        cost_estimate=cost(5e9, 17),
        name="forward",
    )(index, state, state, state, low, high, y_low, y_high, volatility)


def first_kernel(*refs, count, lines, parts, length, halo):
    pieces, matrix3, out = refs[:count], refs[count], refs[count + 1]
    pieces = [piece.reshape(piece.shape[0] * lines, piece.shape[2]) for piece in pieces]
    out = out.reshape(out.shape[0] * lines, out.shape[2])
    rows = length + 2 * halo

    def pair(step, carry):
        y = step * 2
        field = jnp.concatenate(
            [
                jnp.concatenate(
                    [piece[pl.ds(y + t, piece.shape[0] // lines, stride=lines), :] for piece in pieces], axis=0
                )
                for t in range(2)
            ],
            axis=1,
        )
        solved = left_product(matrix3[...], field)
        width = solved.shape[1] // 2
        for t in range(2):
            half = solved[:, t * width : (t + 1) * width]
            for part in range(parts):
                base = part * rows
                out[pl.ds((base + halo) * lines + y + t, length, stride=lines), :] = half[part * length : (part + 1) * length]
                if halo:
                    zero = jnp.zeros((1, width), F32)
                    before = half[part * length - 1 : part * length] if part > 0 else zero
                    after = half[(part + 1) * length : (part + 1) * length + 1] if part < parts - 1 else zero
                    out[pl.ds(base * lines + y + t, 1), :] = before
                    out[pl.ds((base + rows - 1) * lines + y + t, 1), :] = after
        return carry

    lax.fori_loop(0, lines // 2, pair, 0)


def first(pieces, matrix3, halo):
    wide = pieces[0].shape[0]
    lines, bz = pieces[0].shape[2:]
    length = sum(piece.shape[1] for piece in pieces)
    rows = length + 2 * halo
    flat = [piece.reshape(-1, lines, bz) for piece in pieces]
    block = 8
    out = pl.pallas_call(
        functools.partial(first_kernel, count=len(flat), lines=block, parts=wide, length=length, halo=halo),
        grid=(lines // block,),
        in_specs=[pl.BlockSpec((piece.shape[0], block, bz), lambda s: (0, s, 0)) for piece in flat]
        + [pl.BlockSpec(matrix3.shape, lambda s: (0, 0))],
        out_specs=pl.BlockSpec((wide * rows, block, bz), lambda s: (0, s, 0)),
        out_shape=jax.ShapeDtypeStruct((wide * rows, lines, bz), F32),
        compiler_params=params(40),
        cost_estimate=cost(7e9, 10),
        name="first",
    )(*flat, matrix3)
    return out.reshape(wide, rows, lines, bz)


def second_kernel(*refs, count, chunked):
    pieces, second3, third3, outs = refs[:count], refs[count], refs[count + 1], refs[count + 2 :]
    per, by, bz = pieces[0].shape
    length = count * by
    field = jnp.concatenate([piece[x] for x in range(per) for piece in pieces], axis=0)
    field = right_product(field, third3[...])
    field = jnp.concatenate([field[x * length : (x + 1) * length] for x in range(per)], axis=1)
    solved = left_product(second3[...], field)
    for x in range(per):
        half = solved[:, x * bz : (x + 1) * bz]
        if chunked:
            for d in range(count):
                out = outs[d]
                out[:, x] = half[d * by : (d + 1) * by].reshape(out.shape[0], out.shape[2], bz)
        else:
            outs[0][x] = half


def second(pieces, second3, third3, wide):
    count = len(pieces)
    xs, by, bz = pieces[0].shape
    per = 2
    if wide:
        out_specs = [pl.BlockSpec((wide, per, by // wide, bz), lambda s: (0, s, 0, 0))] * count
        out_shape = [jax.ShapeDtypeStruct((wide, xs, by // wide, bz), F32)] * count
    else:
        out_specs = [pl.BlockSpec((per, count * by, bz), lambda s: (s, 0, 0))]
        out_shape = [jax.ShapeDtypeStruct((xs, count * by, bz), F32)]
    return pl.pallas_call(
        functools.partial(second_kernel, count=count, chunked=bool(wide)),
        grid=(xs // per,),
        in_specs=[pl.BlockSpec((per, by, bz), lambda s: (s, 0, 0))] * count
        + [pl.BlockSpec(second3.shape, lambda s: (0, 0)), pl.BlockSpec(third3.shape, lambda s: (0, 0))],
        out_specs=out_specs,
        out_shape=out_shape,
        compiler_params=params(40),
        cost_estimate=cost(9e9, 10),
        name="second",
    )(*pieces, second3, third3)


def piece_specs(size, tail, per, n):
    return [pl.BlockSpec((size,) + tail, lambda s, i, d=d: (jnp.clip(s - d * per, 0, per - 1), 0, 0)) for d in range(n)]


def chunk_piece_specs(wide, lines, bz, per, order):
    return [
        pl.BlockSpec((wide, PLANES, lines, bz), lambda s, i, d=d: (0, jnp.clip(s - d * per, 0, per - 1), 0, 0))
        for d in order
    ]


def store_piece(outs, turn, kept):
    for d, out in enumerate(outs):

        @pl.when(turn == d)
        def _(out=out):
            out[...] = kept[...]


def select(values, turn):
    result = values[0]
    for d in range(1, len(values)):
        result = jnp.where(turn == d, values[d], result)
    return result


def lifted_kernel(i, solved, state, low, high, y_low, y_high, *refs, per, n, size, xs):
    outs, kept = refs[:n], refs[n]
    step = pl.program_id(0)
    bx = state.shape[0]
    base = lax.rem(i[0] + step // per, n) * xs + lax.rem(step, per) * size
    for k in range(size):
        row = base + k
        v = state[jnp.clip(row - 1, 0, bx - 1)]
        v = jnp.where(row == 0, low[0], jnp.where(row == bx + 1, high[0], v))
        up, down = y_pair(v, y_low[pl.ds(row, 1), :], y_high[pl.ds(row, 1), :])
        kept[k] = chunk_plane(solved, row) - damping * (up + down - 2.0 * v)
    store_piece(outs, step // per, kept)


def lifted(index, solved, state, low, high, y_low, y_high, n):
    bx, by, bz = state.shape
    xs = bx // n
    size = next(k for k in range(9, 0, -1) if (xs + 2) % k == 0)
    per = (xs + 2) // size
    return pl.pallas_call(
        functools.partial(lifted_kernel, per=per, n=n, size=size, xs=xs),
        grid_spec=pltpu.PrefetchScalarGridSpec(
            num_scalar_prefetch=1,
            grid=(n * per,),
            in_specs=[whole(v.shape) for v in (solved, state, low, high, y_low, y_high)],
            out_specs=piece_specs(size, (by, bz), per, n),
            scratch_shapes=[pltpu.VMEM((size, by, bz), F32)],
        ),
        out_shape=[jax.ShapeDtypeStruct((xs + 2, by, bz), F32)] * n,
        compiler_params=params(32),
        cost_estimate=cost(2e9, 13),
        name="lifted",
    )(index, solved, state, low, high, y_low, y_high)


def reaction_kernel(
    i, carried, carried_low, carried_high, vol, before, after, low, high, vol_low, vol_high, cotangent, *refs, per, n, blocks
):
    outs, kept = refs[:n], refs[n]
    step = pl.program_id(0)
    block = rotated(per, n)(step, i)

    def plane(k):
        sigma = pick_plane(k, PLANES, block, vol, before, after, low, high, blocks)
        return (0.5 * correction) * sigma * sigma * chunk_plane(carried, block * PLANES + k + 1)

    def rows(k):
        at = pl.ds(block * PLANES + k + 1, 1)
        s_low, s_high = vol_low[at, :], vol_high[at, :]
        return (
            (0.5 * correction) * s_low * s_low * carried_low[at, :],
            (0.5 * correction) * s_high * s_high * carried_high[at, :],
        )

    def emit(k, v, prev, nxt, mixed, inner):
        kept[k] = cotangent[k] + mixed

    sweep(PLANES, plane, rows, emit, False)
    store_piece(outs, step // per, kept)


def react(index, carried, carried_low, carried_high, vol, low, high, vol_low, vol_high, cotangent, n):
    bx, by, bz = vol.shape
    xs = bx // n
    per = xs // PLANES
    block = rotated(per, n)
    return pl.pallas_call(
        functools.partial(reaction_kernel, per=per, n=n, blocks=bx // PLANES),
        grid_spec=pltpu.PrefetchScalarGridSpec(
            num_scalar_prefetch=1,
            grid=(n * per,),
            in_specs=[whole(carried.shape), whole(carried_low.shape), whole(carried_high.shape)]
            + plane_specs(block, bx - 1, vol.shape)
            + [whole(low.shape), whole(high.shape), whole(vol_low.shape), whole(vol_high.shape)]
            + [pl.BlockSpec((PLANES, by, bz), lambda s, i: (block(s, i), 0, 0))],
            out_specs=piece_specs(PLANES, (by, bz), per, n),
            scratch_shapes=[pltpu.VMEM((PLANES, by, bz), F32)],
        ),
        out_shape=[jax.ShapeDtypeStruct((xs, by, bz), F32)] * n,
        compiler_params=params(40),
        cost_estimate=cost(4e9, 17),
        name="reaction",
    )(index, carried, carried_low, carried_high, vol, vol, vol, low, high, vol_low, vol_high, cotangent)


def lines_kernel(i, *refs, per, n):
    totals, uppers = refs[:n], refs[n : 2 * n]
    cotangent, upper_low, upper_high, third3, out = refs[2 * n :]
    step = pl.program_id(0)
    turn = step // per
    block = rotated(per, n)(step, i)
    for k in range(PLANES):
        total = select([ref[k] for ref in totals], turn)
        upper = select([chunk_plane(ref, k) for ref in uppers], turn)
        at = pl.ds(block * PLANES + k, 1)
        up, down = y_pair(upper, upper_low[at, :], upper_high[at, :])
        third = right_product(total, third3[...])
        z_up, z_down = z_pair(third)
        lines = (up + down - 2.0 * upper) + (z_up + z_down - 2.0 * third)
        out[k] = cotangent[k] - total - damping * lines


def gather_lines(index, totals, uppers, cotangent, upper_low, upper_high, third3):
    n = len(totals)
    bx, by, bz = cotangent.shape
    xs = bx // n
    per = xs // PLANES
    wide, lines = uppers[0].shape[0], uppers[0].shape[2]
    block = rotated(per, n)
    order = [(n - e) % n for e in range(n)]
    return pl.pallas_call(
        functools.partial(lines_kernel, per=per, n=n),
        grid_spec=pltpu.PrefetchScalarGridSpec(
            num_scalar_prefetch=1,
            grid=(n * per,),
            in_specs=piece_specs(PLANES, (by, bz), per, n)
            + chunk_piece_specs(wide, lines, bz, per, range(n))
            + [pl.BlockSpec((PLANES, by, bz), lambda s, i: (block(s, i), 0, 0))]
            + [whole(upper_low.shape), whole(upper_high.shape), whole(third3.shape)],
            out_specs=pl.BlockSpec((PLANES, by, bz), lambda s, i: (block(s, i), 0, 0)),
        ),
        out_shape=jax.ShapeDtypeStruct(cotangent.shape, F32),
        compiler_params=params(40),
        cost_estimate=cost(5e9, 17),
        name="lines",
    )(index, *totals, *[uppers[order[d]] for d in range(n)], cotangent, upper_low, upper_high, third3)


def mixed_kernel(i, field, *refs, n):
    outs, scratch = refs[:n], refs[n]
    by = outs[0].shape[1]

    def emit(k, v, prev, nxt, mixed, inner):
        scratch[...] = mixed
        for d, out in enumerate(outs):
            start = pl.multiple_of(lax.rem(i[0] + d, n) * by, by)
            out[k] = scratch[pl.ds(start, by), :]

    zero = jnp.zeros((1, field.shape[2]), F32)
    sweep(field.shape[0] - 2, lambda k: field[k + 1], lambda k: (zero, zero), emit, False)


def mix(index, field, n):
    rows, ny, bz = field.shape
    xs, by = rows - 2, ny // n
    return pl.pallas_call(
        functools.partial(mixed_kernel, n=n),
        grid_spec=pltpu.PrefetchScalarGridSpec(
            num_scalar_prefetch=1,
            grid=(1,),
            in_specs=[whole(field.shape)],
            out_specs=[whole((xs, by, bz))] * n,
            scratch_shapes=[pltpu.VMEM((ny, bz), F32)],
        ),
        out_shape=[jax.ShapeDtypeStruct((xs, by, bz), F32)] * n,
        compiler_params=params(40),
        cost_estimate=cost(4e9, 9),
        name="mixed",
    )(index, field)


def patch_sums(out, step, planes, patch, patch_t, groups):
    @pl.when(step == 0)
    def _():
        out[...] = jnp.zeros_like(out)

    count, (by, bz) = len(planes), planes[0].shape
    value_high, value_low = split(jnp.concatenate(planes, axis=0))
    ones = jnp.ones((2 * bz, 128), BF16)
    column = jnp.dot(jnp.concatenate([value_high, value_low], axis=1), ones, preferred_element_type=F32)
    number = jnp.concatenate([patch[pl.ds(k, 1), :] for k in range(count)], axis=1)
    coarse = lax.broadcasted_iota(jnp.int32, (groups, count * by), 0) == lax.shift_right_logical(number, 7)
    number_t = patch_t[...].reshape(count * by, 1)
    lane = lax.broadcasted_iota(jnp.int32, (count * by, 128), 1)
    high, low = split(jnp.where(lane == lax.bitwise_and(number_t, 127), column, 0.0))
    out[...] += jnp.dot(
        jnp.where(coarse, 1.0, 0.0).astype(BF16), jnp.concatenate([high, low], axis=1), preferred_element_type=F32
    )


def frozen_kernel(
    i, state, before, after, low, high, q_low, q_high, third3, vol, carried, patch, patch_t, weight, out, *, blocks, groups
):
    block = pl.program_id(0)
    planes = []

    def plane(k):
        v = pick_plane(k, PLANES, block, state, before, after, low, high, blocks)
        up, down = z_pair(v)
        return v + damping * right_product(up + down - 2.0 * v, third3[...])

    def emit(k, v, prev, nxt, mixed, inner):
        w = correction * vol[k] * chunk_plane(carried, block * PLANES + k + 1)
        weight[k] = w
        planes.append(-w * mixed)

    sweep(
        PLANES,
        plane,
        lambda k: (q_low[pl.ds(block * PLANES + k + 1, 1), :], q_high[pl.ds(block * PLANES + k + 1, 1), :]),
        emit,
        False,
    )
    patch_sums(out, block, planes, patch, patch_t, groups)


def frozen(index, state, low, high, q_low, q_high, third3, vol, carried, patch, patch_t, groups):
    bx, by, bz = state.shape
    blocks = bx // PLANES
    main = pl.BlockSpec((PLANES, by, bz), lambda s, i: (s, 0, 0))
    return pl.pallas_call(
        functools.partial(frozen_kernel, blocks=blocks, groups=groups),
        grid_spec=pltpu.PrefetchScalarGridSpec(
            num_scalar_prefetch=1,
            grid=(blocks,),
            in_specs=plane_specs(natural, bx - 1, state.shape)
            + [whole(low.shape), whole(high.shape), whole(q_low.shape), whole(q_high.shape), whole(third3.shape)]
            + [main, whole(carried.shape)]
            + [pl.BlockSpec((PLANES, by), lambda s, i: (s, 0))]
            + [pl.BlockSpec((PLANES, by, 1), lambda s, i: (s, 0, 0))],
            out_specs=[main, whole((groups, 256))],
        ),
        out_shape=[jax.ShapeDtypeStruct(state.shape, F32), jax.ShapeDtypeStruct((groups, 256), F32)],
        compiler_params=params(32),
        cost_estimate=cost(5e9, 17),
        name="frozen",
    )(index, state, state, state, low, high, q_low, q_high, third3, vol, carried, patch, patch_t)


def column_kernel(i, *refs, per, n, groups):
    drifts = refs[:n]
    weight, source, start, patch, patch_t, given, out = refs[n:]
    step = pl.program_id(0)
    turn = step // per
    block = rotated(per, n)(step, i)
    planes = [
        weight[k] * select([ref[k] for ref in drifts], turn)
        + source[k] * chunk_plane(start, block * PLANES + k + 1)
        for k in range(PLANES)
    ]
    patch_sums(out, step, planes, patch, patch_t, groups)

    @pl.when(step == pl.num_programs(0) - 1)
    def _():
        out[...] += given[...]


def column_sums(index, drifts, weight, source, start, patch, patch_t, given):
    n = len(drifts)
    bx, by, bz = source.shape
    xs = bx // n
    per = xs // PLANES
    groups = given.shape[0]
    block = rotated(per, n)
    order = [(n - e) % n for e in range(n)]
    main = pl.BlockSpec((PLANES, by, bz), lambda s, i: (block(s, i), 0, 0))
    return pl.pallas_call(
        functools.partial(column_kernel, per=per, n=n, groups=groups),
        grid_spec=pltpu.PrefetchScalarGridSpec(
            num_scalar_prefetch=1,
            grid=(n * per,),
            in_specs=piece_specs(PLANES, (by, bz), per, n)
            + [main, main, whole(start.shape)]
            + [pl.BlockSpec((PLANES, by), lambda s, i: (block(s, i), 0))]
            + [pl.BlockSpec((PLANES, by, 1), lambda s, i: (block(s, i), 0, 0)), whole(given.shape)],
            out_specs=whole(given.shape),
        ),
        out_shape=jax.ShapeDtypeStruct(given.shape, F32),
        compiler_params=params(40),
        cost_estimate=cost(4e9, 17),
        name="column",
    )(index, *[drifts[order[d]] for d in range(n)], weight, source, start, patch, patch_t, given)


def adjoint_kernel(
    i, start, start_low, start_high, vol, before, after, low, high, vol_low, vol_high, tail, out, *, blocks
):
    block = pl.program_id(0)
    raw = {}

    def plane(k):
        sigma = pick_plane(k, PLANES, block, vol, before, after, low, high, blocks)
        raw[k] = chunk_plane(start, block * PLANES + k + 1)
        return (0.5 * time_step) * sigma * sigma * raw[k]

    def rows(k):
        at = pl.ds(block * PLANES + k + 1, 1)
        s_low, s_high = vol_low[at, :], vol_high[at, :]
        return (
            (0.5 * time_step) * s_low * s_low * start_low[at, :],
            (0.5 * time_step) * s_high * s_high * start_high[at, :],
        )

    def emit(k, v, prev, nxt, mixed, inner):
        spread = mixed + (prev + nxt - 2.0 * v) + inner
        lines = raw[k - 1] + raw[k + 1] - 2.0 * raw[k]
        out[k] = raw[k] + spread + tail[k] - damping * lines

    sweep(PLANES, plane, rows, emit, True)


def finish(index, start, start_low, start_high, vol, low, high, vol_low, vol_high, tail):
    bx, by, bz = vol.shape
    return pl.pallas_call(
        functools.partial(adjoint_kernel, blocks=bx // PLANES),
        grid_spec=pltpu.PrefetchScalarGridSpec(
            num_scalar_prefetch=1,
            grid=(bx // PLANES,),
            in_specs=[whole(start.shape), whole(start_low.shape), whole(start_high.shape)]
            + plane_specs(natural, bx - 1, vol.shape)
            + [whole(low.shape), whole(high.shape), whole(vol_low.shape), whole(vol_high.shape)]
            + [pl.BlockSpec((PLANES, by, bz), lambda s, i: (s, 0, 0))],
            out_specs=pl.BlockSpec((PLANES, by, bz), lambda s, i: (s, 0, 0)),
        ),
        out_shape=jax.ShapeDtypeStruct(vol.shape, F32),
        compiler_params=params(40),
        cost_estimate=cost(5e9, 17),
        name="adjoint",
    )(index, start, start_low, start_high, vol, vol, vol, low, high, vol_low, vol_high, tail)


def neighbours(low_edge, high_edge, axis):
    count = lax.axis_size(axis)
    up = [(k, k + 1) for k in range(count - 1)]
    down = [(k + 1, k) for k in range(count - 1)]
    return lax.ppermute(high_edge, axis, up), lax.ppermute(low_edge, axis, down)


def far_and_near(n):
    return [n // 2] if n > 1 else [], [d for d in range(1, n) if d != n // 2]


def send(pieces, chosen, *earlier):
    n = len(pieces)
    result = list(pieces)
    for d in chosen:
        piece = after(pieces[d], *earlier) if earlier else pieces[d]
        result[d] = lax.ppermute(piece, "narrow", [(k, (k + d) % n) for k in range(n)])
    return result


def pick(pieces, chosen):
    return [pieces[d] for d in chosen]


def after(value, *earlier):
    return lax.optimization_barrier((value, earlier))[0]


def across(piece):
    return lax.all_to_all(piece, "wide", split_axis=0, concat_axis=0, tiled=True)


def row_major(value):
    return with_layout_constraint(value, Layout(major_to_minor=tuple(range(value.ndim))))


def cross_both(pieces, before, between, near, far):
    pieces = [row_major(piece) for piece in pieces]
    lines = send(pieces, near)
    lines = send(lines, far, *pick(lines, near))
    lines = [row_major(line) for line in lines]
    block = jnp.concatenate(pick(lines, [0] + near), axis=1)
    chunks = [across(after(block, *before) if before else block)]
    for d in far:
        chunks.append(across(after(lines[d], chunks[-1], *between)))
    return lines, chunks, pick(lines, far)


def y_edges(chunks):
    return neighbours(chunks[0, :, 0, :], chunks[-1, :, -1, :], "narrow")


def on_device_kernels(state, volatility, cotangent, solve_first, solve_second, solve_third, patch_index):
    n, wide = lax.axis_size("narrow"), lax.axis_size("wide")
    here = lax.axis_index("narrow")
    index = here.astype(jnp.int32).reshape(1)
    bx, by, bz = state.shape
    xs = bx // n
    groups = PATCHES // 128

    ahead = (here + jnp.arange(n)) % n
    back = (here - jnp.arange(n)) % n

    far, near = far_and_near(n)
    every = range(n)

    cot_pieces = [lax.dynamic_slice_in_dim(cotangent, ahead[d] * xs, xs, 0) for d in range(n)]
    early, late = near[:1], near[1:]
    both_low, both_high = neighbours(
        jnp.stack([state[0], volatility[0]]), jnp.stack([state[-1], volatility[-1]]), "wide"
    )
    both = jnp.stack([state[:, :: by - 1], volatility[:, :: by - 1]])
    both = jnp.concatenate([both_low[:, None, :: by - 1], both, both_high[:, None, :: by - 1]], axis=1)
    y_low, y_high = neighbours(both[:, :, 0], both[:, :, 1], "narrow")
    state_x = (both_low[0:1], both_high[0:1])
    vol_x = (both_low[1:2], both_high[1:2])
    state_y = (y_low[0], y_high[0])
    vol_y = (y_low[1], y_high[1])
    cot_lines = send(cot_pieces, near, y_low, y_high)

    second_t = solve_second.T.reshape(n, by, n, by)
    second_t3 = left_form(second_t[ahead][:, :, back].reshape(n * by, n * by))
    second_n = solve_second.reshape(n * by, n, by)
    second_n3 = left_form(second_n[:, back].reshape(n * by, n * by))
    third_t3 = right_form(solve_third)
    third_n3 = right_form(solve_third.T)
    first_n3 = left_form(solve_first)
    first_t = solve_first.T.reshape(wide * bx, wide, n, xs)
    first_t = first_t[:, :, back]
    groups_of = [[0] + near] + [[d] for d in far]
    first_t3 = left_form(
        jnp.concatenate([first_t[:, :, jnp.array(g)].reshape(wide * bx, -1) for g in groups_of], axis=1)
    )

    a, source = forward(index, state, volatility, *state_x, *state_y, wide)
    a = after(a, *pick(cot_lines, early))
    cot_lines = send(cot_lines, far, *pick(cot_lines, near))
    forward_lines = after(first([across(a)], first_n3, 1), *pick(cot_lines, far), second_t3, third_t3)
    back = second(after(cot_lines, forward_lines), second_t3, third_t3, wide)
    solved = across(forward_lines)

    lifted_pieces = lifted(index, solved, state, *state_x, *state_y, n)
    back, carried_chunks, gone = cross_both(back, (solved,), lifted_pieces, near, far)
    carried_lines = first(carried_chunks, first_t3, 1)
    level_lines = send(lifted_pieces, late, gone)
    carried = across(after(carried_lines, *pick(level_lines, late)))

    level_lines = send(level_lines, far, *pick(level_lines, late))
    carried = after(carried, *pick(level_lines, far))
    carried_y = y_edges(carried)
    level_lines = send(level_lines, early, *carried_y)
    totals = react(index, carried, *carried_y, volatility, *vol_x, *vol_y, cotangent, n)
    total_lines = send(totals, near)
    total_lines = send(total_lines, far, *pick(total_lines, near))

    uppers = second(total_lines, second_t3, third_t3, wide)
    level = second(after(level_lines, uppers), second_n3, third_n3, 0)[0]
    drift_pieces = mix(index, level, n)

    def frozen_rows(rows):
        padded = jnp.pad(rows, ((0, 0), (1, 1)))
        curved = padded[:, 2:] + padded[:, :-2] - 2.0 * rows
        return rows + damping * jnp.dot(curved, solve_third.T, precision=lax.Precision.HIGHEST)

    patch_t = patch_index[:, :, None]
    weight, sums = frozen(
        index,
        after(state, *drift_pieces),
        *state_x,
        frozen_rows(state_y[0]),
        frozen_rows(state_y[1]),
        third_n3,
        volatility,
        carried,
        patch_index,
        patch_t,
        groups,
    )

    uppers, start_chunks, gone = cross_both(uppers, (), (), near, far)
    drifts = send(drift_pieces, early, *pick(uppers, near))
    start_lines = first(start_chunks, first_t3, 1)
    drifts = send(drifts, late, gone)
    start = across(after(start_lines, *pick(drifts, near)))

    order = (here - jnp.arange(n)) % n
    edge_low = jnp.stack([piece[0, :, 0] for piece in uppers])[order].reshape(bx, bz)
    edge_high = jnp.stack([piece[-1, :, -1] for piece in uppers])[order].reshape(bx, bz)
    upper_y = neighbours(edge_low, edge_high, "narrow")
    drifts = send(drifts, far, *pick(drifts, late), *upper_y)
    tail = gather_lines(index, totals, uppers, cotangent, *upper_y, third_t3)

    start = after(start, tail)
    start_y = y_edges(start)
    start = after(start, *start_y)
    sums = column_sums(index, drifts, weight, source, start, patch_index, patch_t, sums)
    count, joint = n * wide, ("wide", "narrow")
    sums = (sums[:, :128] + sums[:, 128:]).reshape(count, PATCHES // count)
    shares = lax.all_to_all(sums, joint, split_axis=0, concat_axis=0, tiled=True)
    vega = jnp.sum(shares, axis=0)

    adjoint = finish(index, start, *start_y, volatility, *vol_x, *vol_y, tail)
    return (adjoint, vega * vega_scale)


def on_device(*args):
    n, wide = lax.axis_size("narrow"), lax.axis_size("wide")
    bx, by, bz = args[0].shape
    aligned = bx % (n * PLANES) == 0 and by % 128 == 0 and by % (wide * 8) == 0 and bz == 128
    aligned = aligned and PATCHES % (n * wide) == 0 and by // wide % 2 == 0
    return on_device_kernels(*args) if aligned else on_device_plain(*args)


def solution(mesh):
    placed = (
        P("wide", "narrow", None),
        P("wide", "narrow", None),
        P("wide", "narrow", None),
        P(),
        P(),
        P(),
        P("wide", "narrow"),
    )
    return jax.shard_map(
        on_device,
        mesh=mesh,
        in_specs=placed,
        out_specs=(P("wide", "narrow", None), P(("wide", "narrow"))),
        check_vma=False,
    )
```

```python
import functools
import jax
import jax.numpy as jnp
from jax import lax
from jax.experimental import pallas as pl
from jax.experimental.layout import Layout, with_layout_constraint
from jax.experimental.pallas import tpu as pltpu
from jax.sharding import PartitionSpec as P

PATCHES = 3072


time_step = 0.4
theta_weight = 0.5
frozen_coef = 0.2
correction = 0.5 * 0.4
vega_scale = 1.0 / 32.0
correlations = ((0, 1, 0.5), (0, 2, 0.3), (1, 2, -0.4))


def padded_2(cells, sides, width):
    for axis, dim in sides:
        count = lax.axis_size(axis)
        ends = count - 1
        head = lax.slice_in_dim(cells, 0, width, axis=dim)
        tail = lax.slice_in_dim(cells, cells.shape[dim] - width, cells.shape[dim], axis=dim)
        cells = jnp.concatenate(
            [
                lax.ppermute(tail, axis, [(i, (i + 1) % count) for i in range(ends)]),
                cells,
                lax.ppermute(head, axis, [((i + 1) % count, i) for i in range(ends)]),
            ],
            axis=dim,
        )
    return cells


def along_third(values, offset):
    if offset == 0:
        return values
    zero_layer = jnp.zeros_like(values[..., :1])
    if offset > 0:
        return jnp.concatenate([values[..., 1:], zero_layer], axis=-1)
    return jnp.concatenate([zero_layer, values[..., :-1]], axis=-1)


def shifted(padded, offsets):
    lead = padded.ndim - 3
    slices = [slice(None)] * lead
    for position in range(2):
        offset = offsets[position]
        length = padded.shape[lead + position]
        slices.append(slice(1 + offset, length - 1 + offset))
    slices.append(slice(None))
    return along_third(padded[tuple(slices)], offsets[2])


def second_parts(padded):
    centre = shifted(padded, [0, 0, 0])
    result = []
    for axis_number in range(3):
        upward = [0, 0, 0]
        upward[axis_number] = 1
        downward = [0, 0, 0]
        downward[axis_number] = -1
        result.append(shifted(padded, upward) + shifted(padded, downward) - 2.0 * centre)
    return tuple(result)


def cross_term(padded, first_axis, second_axis):

    def corner(sign_first, sign_second):
        offsets = [0, 0, 0]
        offsets[first_axis] = sign_first
        offsets[second_axis] = sign_second
        return shifted(padded, offsets)

    return 0.25 * (corner(1, 1) - corner(1, -1) - corner(-1, 1) + corner(-1, -1))


def mixed_of(padded):
    total = None
    for first_axis, second_axis, weight in correlations:
        term = weight * cross_term(padded, first_axis, second_axis)
        total = term if total is None else total + term
    return total


def contract(matrix, field, axis_number, transposed):
    letters = "xyz"
    source = letters[axis_number]
    matrix_form = source + "w" if transposed else "w" + source
    result_form = letters.replace(source, "w")
    return jnp.einsum(
        matrix_form + "," + letters + "->" + result_form,
        matrix,
        field,
        precision=lax.Precision.HIGHEST,
    )


def line_x(field, matrix, transposed):

    def solve_lines(pieces):
        solved = contract(matrix, pieces, 0, transposed)
        return lax.all_to_all(solved, "wide", split_axis=0, concat_axis=1, tiled=True)

    return solve_lines(lax.all_to_all(field, "wide", split_axis=1, concat_axis=0, tiled=True))


def line_y(field, matrix, transposed):

    def solve_lines(pieces):
        solved = contract(matrix, pieces, 1, transposed)
        return lax.all_to_all(solved, "narrow", split_axis=1, concat_axis=2, tiled=True)

    return solve_lines(lax.all_to_all(field, "narrow", split_axis=2, concat_axis=1, tiled=True))


def rimmed(stacked):
    return padded_2(stacked, (("wide", 1), ("narrow", 2)), 1)


def third_second(field):
    return along_third(field, 1) + along_third(field, -1) - 2.0 * field


def on_device_plain(state, volatility, cotangent, solve_first, solve_second, solve_third, patch_index):
    coefficient = 0.5 * volatility * volatility
    padded = rimmed(state[None])
    parts = second_parts(padded)
    second_x, second_y, second_z = (parts[0][0], parts[1][0], parts[2][0])
    source = mixed_of(padded)[0] + second_x + second_y + second_z
    start = state + time_step * coefficient * source
    damping = theta_weight * time_step * frozen_coef
    level = line_x(start - damping * second_x, solve_first, False)
    level = line_y(level - damping * second_y, solve_second, False)
    level = contract(solve_third, level - damping * second_z, 2, False)
    drift = mixed_of(rimmed((level - state)[None]))[0]
    back_third = contract(solve_third, cotangent, 2, True)
    back_second = line_y(back_third, solve_second, True)
    carried = line_x(back_second, solve_first, True)
    reaction = mixed_of(rimmed((correction * coefficient * carried)[None]))[0]
    total = cotangent + reaction
    upper_third = contract(solve_third, total, 2, True)
    upper_second = line_y(upper_third, solve_second, True)
    adjoint_start = line_x(upper_second, solve_first, True)
    scaled = time_step * coefficient * adjoint_start
    padded = rimmed(jnp.stack([scaled, adjoint_start, upper_second]))
    parts = second_parts(padded)
    spread = mixed_of(padded[0:1])[0] + parts[0][0] + parts[1][0] + parts[2][0]
    lines = parts[0][1] + parts[1][2] + third_second(upper_third)
    adjoint = adjoint_start + spread - reaction - damping * lines
    sensitivity = volatility * (correction * carried * drift + time_step * adjoint_start * source)
    column = jnp.sum(sensitivity, axis=2)
    partial_sums = jax.ops.segment_sum(
        column.reshape(-1), patch_index.reshape(-1), num_segments=PATCHES
    )
    vega = lax.psum_scatter(partial_sums, ("wide", "narrow"), scatter_dimension=0, tiled=True)
    return (adjoint, vega * vega_scale)


F32 = jnp.float32
BF16 = jnp.bfloat16
damping = 0.5 * 0.4 * 0.2
MIB = 1024 * 1024
PLANES = 8


def params(mib):
    return pltpu.CompilerParams(vmem_limit_bytes=60 * MIB)


def cost(flops, mib):
    return pl.CostEstimate(flops=int(flops / 50), bytes_accessed=int(mib * MIB / 50), transcendentals=0)


def halves(x):
    high = lax.reduce_precision(x, 8, 7)
    return high.astype(BF16), (x - high).astype(BF16)


def left_form(matrix):
    high, low = halves(matrix)
    return jnp.concatenate([high, high, low], axis=1)


def right_form(matrix):
    high, low = halves(matrix)
    return jnp.concatenate([high, high, low], axis=0)


def split(x):
    high = x.astype(BF16)
    return high, (x - high.astype(F32)).astype(BF16)


def left_product(matrix3, field):
    high, low = split(field)
    return jnp.dot(matrix3, jnp.concatenate([high, low, high], axis=0), preferred_element_type=F32)


def right_product(field, matrix3):
    high, low = split(field)
    return jnp.dot(jnp.concatenate([high, low, high], axis=1), matrix3, preferred_element_type=F32)


def y_pair(v, low_row, high_row):
    n = v.shape[0]
    row = lax.broadcasted_iota(jnp.int32, (8, v.shape[1]), 0)
    up, down = pltpu.roll(v, n - 1, 0), pltpu.roll(v, 1, 0)
    up = jnp.concatenate([up[: n - 8], jnp.where(row == 7, high_row, up[n - 8 :])], axis=0)
    down = jnp.concatenate([jnp.where(row == 0, low_row, down[:8]), down[8:]], axis=0)
    return up, down


def z_pair(v):
    n = v.shape[1]
    lane = lax.broadcasted_iota(jnp.int32, v.shape, 1)
    up = jnp.where(lane == n - 1, 0.0, pltpu.roll(v, n - 1, 1))
    down = jnp.where(lane == 0, 0.0, pltpu.roll(v, 1, 1))
    return up, down


def sweep(count, plane, rows, emit, full):
    v, p, rest, inner = {}, {}, {}, {}
    for k in range(-1, count + 1):
        centre = plane(k)
        y_up, y_down = y_pair(centre, *rows(k))
        z_up, z_down = z_pair(centre)
        e = y_up - y_down
        v[k] = centre
        p[k] = 0.125 * e + 0.075 * (z_up - z_down)
        if 0 <= k < count:
            e_up, e_down = z_pair(e)
            rest[k] = -0.1 * (e_up - e_down)
            if full:
                inner[k] = (y_up + y_down) + (z_up + z_down) - 4.0 * centre
        if k >= 1:
            mixed = (p[k] - p[k - 2]) + rest[k - 1]
            emit(k - 1, v[k - 1], v[k - 2], v[k], mixed, inner.get(k - 1))


def chunk_plane(ref, x):
    value = ref[:, x]
    return value.reshape(value.shape[0] * value.shape[1], value.shape[2])


def plane_specs(step_block, last, shape):
    tail = shape[1:]
    return [
        pl.BlockSpec((PLANES,) + tail, lambda s, i: (step_block(s, i), 0, 0)),
        pl.BlockSpec((1,) + tail, lambda s, i: (jnp.maximum(step_block(s, i) * PLANES - 1, 0), 0, 0)),
        pl.BlockSpec((1,) + tail, lambda s, i: (jnp.minimum(step_block(s, i) * PLANES + PLANES, last), 0, 0)),
    ]


def whole(shape):
    return pl.BlockSpec(shape, lambda s, i: (0,) * len(shape))


def pick_plane(k, count, block, main, before, after, low, high, blocks):
    if k < 0:
        return jnp.where(block == 0, low[0], before[0])
    if k >= count:
        return jnp.where(block == blocks - 1, high[0], after[0])
    return main[k]


def natural(s, i):
    return s


def rotated(per, n):
    def block(s, i):
        return lax.rem(i[0] + s // per, n) * per + lax.rem(s, per)

    return block


def piece_map(d, per):
    return lambda s: jnp.clip(s - d * per, 0, per - 1)


def forward_kernel(i, state, before, after, low, high, y_low, y_high, volatility, a_out, source_out, *, blocks):
    block = pl.program_id(0)

    def emit(k, v, prev, nxt, mixed, inner):
        second_x = prev + nxt - 2.0 * v
        source = mixed + second_x + inner
        sigma = volatility[k]
        a = v + (time_step * 0.5) * sigma * sigma * source - damping * second_x
        a_out[:, k] = a.reshape(a_out.shape[0], a_out.shape[2], a_out.shape[3])
        source_out[k] = time_step * sigma * source

    sweep(
        PLANES,
        lambda k: pick_plane(k, PLANES, block, state, before, after, low, high, blocks),
        lambda k: (y_low[pl.ds(block * PLANES + k + 1, 1), :], y_high[pl.ds(block * PLANES + k + 1, 1), :]),
        emit,
        True,
    )


def forward(index, state, volatility, low, high, y_low, y_high, wide):
    bx, by, bz = state.shape
    blocks = bx // PLANES
    return pl.pallas_call(
        functools.partial(forward_kernel, blocks=blocks),
        grid_spec=pltpu.PrefetchScalarGridSpec(
            num_scalar_prefetch=1,
            grid=(blocks,),
            in_specs=plane_specs(natural, bx - 1, state.shape)
            + [whole(low.shape), whole(high.shape), whole(y_low.shape), whole(y_high.shape)]
            + [pl.BlockSpec((PLANES, by, bz), lambda s, i: (s, 0, 0))],
            out_specs=[
                pl.BlockSpec((wide, PLANES, by // wide, bz), lambda s, i: (0, s, 0, 0)),
                pl.BlockSpec((PLANES, by, bz), lambda s, i: (s, 0, 0)),
            ],
        ),
        out_shape=[
            jax.ShapeDtypeStruct((wide, bx, by // wide, bz), F32),
            jax.ShapeDtypeStruct(state.shape, F32),
        ],
        compiler_params=params(32),
        cost_estimate=cost(5e9, 17),
        name="forward",
    )(index, state, state, state, low, high, y_low, y_high, volatility)


def first_kernel(*refs, count, lines, parts, length, halo):
    pieces, matrix3, out = refs[:count], refs[count], refs[count + 1]
    pieces = [piece.reshape(piece.shape[0] * lines, piece.shape[2]) for piece in pieces]
    out = out.reshape(out.shape[0] * lines, out.shape[2])
    rows = length + 2 * halo

    def pair(step, carry):
        y = step * 2
        field = jnp.concatenate(
            [
                jnp.concatenate(
                    [piece[pl.ds(y + t, piece.shape[0] // lines, stride=lines), :] for piece in pieces], axis=0
                )
                for t in range(2)
            ],
            axis=1,
        )
        solved = left_product(matrix3[...], field)
        width = solved.shape[1] // 2
        for t in range(2):
            half = solved[:, t * width : (t + 1) * width]
            for part in range(parts):
                base = part * rows
                out[pl.ds((base + halo) * lines + y + t, length, stride=lines), :] = half[part * length : (part + 1) * length]
                if halo:
                    zero = jnp.zeros((1, width), F32)
                    before = half[part * length - 1 : part * length] if part > 0 else zero
                    after = half[(part + 1) * length : (part + 1) * length + 1] if part < parts - 1 else zero
                    out[pl.ds(base * lines + y + t, 1), :] = before
                    out[pl.ds((base + rows - 1) * lines + y + t, 1), :] = after
        return carry

    lax.fori_loop(0, lines // 2, pair, 0)


def first(pieces, matrix3, halo):
    wide = pieces[0].shape[0]
    lines, bz = pieces[0].shape[2:]
    length = sum(piece.shape[1] for piece in pieces)
    rows = length + 2 * halo
    flat = [piece.reshape(-1, lines, bz) for piece in pieces]
    block = 8
    out = pl.pallas_call(
        functools.partial(first_kernel, count=len(flat), lines=block, parts=wide, length=length, halo=halo),
        grid=(lines // block,),
        in_specs=[pl.BlockSpec((piece.shape[0], block, bz), lambda s: (0, s, 0)) for piece in flat]
        + [pl.BlockSpec(matrix3.shape, lambda s: (0, 0))],
        out_specs=pl.BlockSpec((wide * rows, block, bz), lambda s: (0, s, 0)),
        out_shape=jax.ShapeDtypeStruct((wide * rows, lines, bz), F32),
        compiler_params=params(40),
        cost_estimate=cost(7e9, 10),
        name="first",
    )(*flat, matrix3)
    return out.reshape(wide, rows, lines, bz)


def second_kernel(*refs, count, chunked):
    pieces, second3, third3, outs = refs[:count], refs[count], refs[count + 1], refs[count + 2 :]
    per, by, bz = pieces[0].shape
    length = count * by
    field = jnp.concatenate([piece[x] for x in range(per) for piece in pieces], axis=0)
    field = right_product(field, third3[...])
    field = jnp.concatenate([field[x * length : (x + 1) * length] for x in range(per)], axis=1)
    solved = left_product(second3[...], field)
    for x in range(per):
        half = solved[:, x * bz : (x + 1) * bz]
        if chunked:
            for d in range(count):
                out = outs[d]
                out[:, x] = half[d * by : (d + 1) * by].reshape(out.shape[0], out.shape[2], bz)
        else:
            outs[0][x] = half


def second(pieces, second3, third3, wide):
    count = len(pieces)
    xs, by, bz = pieces[0].shape
    per = 2
    if wide:
        out_specs = [pl.BlockSpec((wide, per, by // wide, bz), lambda s: (0, s, 0, 0))] * count
        out_shape = [jax.ShapeDtypeStruct((wide, xs, by // wide, bz), F32)] * count
    else:
        out_specs = [pl.BlockSpec((per, count * by, bz), lambda s: (s, 0, 0))]
        out_shape = [jax.ShapeDtypeStruct((xs, count * by, bz), F32)]
    return pl.pallas_call(
        functools.partial(second_kernel, count=count, chunked=bool(wide)),
        grid=(xs // per,),
        in_specs=[pl.BlockSpec((per, by, bz), lambda s: (s, 0, 0))] * count
        + [pl.BlockSpec(second3.shape, lambda s: (0, 0)), pl.BlockSpec(third3.shape, lambda s: (0, 0))],
        out_specs=out_specs,
        out_shape=out_shape,
        compiler_params=params(40),
        cost_estimate=cost(9e9, 10),
        name="second",
    )(*pieces, second3, third3)


def piece_specs(size, tail, per, n):
    return [pl.BlockSpec((size,) + tail, lambda s, i, d=d: (jnp.clip(s - d * per, 0, per - 1), 0, 0)) for d in range(n)]


def chunk_piece_specs(wide, lines, bz, per, order):
    return [
        pl.BlockSpec((wide, PLANES, lines, bz), lambda s, i, d=d: (0, jnp.clip(s - d * per, 0, per - 1), 0, 0))
        for d in order
    ]


def store_piece(outs, turn, kept):
    for d, out in enumerate(outs):

        @pl.when(turn == d)
        def _(out=out):
            out[...] = kept[...]


def select(values, turn):
    result = values[0]
    for d in range(1, len(values)):
        result = jnp.where(turn == d, values[d], result)
    return result


def lifted_kernel(i, solved, state, low, high, y_low, y_high, *refs, per, n, size, xs):
    outs, kept = refs[:n], refs[n]
    step = pl.program_id(0)
    bx = state.shape[0]
    base = lax.rem(i[0] + step // per, n) * xs + lax.rem(step, per) * size
    for k in range(size):
        row = base + k
        v = state[jnp.clip(row - 1, 0, bx - 1)]
        v = jnp.where(row == 0, low[0], jnp.where(row == bx + 1, high[0], v))
        up, down = y_pair(v, y_low[pl.ds(row, 1), :], y_high[pl.ds(row, 1), :])
        kept[k] = chunk_plane(solved, row) - damping * (up + down - 2.0 * v)
    store_piece(outs, step // per, kept)


def lifted(index, solved, state, low, high, y_low, y_high, n):
    bx, by, bz = state.shape
    xs = bx // n
    size = next(k for k in range(9, 0, -1) if (xs + 2) % k == 0)
    per = (xs + 2) // size
    return pl.pallas_call(
        functools.partial(lifted_kernel, per=per, n=n, size=size, xs=xs),
        grid_spec=pltpu.PrefetchScalarGridSpec(
            num_scalar_prefetch=1,
            grid=(n * per,),
            in_specs=[whole(v.shape) for v in (solved, state, low, high, y_low, y_high)],
            out_specs=piece_specs(size, (by, bz), per, n),
            scratch_shapes=[pltpu.VMEM((size, by, bz), F32)],
        ),
        out_shape=[jax.ShapeDtypeStruct((xs + 2, by, bz), F32)] * n,
        compiler_params=params(32),
        cost_estimate=cost(2e9, 13),
        name="lifted",
    )(index, solved, state, low, high, y_low, y_high)


def reaction_kernel(
    i, carried, carried_low, carried_high, vol, before, after, low, high, vol_low, vol_high, cotangent, *refs, per, n, blocks
):
    outs, kept = refs[:n], refs[n]
    step = pl.program_id(0)
    block = rotated(per, n)(step, i)

    def plane(k):
        sigma = pick_plane(k, PLANES, block, vol, before, after, low, high, blocks)
        return (0.5 * correction) * sigma * sigma * chunk_plane(carried, block * PLANES + k + 1)

    def rows(k):
        at = pl.ds(block * PLANES + k + 1, 1)
        s_low, s_high = vol_low[at, :], vol_high[at, :]
        return (
            (0.5 * correction) * s_low * s_low * carried_low[at, :],
            (0.5 * correction) * s_high * s_high * carried_high[at, :],
        )

    def emit(k, v, prev, nxt, mixed, inner):
        kept[k] = cotangent[k] + mixed

    sweep(PLANES, plane, rows, emit, False)
    store_piece(outs, step // per, kept)


def react(index, carried, carried_low, carried_high, vol, low, high, vol_low, vol_high, cotangent, n):
    bx, by, bz = vol.shape
    xs = bx // n
    per = xs // PLANES
    block = rotated(per, n)
    return pl.pallas_call(
        functools.partial(reaction_kernel, per=per, n=n, blocks=bx // PLANES),
        grid_spec=pltpu.PrefetchScalarGridSpec(
            num_scalar_prefetch=1,
            grid=(n * per,),
            in_specs=[whole(carried.shape), whole(carried_low.shape), whole(carried_high.shape)]
            + plane_specs(block, bx - 1, vol.shape)
            + [whole(low.shape), whole(high.shape), whole(vol_low.shape), whole(vol_high.shape)]
            + [pl.BlockSpec((PLANES, by, bz), lambda s, i: (block(s, i), 0, 0))],
            out_specs=piece_specs(PLANES, (by, bz), per, n),
            scratch_shapes=[pltpu.VMEM((PLANES, by, bz), F32)],
        ),
        out_shape=[jax.ShapeDtypeStruct((xs, by, bz), F32)] * n,
        compiler_params=params(40),
        cost_estimate=cost(4e9, 17),
        name="reaction",
    )(index, carried, carried_low, carried_high, vol, vol, vol, low, high, vol_low, vol_high, cotangent)


def lines_kernel(i, *refs, per, n):
    totals, uppers = refs[:n], refs[n : 2 * n]
    cotangent, upper_low, upper_high, third3, out = refs[2 * n :]
    step = pl.program_id(0)
    turn = step // per
    block = rotated(per, n)(step, i)
    for k in range(PLANES):
        total = select([ref[k] for ref in totals], turn)
        upper = select([chunk_plane(ref, k) for ref in uppers], turn)
        at = pl.ds(block * PLANES + k, 1)
        up, down = y_pair(upper, upper_low[at, :], upper_high[at, :])
        third = right_product(total, third3[...])
        z_up, z_down = z_pair(third)
        lines = (up + down - 2.0 * upper) + (z_up + z_down - 2.0 * third)
        out[k] = cotangent[k] - total - damping * lines


def gather_lines(index, totals, uppers, cotangent, upper_low, upper_high, third3):
    n = len(totals)
    bx, by, bz = cotangent.shape
    xs = bx // n
    per = xs // PLANES
    wide, lines = uppers[0].shape[0], uppers[0].shape[2]
    block = rotated(per, n)
    order = [(n - e) % n for e in range(n)]
    return pl.pallas_call(
        functools.partial(lines_kernel, per=per, n=n),
        grid_spec=pltpu.PrefetchScalarGridSpec(
            num_scalar_prefetch=1,
            grid=(n * per,),
            in_specs=piece_specs(PLANES, (by, bz), per, n)
            + chunk_piece_specs(wide, lines, bz, per, range(n))
            + [pl.BlockSpec((PLANES, by, bz), lambda s, i: (block(s, i), 0, 0))]
            + [whole(upper_low.shape), whole(upper_high.shape), whole(third3.shape)],
            out_specs=pl.BlockSpec((PLANES, by, bz), lambda s, i: (block(s, i), 0, 0)),
        ),
        out_shape=jax.ShapeDtypeStruct(cotangent.shape, F32),
        compiler_params=params(40),
        cost_estimate=cost(5e9, 17),
        name="lines",
    )(index, *totals, *[uppers[order[d]] for d in range(n)], cotangent, upper_low, upper_high, third3)


def mixed_kernel(i, field, *refs, n):
    outs, scratch = refs[:n], refs[n]
    by = outs[0].shape[1]

    def emit(k, v, prev, nxt, mixed, inner):
        scratch[...] = mixed
        for d, out in enumerate(outs):
            start = pl.multiple_of(lax.rem(i[0] + d, n) * by, by)
            out[k] = scratch[pl.ds(start, by), :]

    zero = jnp.zeros((1, field.shape[2]), F32)
    sweep(field.shape[0] - 2, lambda k: field[k + 1], lambda k: (zero, zero), emit, False)


def mix(index, field, n):
    rows, ny, bz = field.shape
    xs, by = rows - 2, ny // n
    return pl.pallas_call(
        functools.partial(mixed_kernel, n=n),
        grid_spec=pltpu.PrefetchScalarGridSpec(
            num_scalar_prefetch=1,
            grid=(1,),
            in_specs=[whole(field.shape)],
            out_specs=[whole((xs, by, bz))] * n,
            scratch_shapes=[pltpu.VMEM((ny, bz), F32)],
        ),
        out_shape=[jax.ShapeDtypeStruct((xs, by, bz), F32)] * n,
        compiler_params=params(40),
        cost_estimate=cost(4e9, 9),
        name="mixed",
    )(index, field)


def patch_sums(out, step, planes, patch, patch_t, groups):
    @pl.when(step == 0)
    def _():
        out[...] = jnp.zeros_like(out)

    count, (by, bz) = len(planes), planes[0].shape
    value_high, value_low = split(jnp.concatenate(planes, axis=0))
    ones = jnp.ones((2 * bz, 128), BF16)
    column = jnp.dot(jnp.concatenate([value_high, value_low], axis=1), ones, preferred_element_type=F32)
    number = jnp.concatenate([patch[pl.ds(k, 1), :] for k in range(count)], axis=1)
    coarse = lax.broadcasted_iota(jnp.int32, (groups, count * by), 0) == lax.shift_right_logical(number, 7)
    number_t = patch_t[...].reshape(count * by, 1)
    lane = lax.broadcasted_iota(jnp.int32, (count * by, 128), 1)
    high, low = split(jnp.where(lane == lax.bitwise_and(number_t, 127), column, 0.0))
    out[...] += jnp.dot(
        jnp.where(coarse, 1.0, 0.0).astype(BF16), jnp.concatenate([high, low], axis=1), preferred_element_type=F32
    )


def frozen_kernel(
    i, state, before, after, low, high, q_low, q_high, third3, vol, carried, patch, patch_t, weight, out, *, blocks, groups
):
    block = pl.program_id(0)
    planes = []

    def plane(k):
        v = pick_plane(k, PLANES, block, state, before, after, low, high, blocks)
        up, down = z_pair(v)
        return v + damping * right_product(up + down - 2.0 * v, third3[...])

    def emit(k, v, prev, nxt, mixed, inner):
        w = correction * vol[k] * chunk_plane(carried, block * PLANES + k + 1)
        weight[k] = w
        planes.append(-w * mixed)

    sweep(
        PLANES,
        plane,
        lambda k: (q_low[pl.ds(block * PLANES + k + 1, 1), :], q_high[pl.ds(block * PLANES + k + 1, 1), :]),
        emit,
        False,
    )
    patch_sums(out, block, planes, patch, patch_t, groups)


def frozen(index, state, low, high, q_low, q_high, third3, vol, carried, patch, patch_t, groups):
    bx, by, bz = state.shape
    blocks = bx // PLANES
    main = pl.BlockSpec((PLANES, by, bz), lambda s, i: (s, 0, 0))
    return pl.pallas_call(
        functools.partial(frozen_kernel, blocks=blocks, groups=groups),
        grid_spec=pltpu.PrefetchScalarGridSpec(
            num_scalar_prefetch=1,
            grid=(blocks,),
            in_specs=plane_specs(natural, bx - 1, state.shape)
            + [whole(low.shape), whole(high.shape), whole(q_low.shape), whole(q_high.shape), whole(third3.shape)]
            + [main, whole(carried.shape)]
            + [pl.BlockSpec((PLANES, by), lambda s, i: (s, 0))]
            + [pl.BlockSpec((PLANES, by, 1), lambda s, i: (s, 0, 0))],
            out_specs=[main, whole((groups, 256))],
        ),
        out_shape=[jax.ShapeDtypeStruct(state.shape, F32), jax.ShapeDtypeStruct((groups, 256), F32)],
        compiler_params=params(32),
        cost_estimate=cost(5e9, 17),
        name="frozen",
    )(index, state, state, state, low, high, q_low, q_high, third3, vol, carried, patch, patch_t)


def column_kernel(i, *refs, per, n, groups):
    drifts = refs[:n]
    weight, source, start, patch, patch_t, given, out = refs[n:]
    step = pl.program_id(0)
    turn = step // per
    block = rotated(per, n)(step, i)
    planes = [
        weight[k] * select([ref[k] for ref in drifts], turn)
        + source[k] * chunk_plane(start, block * PLANES + k + 1)
        for k in range(PLANES)
    ]
    patch_sums(out, step, planes, patch, patch_t, groups)

    @pl.when(step == pl.num_programs(0) - 1)
    def _():
        out[...] += given[...]


def column_sums(index, drifts, weight, source, start, patch, patch_t, given):
    n = len(drifts)
    bx, by, bz = source.shape
    xs = bx // n
    per = xs // PLANES
    groups = given.shape[0]
    block = rotated(per, n)
    order = [(n - e) % n for e in range(n)]
    main = pl.BlockSpec((PLANES, by, bz), lambda s, i: (block(s, i), 0, 0))
    return pl.pallas_call(
        functools.partial(column_kernel, per=per, n=n, groups=groups),
        grid_spec=pltpu.PrefetchScalarGridSpec(
            num_scalar_prefetch=1,
            grid=(n * per,),
            in_specs=piece_specs(PLANES, (by, bz), per, n)
            + [main, main, whole(start.shape)]
            + [pl.BlockSpec((PLANES, by), lambda s, i: (block(s, i), 0))]
            + [pl.BlockSpec((PLANES, by, 1), lambda s, i: (block(s, i), 0, 0)), whole(given.shape)],
            out_specs=whole(given.shape),
        ),
        out_shape=jax.ShapeDtypeStruct(given.shape, F32),
        compiler_params=params(40),
        cost_estimate=cost(4e9, 17),
        name="column",
    )(index, *[drifts[order[d]] for d in range(n)], weight, source, start, patch, patch_t, given)


def adjoint_kernel(
    i, start, start_low, start_high, vol, before, after, low, high, vol_low, vol_high, tail, out, *, blocks
):
    block = pl.program_id(0)
    raw = {}

    def plane(k):
        sigma = pick_plane(k, PLANES, block, vol, before, after, low, high, blocks)
        raw[k] = chunk_plane(start, block * PLANES + k + 1)
        return (0.5 * time_step) * sigma * sigma * raw[k]

    def rows(k):
        at = pl.ds(block * PLANES + k + 1, 1)
        s_low, s_high = vol_low[at, :], vol_high[at, :]
        return (
            (0.5 * time_step) * s_low * s_low * start_low[at, :],
            (0.5 * time_step) * s_high * s_high * start_high[at, :],
        )

    def emit(k, v, prev, nxt, mixed, inner):
        spread = mixed + (prev + nxt - 2.0 * v) + inner
        lines = raw[k - 1] + raw[k + 1] - 2.0 * raw[k]
        out[k] = raw[k] + spread + tail[k] - damping * lines

    sweep(PLANES, plane, rows, emit, True)


def finish(index, start, start_low, start_high, vol, low, high, vol_low, vol_high, tail):
    bx, by, bz = vol.shape
    return pl.pallas_call(
        functools.partial(adjoint_kernel, blocks=bx // PLANES),
        grid_spec=pltpu.PrefetchScalarGridSpec(
            num_scalar_prefetch=1,
            grid=(bx // PLANES,),
            in_specs=[whole(start.shape), whole(start_low.shape), whole(start_high.shape)]
            + plane_specs(natural, bx - 1, vol.shape)
            + [whole(low.shape), whole(high.shape), whole(vol_low.shape), whole(vol_high.shape)]
            + [pl.BlockSpec((PLANES, by, bz), lambda s, i: (s, 0, 0))],
            out_specs=pl.BlockSpec((PLANES, by, bz), lambda s, i: (s, 0, 0)),
        ),
        out_shape=jax.ShapeDtypeStruct(vol.shape, F32),
        compiler_params=params(40),
        cost_estimate=cost(5e9, 17),
        name="adjoint",
    )(index, start, start_low, start_high, vol, vol, vol, low, high, vol_low, vol_high, tail)


def neighbours(low_edge, high_edge, axis):
    count = lax.axis_size(axis)
    up = [(k, k + 1) for k in range(count - 1)]
    down = [(k + 1, k) for k in range(count - 1)]
    return lax.ppermute(high_edge, axis, up), lax.ppermute(low_edge, axis, down)


def far_and_near(n):
    return [n // 2] if n > 1 else [], [d for d in range(1, n) if d != n // 2]


def send(pieces, chosen, *earlier):
    n = len(pieces)
    result = list(pieces)
    for d in chosen:
        piece = after(pieces[d], *earlier) if earlier else pieces[d]
        result[d] = lax.ppermute(piece, "narrow", [(k, (k + d) % n) for k in range(n)])
    return result


def pick(pieces, chosen):
    return [pieces[d] for d in chosen]


def after(value, *earlier):
    return lax.optimization_barrier((value, earlier))[0]


def across(piece):
    return lax.all_to_all(piece, "wide", split_axis=0, concat_axis=0, tiled=True)


def row_major(value):
    return with_layout_constraint(value, Layout(major_to_minor=tuple(range(value.ndim))))


def cross_both(pieces, before, between, near, far):
    pieces = [row_major(piece) for piece in pieces]
    lines = send(pieces, near)
    lines = send(lines, far, *pick(lines, near))
    lines = [row_major(line) for line in lines]
    block = jnp.concatenate(pick(lines, [0] + near), axis=1)
    chunks = [across(after(block, *before) if before else block)]
    for d in far:
        chunks.append(across(after(lines[d], chunks[-1], *between)))
    return lines, chunks, pick(lines, far)


def y_edges(chunks):
    return neighbours(chunks[0, :, 0, :], chunks[-1, :, -1, :], "narrow")


def on_device_kernels(state, volatility, cotangent, solve_first, solve_second, solve_third, patch_index):
    n, wide = lax.axis_size("narrow"), lax.axis_size("wide")
    here = lax.axis_index("narrow")
    index = here.astype(jnp.int32).reshape(1)
    bx, by, bz = state.shape
    xs = bx // n
    groups = PATCHES // 128

    ahead = (here + jnp.arange(n)) % n
    back = (here - jnp.arange(n)) % n

    far, near = far_and_near(n)
    every = range(n)

    cot_pieces = [lax.dynamic_slice_in_dim(cotangent, ahead[d] * xs, xs, 0) for d in range(n)]
    early, late = near[:1], near[1:]
    both_low, both_high = neighbours(
        jnp.stack([state[0], volatility[0]]), jnp.stack([state[-1], volatility[-1]]), "wide"
    )
    both = jnp.stack([state[:, :: by - 1], volatility[:, :: by - 1]])
    both = jnp.concatenate([both_low[:, None, :: by - 1], both, both_high[:, None, :: by - 1]], axis=1)
    y_low, y_high = neighbours(both[:, :, 0], both[:, :, 1], "narrow")
    state_x = (both_low[0:1], both_high[0:1])
    vol_x = (both_low[1:2], both_high[1:2])
    state_y = (y_low[0], y_high[0])
    vol_y = (y_low[1], y_high[1])
    cot_lines = send(cot_pieces, near, y_low, y_high)

    second_t = solve_second.T.reshape(n, by, n, by)
    second_t3 = left_form(second_t[ahead][:, :, back].reshape(n * by, n * by))
    second_n = solve_second.reshape(n * by, n, by)
    second_n3 = left_form(second_n[:, back].reshape(n * by, n * by))
    third_t3 = right_form(solve_third)
    third_n3 = right_form(solve_third.T)
    first_n3 = left_form(solve_first)
    first_t = solve_first.T.reshape(wide * bx, wide, n, xs)
    first_t = first_t[:, :, back]
    groups_of = [[0] + near] + [[d] for d in far]
    first_t3 = left_form(
        jnp.concatenate([first_t[:, :, jnp.array(g)].reshape(wide * bx, -1) for g in groups_of], axis=1)
    )

    a, source = forward(index, state, volatility, *state_x, *state_y, wide)
    a = after(a, *pick(cot_lines, early))
    cot_lines = send(cot_lines, far, *pick(cot_lines, near))
    forward_lines = after(first([across(a)], first_n3, 1), *pick(cot_lines, far), second_t3, third_t3)
    back = second(after(cot_lines, forward_lines), second_t3, third_t3, wide)
    solved = across(forward_lines)

    lifted_pieces = lifted(index, solved, state, *state_x, *state_y, n)
    back, carried_chunks, gone = cross_both(back, (solved,), lifted_pieces, near, far)
    carried_lines = first(carried_chunks, first_t3, 1)
    level_lines = send(lifted_pieces, late, gone)
    carried = across(after(carried_lines, *pick(level_lines, late)))

    level_lines = send(level_lines, far, *pick(level_lines, late))
    carried = after(carried, *pick(level_lines, far))
    carried_y = y_edges(carried)
    level_lines = send(level_lines, early, *carried_y)
    totals = react(index, carried, *carried_y, volatility, *vol_x, *vol_y, cotangent, n)
    total_lines = send(totals, near)
    total_lines = send(total_lines, far, *pick(total_lines, near))

    uppers = second(after(total_lines, *pick(level_lines, early)), second_t3, third_t3, wide)
    level = second(after(level_lines, uppers), second_n3, third_n3, 0)[0]
    drift_pieces = mix(index, level, n)

    def frozen_rows(rows):
        padded = jnp.pad(rows, ((0, 0), (1, 1)))
        curved = padded[:, 2:] + padded[:, :-2] - 2.0 * rows
        return rows + damping * jnp.dot(curved, solve_third.T, precision=lax.Precision.HIGHEST)

    patch_t = patch_index[:, :, None]
    weight, sums = frozen(
        index,
        after(state, *drift_pieces),
        *state_x,
        frozen_rows(state_y[0]),
        frozen_rows(state_y[1]),
        third_n3,
        volatility,
        carried,
        patch_index,
        patch_t,
        groups,
    )

    uppers, start_chunks, gone = cross_both(uppers, drift_pieces, (sums,), near, far)
    drifts = send(drift_pieces, early, *pick(uppers, near))
    start_lines = first(start_chunks, first_t3, 1)
    drifts = send(drifts, late, gone)
    start = across(after(start_lines, *pick(drifts, near)))

    order = (here - jnp.arange(n)) % n
    edge_low = jnp.stack([piece[0, :, 0] for piece in uppers])[order].reshape(bx, bz)
    edge_high = jnp.stack([piece[-1, :, -1] for piece in uppers])[order].reshape(bx, bz)
    upper_y = neighbours(edge_low, edge_high, "narrow")
    drifts = send(drifts, far, *pick(drifts, late), *upper_y)
    tail = gather_lines(index, totals, uppers, cotangent, *upper_y, third_t3)

    start = after(start, tail)
    start_y = y_edges(start)
    start = after(start, *start_y)
    sums = column_sums(index, drifts, weight, source, start, patch_index, patch_t, sums)
    count, joint = n * wide, ("wide", "narrow")
    sums = (sums[:, :128] + sums[:, 128:]).reshape(count, PATCHES // count)
    shares = lax.all_to_all(sums, joint, split_axis=0, concat_axis=0, tiled=True)
    vega = jnp.sum(shares, axis=0)

    adjoint = finish(index, start, *start_y, volatility, *vol_x, *vol_y, tail)
    return (adjoint, vega * vega_scale)


def on_device(*args):
    n, wide = lax.axis_size("narrow"), lax.axis_size("wide")
    bx, by, bz = args[0].shape
    aligned = bx % (n * PLANES) == 0 and by % 128 == 0 and by % (wide * 8) == 0 and bz == 128
    aligned = aligned and PATCHES % (n * wide) == 0 and by // wide % 2 == 0
    return on_device_kernels(*args) if aligned else on_device_plain(*args)


def solution(mesh):
    placed = (
        P("wide", "narrow", None),
        P("wide", "narrow", None),
        P("wide", "narrow", None),
        P(),
        P(),
        P(),
        P("wide", "narrow"),
    )
    return jax.shard_map(
        on_device,
        mesh=mesh,
        in_specs=placed,
        out_specs=(P("wide", "narrow", None), P(("wide", "narrow"))),
        check_vma=False,
    )
```

```python
import functools
import jax
import jax.numpy as jnp
from jax import lax
from jax.experimental import pallas as pl
from jax.experimental.layout import Layout, with_layout_constraint
from jax.experimental.pallas import tpu as pltpu
from jax.sharding import PartitionSpec as P

PATCHES = 3072


time_step = 0.4
theta_weight = 0.5
frozen_coef = 0.2
correction = 0.5 * 0.4
vega_scale = 1.0 / 32.0
correlations = ((0, 1, 0.5), (0, 2, 0.3), (1, 2, -0.4))


def padded_2(cells, sides, width):
    for axis, dim in sides:
        count = lax.axis_size(axis)
        ends = count - 1
        head = lax.slice_in_dim(cells, 0, width, axis=dim)
        tail = lax.slice_in_dim(cells, cells.shape[dim] - width, cells.shape[dim], axis=dim)
        cells = jnp.concatenate(
            [
                lax.ppermute(tail, axis, [(i, (i + 1) % count) for i in range(ends)]),
                cells,
                lax.ppermute(head, axis, [((i + 1) % count, i) for i in range(ends)]),
            ],
            axis=dim,
        )
    return cells


def along_third(values, offset):
    if offset == 0:
        return values
    zero_layer = jnp.zeros_like(values[..., :1])
    if offset > 0:
        return jnp.concatenate([values[..., 1:], zero_layer], axis=-1)
    return jnp.concatenate([zero_layer, values[..., :-1]], axis=-1)


def shifted(padded, offsets):
    lead = padded.ndim - 3
    slices = [slice(None)] * lead
    for position in range(2):
        offset = offsets[position]
        length = padded.shape[lead + position]
        slices.append(slice(1 + offset, length - 1 + offset))
    slices.append(slice(None))
    return along_third(padded[tuple(slices)], offsets[2])


def second_parts(padded):
    centre = shifted(padded, [0, 0, 0])
    result = []
    for axis_number in range(3):
        upward = [0, 0, 0]
        upward[axis_number] = 1
        downward = [0, 0, 0]
        downward[axis_number] = -1
        result.append(shifted(padded, upward) + shifted(padded, downward) - 2.0 * centre)
    return tuple(result)


def cross_term(padded, first_axis, second_axis):

    def corner(sign_first, sign_second):
        offsets = [0, 0, 0]
        offsets[first_axis] = sign_first
        offsets[second_axis] = sign_second
        return shifted(padded, offsets)

    return 0.25 * (corner(1, 1) - corner(1, -1) - corner(-1, 1) + corner(-1, -1))


def mixed_of(padded):
    total = None
    for first_axis, second_axis, weight in correlations:
        term = weight * cross_term(padded, first_axis, second_axis)
        total = term if total is None else total + term
    return total


def contract(matrix, field, axis_number, transposed):
    letters = "xyz"
    source = letters[axis_number]
    matrix_form = source + "w" if transposed else "w" + source
    result_form = letters.replace(source, "w")
    return jnp.einsum(
        matrix_form + "," + letters + "->" + result_form,
        matrix,
        field,
        precision=lax.Precision.HIGHEST,
    )


def line_x(field, matrix, transposed):

    def solve_lines(pieces):
        solved = contract(matrix, pieces, 0, transposed)
        return lax.all_to_all(solved, "wide", split_axis=0, concat_axis=1, tiled=True)

    return solve_lines(lax.all_to_all(field, "wide", split_axis=1, concat_axis=0, tiled=True))


def line_y(field, matrix, transposed):

    def solve_lines(pieces):
        solved = contract(matrix, pieces, 1, transposed)
        return lax.all_to_all(solved, "narrow", split_axis=1, concat_axis=2, tiled=True)

    return solve_lines(lax.all_to_all(field, "narrow", split_axis=2, concat_axis=1, tiled=True))


def rimmed(stacked):
    return padded_2(stacked, (("wide", 1), ("narrow", 2)), 1)


def third_second(field):
    return along_third(field, 1) + along_third(field, -1) - 2.0 * field


def on_device_plain(state, volatility, cotangent, solve_first, solve_second, solve_third, patch_index):
    coefficient = 0.5 * volatility * volatility
    padded = rimmed(state[None])
    parts = second_parts(padded)
    second_x, second_y, second_z = (parts[0][0], parts[1][0], parts[2][0])
    source = mixed_of(padded)[0] + second_x + second_y + second_z
    start = state + time_step * coefficient * source
    damping = theta_weight * time_step * frozen_coef
    level = line_x(start - damping * second_x, solve_first, False)
    level = line_y(level - damping * second_y, solve_second, False)
    level = contract(solve_third, level - damping * second_z, 2, False)
    drift = mixed_of(rimmed((level - state)[None]))[0]
    back_third = contract(solve_third, cotangent, 2, True)
    back_second = line_y(back_third, solve_second, True)
    carried = line_x(back_second, solve_first, True)
    reaction = mixed_of(rimmed((correction * coefficient * carried)[None]))[0]
    total = cotangent + reaction
    upper_third = contract(solve_third, total, 2, True)
    upper_second = line_y(upper_third, solve_second, True)
    adjoint_start = line_x(upper_second, solve_first, True)
    scaled = time_step * coefficient * adjoint_start
    padded = rimmed(jnp.stack([scaled, adjoint_start, upper_second]))
    parts = second_parts(padded)
    spread = mixed_of(padded[0:1])[0] + parts[0][0] + parts[1][0] + parts[2][0]
    lines = parts[0][1] + parts[1][2] + third_second(upper_third)
    adjoint = adjoint_start + spread - reaction - damping * lines
    sensitivity = volatility * (correction * carried * drift + time_step * adjoint_start * source)
    column = jnp.sum(sensitivity, axis=2)
    partial_sums = jax.ops.segment_sum(
        column.reshape(-1), patch_index.reshape(-1), num_segments=PATCHES
    )
    vega = lax.psum_scatter(partial_sums, ("wide", "narrow"), scatter_dimension=0, tiled=True)
    return (adjoint, vega * vega_scale)


F32 = jnp.float32
BF16 = jnp.bfloat16
damping = 0.5 * 0.4 * 0.2
MIB = 1024 * 1024
PLANES = 8


def params(mib):
    return pltpu.CompilerParams(vmem_limit_bytes=60 * MIB)


def cost(flops, mib):
    return pl.CostEstimate(flops=int(flops / 50), bytes_accessed=int(mib * MIB / 50), transcendentals=0)


def halves(x):
    high = lax.reduce_precision(x, 8, 7)
    return high.astype(BF16), (x - high).astype(BF16)


def left_form(matrix):
    high, low = halves(matrix)
    return jnp.concatenate([high, high, low], axis=1)


def right_form(matrix):
    high, low = halves(matrix)
    return jnp.concatenate([high, high, low], axis=0)


def split(x):
    high = x.astype(BF16)
    return high, (x - high.astype(F32)).astype(BF16)


def left_product(matrix3, field):
    high, low = split(field)
    return jnp.dot(matrix3, jnp.concatenate([high, low, high], axis=0), preferred_element_type=F32)


def right_product(field, matrix3):
    high, low = split(field)
    return jnp.dot(jnp.concatenate([high, low, high], axis=1), matrix3, preferred_element_type=F32)


def y_pair(v, low_row, high_row):
    n = v.shape[0]
    row = lax.broadcasted_iota(jnp.int32, (8, v.shape[1]), 0)
    up, down = pltpu.roll(v, n - 1, 0), pltpu.roll(v, 1, 0)
    up = jnp.concatenate([up[: n - 8], jnp.where(row == 7, high_row, up[n - 8 :])], axis=0)
    down = jnp.concatenate([jnp.where(row == 0, low_row, down[:8]), down[8:]], axis=0)
    return up, down


def z_pair(v):
    n = v.shape[1]
    lane = lax.broadcasted_iota(jnp.int32, v.shape, 1)
    up = jnp.where(lane == n - 1, 0.0, pltpu.roll(v, n - 1, 1))
    down = jnp.where(lane == 0, 0.0, pltpu.roll(v, 1, 1))
    return up, down


def sweep(count, plane, rows, emit, full):
    v, p, rest, inner = {}, {}, {}, {}
    for k in range(-1, count + 1):
        centre = plane(k)
        y_up, y_down = y_pair(centre, *rows(k))
        z_up, z_down = z_pair(centre)
        e = y_up - y_down
        v[k] = centre
        p[k] = 0.125 * e + 0.075 * (z_up - z_down)
        if 0 <= k < count:
            e_up, e_down = z_pair(e)
            rest[k] = -0.1 * (e_up - e_down)
            if full:
                inner[k] = (y_up + y_down) + (z_up + z_down) - 4.0 * centre
        if k >= 1:
            mixed = (p[k] - p[k - 2]) + rest[k - 1]
            emit(k - 1, v[k - 1], v[k - 2], v[k], mixed, inner.get(k - 1))


def chunk_plane(ref, x):
    value = ref[:, x]
    return value.reshape(value.shape[0] * value.shape[1], value.shape[2])


def plane_specs(step_block, last, shape):
    tail = shape[1:]
    return [
        pl.BlockSpec((PLANES,) + tail, lambda s, i: (step_block(s, i), 0, 0)),
        pl.BlockSpec((1,) + tail, lambda s, i: (jnp.maximum(step_block(s, i) * PLANES - 1, 0), 0, 0)),
        pl.BlockSpec((1,) + tail, lambda s, i: (jnp.minimum(step_block(s, i) * PLANES + PLANES, last), 0, 0)),
    ]


def whole(shape):
    return pl.BlockSpec(shape, lambda s, i: (0,) * len(shape))


def pick_plane(k, count, block, main, before, after, low, high, blocks):
    if k < 0:
        return jnp.where(block == 0, low[0], before[0])
    if k >= count:
        return jnp.where(block == blocks - 1, high[0], after[0])
    return main[k]


def natural(s, i):
    return s


def rotated(per, n):
    def block(s, i):
        return lax.rem(i[0] + s // per, n) * per + lax.rem(s, per)

    return block


def piece_map(d, per):
    return lambda s: jnp.clip(s - d * per, 0, per - 1)


def forward_kernel(i, state, before, after, low, high, y_low, y_high, volatility, a_out, source_out, *, blocks):
    block = pl.program_id(0)

    def emit(k, v, prev, nxt, mixed, inner):
        second_x = prev + nxt - 2.0 * v
        source = mixed + second_x + inner
        sigma = volatility[k]
        a = v + (time_step * 0.5) * sigma * sigma * source - damping * second_x
        a_out[:, k] = a.reshape(a_out.shape[0], a_out.shape[2], a_out.shape[3])
        source_out[k] = time_step * sigma * source

    sweep(
        PLANES,
        lambda k: pick_plane(k, PLANES, block, state, before, after, low, high, blocks),
        lambda k: (y_low[pl.ds(block * PLANES + k + 1, 1), :], y_high[pl.ds(block * PLANES + k + 1, 1), :]),
        emit,
        True,
    )


def forward(index, state, volatility, low, high, y_low, y_high, wide):
    bx, by, bz = state.shape
    blocks = bx // PLANES
    return pl.pallas_call(
        functools.partial(forward_kernel, blocks=blocks),
        grid_spec=pltpu.PrefetchScalarGridSpec(
            num_scalar_prefetch=1,
            grid=(blocks,),
            in_specs=plane_specs(natural, bx - 1, state.shape)
            + [whole(low.shape), whole(high.shape), whole(y_low.shape), whole(y_high.shape)]
            + [pl.BlockSpec((PLANES, by, bz), lambda s, i: (s, 0, 0))],
            out_specs=[
                pl.BlockSpec((wide, PLANES, by // wide, bz), lambda s, i: (0, s, 0, 0)),
                pl.BlockSpec((PLANES, by, bz), lambda s, i: (s, 0, 0)),
            ],
        ),
        out_shape=[
            jax.ShapeDtypeStruct((wide, bx, by // wide, bz), F32),
            jax.ShapeDtypeStruct(state.shape, F32),
        ],
        compiler_params=params(32),
        cost_estimate=cost(5e9, 17),
        name="forward",
    )(index, state, state, state, low, high, y_low, y_high, volatility)


def first_kernel(*refs, count, lines, parts, length, halo):
    pieces, matrix3, out = refs[:count], refs[count], refs[count + 1]
    pieces = [piece.reshape(piece.shape[0] * lines, piece.shape[2]) for piece in pieces]
    out = out.reshape(out.shape[0] * lines, out.shape[2])
    rows = length + 2 * halo

    def pair(step, carry):
        y = step * 2
        field = jnp.concatenate(
            [
                jnp.concatenate(
                    [piece[pl.ds(y + t, piece.shape[0] // lines, stride=lines), :] for piece in pieces], axis=0
                )
                for t in range(2)
            ],
            axis=1,
        )
        solved = left_product(matrix3[...], field)
        width = solved.shape[1] // 2
        for t in range(2):
            half = solved[:, t * width : (t + 1) * width]
            for part in range(parts):
                base = part * rows
                out[pl.ds((base + halo) * lines + y + t, length, stride=lines), :] = half[part * length : (part + 1) * length]
                if halo:
                    zero = jnp.zeros((1, width), F32)
                    before = half[part * length - 1 : part * length] if part > 0 else zero
                    after = half[(part + 1) * length : (part + 1) * length + 1] if part < parts - 1 else zero
                    out[pl.ds(base * lines + y + t, 1), :] = before
                    out[pl.ds((base + rows - 1) * lines + y + t, 1), :] = after
        return carry

    lax.fori_loop(0, lines // 2, pair, 0)


def first(pieces, matrix3, halo):
    wide = pieces[0].shape[0]
    lines, bz = pieces[0].shape[2:]
    length = sum(piece.shape[1] for piece in pieces)
    rows = length + 2 * halo
    flat = [piece.reshape(-1, lines, bz) for piece in pieces]
    block = 8
    out = pl.pallas_call(
        functools.partial(first_kernel, count=len(flat), lines=block, parts=wide, length=length, halo=halo),
        grid=(lines // block,),
        in_specs=[pl.BlockSpec((piece.shape[0], block, bz), lambda s: (0, s, 0)) for piece in flat]
        + [pl.BlockSpec(matrix3.shape, lambda s: (0, 0))],
        out_specs=pl.BlockSpec((wide * rows, block, bz), lambda s: (0, s, 0)),
        out_shape=jax.ShapeDtypeStruct((wide * rows, lines, bz), F32),
        compiler_params=params(40),
        cost_estimate=cost(7e9, 10),
        name="first",
    )(*flat, matrix3)
    return out.reshape(wide, rows, lines, bz)


def second_kernel(*refs, count, chunked):
    pieces, second3, third3, outs = refs[:count], refs[count], refs[count + 1], refs[count + 2 :]
    per, by, bz = pieces[0].shape
    length = count * by
    field = jnp.concatenate([piece[x] for x in range(per) for piece in pieces], axis=0)
    field = right_product(field, third3[...])
    field = jnp.concatenate([field[x * length : (x + 1) * length] for x in range(per)], axis=1)
    solved = left_product(second3[...], field)
    for x in range(per):
        half = solved[:, x * bz : (x + 1) * bz]
        if chunked:
            for d in range(count):
                out = outs[d]
                out[:, x] = half[d * by : (d + 1) * by].reshape(out.shape[0], out.shape[2], bz)
        else:
            outs[0][x] = half


def second(pieces, second3, third3, wide):
    count = len(pieces)
    xs, by, bz = pieces[0].shape
    per = 2
    if wide:
        out_specs = [pl.BlockSpec((wide, per, by // wide, bz), lambda s: (0, s, 0, 0))] * count
        out_shape = [jax.ShapeDtypeStruct((wide, xs, by // wide, bz), F32)] * count
    else:
        out_specs = [pl.BlockSpec((per, count * by, bz), lambda s: (s, 0, 0))]
        out_shape = [jax.ShapeDtypeStruct((xs, count * by, bz), F32)]
    return pl.pallas_call(
        functools.partial(second_kernel, count=count, chunked=bool(wide)),
        grid=(xs // per,),
        in_specs=[pl.BlockSpec((per, by, bz), lambda s: (s, 0, 0))] * count
        + [pl.BlockSpec(second3.shape, lambda s: (0, 0)), pl.BlockSpec(third3.shape, lambda s: (0, 0))],
        out_specs=out_specs,
        out_shape=out_shape,
        compiler_params=params(40),
        cost_estimate=cost(9e9, 10),
        name="second",
    )(*pieces, second3, third3)


def piece_specs(size, tail, per, n):
    return [pl.BlockSpec((size,) + tail, lambda s, i, d=d: (jnp.clip(s - d * per, 0, per - 1), 0, 0)) for d in range(n)]


def chunk_piece_specs(wide, lines, bz, per, order):
    return [
        pl.BlockSpec((wide, PLANES, lines, bz), lambda s, i, d=d: (0, jnp.clip(s - d * per, 0, per - 1), 0, 0))
        for d in order
    ]


def store_piece(outs, turn, kept):
    for d, out in enumerate(outs):

        @pl.when(turn == d)
        def _(out=out):
            out[...] = kept[...]


def select(values, turn):
    result = values[0]
    for d in range(1, len(values)):
        result = jnp.where(turn == d, values[d], result)
    return result


def lifted_kernel(i, solved, state, low, high, y_low, y_high, *refs, per, n, size, xs):
    outs, kept = refs[:n], refs[n]
    step = pl.program_id(0)
    bx = state.shape[0]
    base = lax.rem(i[0] + step // per, n) * xs + lax.rem(step, per) * size
    for k in range(size):
        row = base + k
        v = state[jnp.clip(row - 1, 0, bx - 1)]
        v = jnp.where(row == 0, low[0], jnp.where(row == bx + 1, high[0], v))
        up, down = y_pair(v, y_low[pl.ds(row, 1), :], y_high[pl.ds(row, 1), :])
        kept[k] = chunk_plane(solved, row) - damping * (up + down - 2.0 * v)
    store_piece(outs, step // per, kept)


def lifted(index, solved, state, low, high, y_low, y_high, n):
    bx, by, bz = state.shape
    xs = bx // n
    size = next(k for k in range(9, 0, -1) if (xs + 2) % k == 0)
    per = (xs + 2) // size
    return pl.pallas_call(
        functools.partial(lifted_kernel, per=per, n=n, size=size, xs=xs),
        grid_spec=pltpu.PrefetchScalarGridSpec(
            num_scalar_prefetch=1,
            grid=(n * per,),
            in_specs=[whole(v.shape) for v in (solved, state, low, high, y_low, y_high)],
            out_specs=piece_specs(size, (by, bz), per, n),
            scratch_shapes=[pltpu.VMEM((size, by, bz), F32)],
        ),
        out_shape=[jax.ShapeDtypeStruct((xs + 2, by, bz), F32)] * n,
        compiler_params=params(32),
        cost_estimate=cost(2e9, 13),
        name="lifted",
    )(index, solved, state, low, high, y_low, y_high)


def reaction_kernel(
    i, carried, carried_low, carried_high, vol, before, after, low, high, vol_low, vol_high, cotangent, *refs, per, n, blocks
):
    outs, kept = refs[:n], refs[n]
    step = pl.program_id(0)
    block = rotated(per, n)(step, i)

    def plane(k):
        sigma = pick_plane(k, PLANES, block, vol, before, after, low, high, blocks)
        return (0.5 * correction) * sigma * sigma * chunk_plane(carried, block * PLANES + k + 1)

    def rows(k):
        at = pl.ds(block * PLANES + k + 1, 1)
        s_low, s_high = vol_low[at, :], vol_high[at, :]
        return (
            (0.5 * correction) * s_low * s_low * carried_low[at, :],
            (0.5 * correction) * s_high * s_high * carried_high[at, :],
        )

    def emit(k, v, prev, nxt, mixed, inner):
        kept[k] = cotangent[k] + mixed

    sweep(PLANES, plane, rows, emit, False)
    store_piece(outs, step // per, kept)


def react(index, carried, carried_low, carried_high, vol, low, high, vol_low, vol_high, cotangent, n):
    bx, by, bz = vol.shape
    xs = bx // n
    per = xs // PLANES
    block = rotated(per, n)
    return pl.pallas_call(
        functools.partial(reaction_kernel, per=per, n=n, blocks=bx // PLANES),
        grid_spec=pltpu.PrefetchScalarGridSpec(
            num_scalar_prefetch=1,
            grid=(n * per,),
            in_specs=[whole(carried.shape), whole(carried_low.shape), whole(carried_high.shape)]
            + plane_specs(block, bx - 1, vol.shape)
            + [whole(low.shape), whole(high.shape), whole(vol_low.shape), whole(vol_high.shape)]
            + [pl.BlockSpec((PLANES, by, bz), lambda s, i: (block(s, i), 0, 0))],
            out_specs=piece_specs(PLANES, (by, bz), per, n),
            scratch_shapes=[pltpu.VMEM((PLANES, by, bz), F32)],
        ),
        out_shape=[jax.ShapeDtypeStruct((xs, by, bz), F32)] * n,
        compiler_params=params(40),
        cost_estimate=cost(4e9, 17),
        name="reaction",
    )(index, carried, carried_low, carried_high, vol, vol, vol, low, high, vol_low, vol_high, cotangent)


def lines_kernel(i, *refs, per, n):
    totals, uppers = refs[:n], refs[n : 2 * n]
    cotangent, upper_low, upper_high, third3, out = refs[2 * n :]
    step = pl.program_id(0)
    turn = step // per
    block = rotated(per, n)(step, i)
    for k in range(PLANES):
        total = select([ref[k] for ref in totals], turn)
        upper = select([chunk_plane(ref, k) for ref in uppers], turn)
        at = pl.ds(block * PLANES + k, 1)
        up, down = y_pair(upper, upper_low[at, :], upper_high[at, :])
        third = right_product(total, third3[...])
        z_up, z_down = z_pair(third)
        lines = (up + down - 2.0 * upper) + (z_up + z_down - 2.0 * third)
        out[k] = cotangent[k] - total - damping * lines


def gather_lines(index, totals, uppers, cotangent, upper_low, upper_high, third3):
    n = len(totals)
    bx, by, bz = cotangent.shape
    xs = bx // n
    per = xs // PLANES
    wide, lines = uppers[0].shape[0], uppers[0].shape[2]
    block = rotated(per, n)
    order = [(n - e) % n for e in range(n)]
    return pl.pallas_call(
        functools.partial(lines_kernel, per=per, n=n),
        grid_spec=pltpu.PrefetchScalarGridSpec(
            num_scalar_prefetch=1,
            grid=(n * per,),
            in_specs=piece_specs(PLANES, (by, bz), per, n)
            + chunk_piece_specs(wide, lines, bz, per, range(n))
            + [pl.BlockSpec((PLANES, by, bz), lambda s, i: (block(s, i), 0, 0))]
            + [whole(upper_low.shape), whole(upper_high.shape), whole(third3.shape)],
            out_specs=pl.BlockSpec((PLANES, by, bz), lambda s, i: (block(s, i), 0, 0)),
        ),
        out_shape=jax.ShapeDtypeStruct(cotangent.shape, F32),
        compiler_params=params(40),
        cost_estimate=cost(5e9, 17),
        name="lines",
    )(index, *totals, *[uppers[order[d]] for d in range(n)], cotangent, upper_low, upper_high, third3)


def mixed_kernel(i, field, *refs, n):
    outs, scratch = refs[:n], refs[n]
    by = outs[0].shape[1]

    def emit(k, v, prev, nxt, mixed, inner):
        scratch[...] = mixed
        for d, out in enumerate(outs):
            start = pl.multiple_of(lax.rem(i[0] + d, n) * by, by)
            out[k] = scratch[pl.ds(start, by), :]

    zero = jnp.zeros((1, field.shape[2]), F32)
    sweep(field.shape[0] - 2, lambda k: field[k + 1], lambda k: (zero, zero), emit, False)


def mix(index, field, n):
    rows, ny, bz = field.shape
    xs, by = rows - 2, ny // n
    return pl.pallas_call(
        functools.partial(mixed_kernel, n=n),
        grid_spec=pltpu.PrefetchScalarGridSpec(
            num_scalar_prefetch=1,
            grid=(1,),
            in_specs=[whole(field.shape)],
            out_specs=[whole((xs, by, bz))] * n,
            scratch_shapes=[pltpu.VMEM((ny, bz), F32)],
        ),
        out_shape=[jax.ShapeDtypeStruct((xs, by, bz), F32)] * n,
        compiler_params=params(40),
        cost_estimate=cost(4e9, 9),
        name="mixed",
    )(index, field)


def patch_sums(out, step, planes, patch, patch_t, groups):
    @pl.when(step == 0)
    def _():
        out[...] = jnp.zeros_like(out)

    count, (by, bz) = len(planes), planes[0].shape
    value_high, value_low = split(jnp.concatenate(planes, axis=0))
    ones = jnp.ones((2 * bz, 128), BF16)
    column = jnp.dot(jnp.concatenate([value_high, value_low], axis=1), ones, preferred_element_type=F32)
    number = jnp.concatenate([patch[pl.ds(k, 1), :] for k in range(count)], axis=1)
    coarse = lax.broadcasted_iota(jnp.int32, (groups, count * by), 0) == lax.shift_right_logical(number, 7)
    number_t = patch_t[...].reshape(count * by, 1)
    lane = lax.broadcasted_iota(jnp.int32, (count * by, 128), 1)
    high, low = split(jnp.where(lane == lax.bitwise_and(number_t, 127), column, 0.0))
    out[...] += jnp.dot(
        jnp.where(coarse, 1.0, 0.0).astype(BF16), jnp.concatenate([high, low], axis=1), preferred_element_type=F32
    )


def frozen_kernel(
    i, state, before, after, low, high, q_low, q_high, third3, vol, carried, patch, patch_t, weight, out, *, blocks, groups
):
    block = pl.program_id(0)
    planes = []

    def plane(k):
        v = pick_plane(k, PLANES, block, state, before, after, low, high, blocks)
        up, down = z_pair(v)
        return v + damping * right_product(up + down - 2.0 * v, third3[...])

    def emit(k, v, prev, nxt, mixed, inner):
        w = correction * vol[k] * chunk_plane(carried, block * PLANES + k + 1)
        weight[k] = w
        planes.append(-w * mixed)

    sweep(
        PLANES,
        plane,
        lambda k: (q_low[pl.ds(block * PLANES + k + 1, 1), :], q_high[pl.ds(block * PLANES + k + 1, 1), :]),
        emit,
        False,
    )
    patch_sums(out, block, planes, patch, patch_t, groups)


def frozen(index, state, low, high, q_low, q_high, third3, vol, carried, patch, patch_t, groups):
    bx, by, bz = state.shape
    blocks = bx // PLANES
    main = pl.BlockSpec((PLANES, by, bz), lambda s, i: (s, 0, 0))
    return pl.pallas_call(
        functools.partial(frozen_kernel, blocks=blocks, groups=groups),
        grid_spec=pltpu.PrefetchScalarGridSpec(
            num_scalar_prefetch=1,
            grid=(blocks,),
            in_specs=plane_specs(natural, bx - 1, state.shape)
            + [whole(low.shape), whole(high.shape), whole(q_low.shape), whole(q_high.shape), whole(third3.shape)]
            + [main, whole(carried.shape)]
            + [pl.BlockSpec((PLANES, by), lambda s, i: (s, 0))]
            + [pl.BlockSpec((PLANES, by, 1), lambda s, i: (s, 0, 0))],
            out_specs=[main, whole((groups, 256))],
        ),
        out_shape=[jax.ShapeDtypeStruct(state.shape, F32), jax.ShapeDtypeStruct((groups, 256), F32)],
        compiler_params=params(32),
        cost_estimate=cost(5e9, 17),
        name="frozen",
    )(index, state, state, state, low, high, q_low, q_high, third3, vol, carried, patch, patch_t)


def column_kernel(i, *refs, per, n, groups):
    drifts = refs[:n]
    weight, source, start, patch, patch_t, given, out = refs[n:]
    step = pl.program_id(0)
    turn = step // per
    block = rotated(per, n)(step, i)
    planes = [
        weight[k] * select([ref[k] for ref in drifts], turn)
        + source[k] * chunk_plane(start, block * PLANES + k + 1)
        for k in range(PLANES)
    ]
    patch_sums(out, step, planes, patch, patch_t, groups)

    @pl.when(step == pl.num_programs(0) - 1)
    def _():
        out[...] += given[...]


def column_sums(index, drifts, weight, source, start, patch, patch_t, given):
    n = len(drifts)
    bx, by, bz = source.shape
    xs = bx // n
    per = xs // PLANES
    groups = given.shape[0]
    block = rotated(per, n)
    order = [(n - e) % n for e in range(n)]
    main = pl.BlockSpec((PLANES, by, bz), lambda s, i: (block(s, i), 0, 0))
    return pl.pallas_call(
        functools.partial(column_kernel, per=per, n=n, groups=groups),
        grid_spec=pltpu.PrefetchScalarGridSpec(
            num_scalar_prefetch=1,
            grid=(n * per,),
            in_specs=piece_specs(PLANES, (by, bz), per, n)
            + [main, main, whole(start.shape)]
            + [pl.BlockSpec((PLANES, by), lambda s, i: (block(s, i), 0))]
            + [pl.BlockSpec((PLANES, by, 1), lambda s, i: (block(s, i), 0, 0)), whole(given.shape)],
            out_specs=whole(given.shape),
        ),
        out_shape=jax.ShapeDtypeStruct(given.shape, F32),
        compiler_params=params(40),
        cost_estimate=cost(4e9, 17),
        name="column",
    )(index, *[drifts[order[d]] for d in range(n)], weight, source, start, patch, patch_t, given)


def adjoint_kernel(
    i, start, start_low, start_high, vol, before, after, low, high, vol_low, vol_high, tail, out, *, blocks
):
    block = pl.program_id(0)
    raw = {}

    def plane(k):
        sigma = pick_plane(k, PLANES, block, vol, before, after, low, high, blocks)
        raw[k] = chunk_plane(start, block * PLANES + k + 1)
        return (0.5 * time_step) * sigma * sigma * raw[k]

    def rows(k):
        at = pl.ds(block * PLANES + k + 1, 1)
        s_low, s_high = vol_low[at, :], vol_high[at, :]
        return (
            (0.5 * time_step) * s_low * s_low * start_low[at, :],
            (0.5 * time_step) * s_high * s_high * start_high[at, :],
        )

    def emit(k, v, prev, nxt, mixed, inner):
        spread = mixed + (prev + nxt - 2.0 * v) + inner
        lines = raw[k - 1] + raw[k + 1] - 2.0 * raw[k]
        out[k] = raw[k] + spread + tail[k] - damping * lines

    sweep(PLANES, plane, rows, emit, True)


def finish(index, start, start_low, start_high, vol, low, high, vol_low, vol_high, tail):
    bx, by, bz = vol.shape
    return pl.pallas_call(
        functools.partial(adjoint_kernel, blocks=bx // PLANES),
        grid_spec=pltpu.PrefetchScalarGridSpec(
            num_scalar_prefetch=1,
            grid=(bx // PLANES,),
            in_specs=[whole(start.shape), whole(start_low.shape), whole(start_high.shape)]
            + plane_specs(natural, bx - 1, vol.shape)
            + [whole(low.shape), whole(high.shape), whole(vol_low.shape), whole(vol_high.shape)]
            + [pl.BlockSpec((PLANES, by, bz), lambda s, i: (s, 0, 0))],
            out_specs=pl.BlockSpec((PLANES, by, bz), lambda s, i: (s, 0, 0)),
        ),
        out_shape=jax.ShapeDtypeStruct(vol.shape, F32),
        compiler_params=params(40),
        cost_estimate=cost(5e9, 17),
        name="adjoint",
    )(index, start, start_low, start_high, vol, vol, vol, low, high, vol_low, vol_high, tail)


def neighbours(low_edge, high_edge, axis):
    count = lax.axis_size(axis)
    up = [(k, k + 1) for k in range(count - 1)]
    down = [(k + 1, k) for k in range(count - 1)]
    return lax.ppermute(high_edge, axis, up), lax.ppermute(low_edge, axis, down)


def far_and_near(n):
    return [n // 2] if n > 1 else [], [d for d in range(1, n) if d != n // 2]


def send(pieces, chosen, *earlier):
    n = len(pieces)
    result = list(pieces)
    for d in chosen:
        piece = after(pieces[d], *earlier) if earlier else pieces[d]
        result[d] = lax.ppermute(piece, "narrow", [(k, (k + d) % n) for k in range(n)])
    return result


def pick(pieces, chosen):
    return [pieces[d] for d in chosen]


def after(value, *earlier):
    return lax.optimization_barrier((value, earlier))[0]


def across(piece):
    return lax.all_to_all(piece, "wide", split_axis=0, concat_axis=0, tiled=True)


def row_major(value):
    return with_layout_constraint(value, Layout(major_to_minor=tuple(range(value.ndim))))


def cross_both(pieces, before, between, near, far):
    pieces = [row_major(piece) for piece in pieces]
    lines = send(pieces, near)
    lines = send(lines, far, *pick(lines, near))
    lines = [row_major(line) for line in lines]
    block = jnp.concatenate(pick(lines, [0] + near), axis=1)
    chunks = [across(after(block, *before) if before else block)]
    for d in far:
        chunks.append(across(after(lines[d], chunks[-1], *between)))
    return lines, chunks, pick(lines, far)


def y_edges(chunks):
    return neighbours(chunks[0, :, 0, :], chunks[-1, :, -1, :], "narrow")


def on_device_kernels(state, volatility, cotangent, solve_first, solve_second, solve_third, patch_index):
    n, wide = lax.axis_size("narrow"), lax.axis_size("wide")
    here = lax.axis_index("narrow")
    index = here.astype(jnp.int32).reshape(1)
    bx, by, bz = state.shape
    xs = bx // n
    groups = PATCHES // 128

    ahead = (here + jnp.arange(n)) % n
    back = (here - jnp.arange(n)) % n

    far, near = far_and_near(n)
    every = range(n)

    cot_pieces = [lax.dynamic_slice_in_dim(cotangent, ahead[d] * xs, xs, 0) for d in range(n)]
    early, late = near[:1], near[1:]
    both_low, both_high = neighbours(
        jnp.stack([state[0], volatility[0]]), jnp.stack([state[-1], volatility[-1]]), "wide"
    )
    both = jnp.stack([state[:, :: by - 1], volatility[:, :: by - 1]])
    both = jnp.concatenate([both_low[:, None, :: by - 1], both, both_high[:, None, :: by - 1]], axis=1)
    y_low, y_high = neighbours(both[:, :, 0], both[:, :, 1], "narrow")
    state_x = (both_low[0:1], both_high[0:1])
    vol_x = (both_low[1:2], both_high[1:2])
    state_y = (y_low[0], y_high[0])
    vol_y = (y_low[1], y_high[1])
    cot_lines = send(cot_pieces, near, y_low, y_high)

    second_t = solve_second.T.reshape(n, by, n, by)
    second_t3 = left_form(second_t[ahead][:, :, back].reshape(n * by, n * by))
    second_n = solve_second.reshape(n * by, n, by)
    second_n3 = left_form(second_n[:, back].reshape(n * by, n * by))
    third_t3 = right_form(solve_third)
    third_n3 = right_form(solve_third.T)
    first_n3 = left_form(solve_first)
    first_t = solve_first.T.reshape(wide * bx, wide, n, xs)
    first_t = first_t[:, :, back]
    groups_of = [[0] + near] + [[d] for d in far]
    first_t3 = left_form(
        jnp.concatenate([first_t[:, :, jnp.array(g)].reshape(wide * bx, -1) for g in groups_of], axis=1)
    )

    a, source = forward(index, state, volatility, *state_x, *state_y, wide)
    a = after(a, *pick(cot_lines, early))
    cot_lines = send(cot_lines, far, *pick(cot_lines, near))
    forward_lines = after(first([across(a)], first_n3, 1), *pick(cot_lines, far), second_t3, third_t3)
    back = second(after(cot_lines, forward_lines), second_t3, third_t3, wide)
    solved = across(forward_lines)

    lifted_pieces = lifted(index, solved, state, *state_x, *state_y, n)
    back, carried_chunks, gone = cross_both(back, (solved,), lifted_pieces, near, far)
    carried_lines = first(carried_chunks, first_t3, 1)
    level_lines = send(lifted_pieces, late, gone)
    carried = across(after(carried_lines, *pick(level_lines, late)))

    level_lines = send(level_lines, far, *pick(level_lines, late))
    carried = after(carried, *pick(level_lines, far))
    carried_y = y_edges(carried)
    level_lines = send(level_lines, early, *carried_y)
    totals = react(index, carried, *carried_y, volatility, *vol_x, *vol_y, cotangent, n)
    total_lines = send(totals, near)

    level = second(after(level_lines, totals), second_n3, third_n3, 0)[0]
    drift_pieces = mix(index, level, n)

    def frozen_rows(rows):
        padded = jnp.pad(rows, ((0, 0), (1, 1)))
        curved = padded[:, 2:] + padded[:, :-2] - 2.0 * rows
        return rows + damping * jnp.dot(curved, solve_third.T, precision=lax.Precision.HIGHEST)

    patch_t = patch_index[:, :, None]
    weight, sums = frozen(
        index,
        after(state, *totals),
        *state_x,
        frozen_rows(state_y[0]),
        frozen_rows(state_y[1]),
        third_n3,
        volatility,
        carried,
        patch_index,
        patch_t,
        groups,
    )

    total_lines = send(total_lines, far, sums, *pick(total_lines, near))
    total_lines = after(total_lines, drift_pieces)
    drifts = send(drift_pieces, early, *total_lines)
    uppers = after(second(total_lines, second_t3, third_t3, wide), *pick(drifts, early))
    uppers, start_chunks, gone = cross_both(uppers, (), (), near, far)
    start_lines = first(start_chunks, first_t3, 1)
    drifts = send(drifts, late, gone)
    start = across(after(start_lines, *pick(drifts, late)))

    order = (here - jnp.arange(n)) % n
    edge_low = jnp.stack([piece[0, :, 0] for piece in uppers])[order].reshape(bx, bz)
    edge_high = jnp.stack([piece[-1, :, -1] for piece in uppers])[order].reshape(bx, bz)
    upper_y = neighbours(edge_low, edge_high, "narrow")
    drifts = send(drifts, far, *pick(drifts, late), *upper_y)
    tail = gather_lines(index, totals, uppers, cotangent, *upper_y, third_t3)

    start = after(start, tail)
    start_y = y_edges(start)
    start = after(start, *start_y)
    sums = column_sums(index, drifts, weight, source, start, patch_index, patch_t, sums)
    count, joint = n * wide, ("wide", "narrow")
    sums = (sums[:, :128] + sums[:, 128:]).reshape(count, PATCHES // count)
    shares = lax.all_to_all(sums, joint, split_axis=0, concat_axis=0, tiled=True)
    vega = jnp.sum(shares, axis=0)

    adjoint = finish(index, start, *start_y, volatility, *vol_x, *vol_y, tail)
    return (adjoint, vega * vega_scale)


def on_device(*args):
    n, wide = lax.axis_size("narrow"), lax.axis_size("wide")
    bx, by, bz = args[0].shape
    aligned = bx % (n * PLANES) == 0 and by % 128 == 0 and by % (wide * 8) == 0 and bz == 128
    aligned = aligned and PATCHES % (n * wide) == 0 and by // wide % 2 == 0
    return on_device_kernels(*args) if aligned else on_device_plain(*args)


def solution(mesh):
    placed = (
        P("wide", "narrow", None),
        P("wide", "narrow", None),
        P("wide", "narrow", None),
        P(),
        P(),
        P(),
        P("wide", "narrow"),
    )
    return jax.shard_map(
        on_device,
        mesh=mesh,
        in_specs=placed,
        out_specs=(P("wide", "narrow", None), P(("wide", "narrow"))),
        check_vma=False,
    )
```

```python
import functools
import jax
import jax.numpy as jnp
from jax import lax
from jax.experimental import pallas as pl
from jax.experimental.layout import Layout, with_layout_constraint
from jax.experimental.pallas import tpu as pltpu
from jax.sharding import PartitionSpec as P

PATCHES = 3072


time_step = 0.4
theta_weight = 0.5
frozen_coef = 0.2
correction = 0.5 * 0.4
vega_scale = 1.0 / 32.0
correlations = ((0, 1, 0.5), (0, 2, 0.3), (1, 2, -0.4))


def padded_2(cells, sides, width):
    for axis, dim in sides:
        count = lax.axis_size(axis)
        ends = count - 1
        head = lax.slice_in_dim(cells, 0, width, axis=dim)
        tail = lax.slice_in_dim(cells, cells.shape[dim] - width, cells.shape[dim], axis=dim)
        cells = jnp.concatenate(
            [
                lax.ppermute(tail, axis, [(i, (i + 1) % count) for i in range(ends)]),
                cells,
                lax.ppermute(head, axis, [((i + 1) % count, i) for i in range(ends)]),
            ],
            axis=dim,
        )
    return cells


def along_third(values, offset):
    if offset == 0:
        return values
    zero_layer = jnp.zeros_like(values[..., :1])
    if offset > 0:
        return jnp.concatenate([values[..., 1:], zero_layer], axis=-1)
    return jnp.concatenate([zero_layer, values[..., :-1]], axis=-1)


def shifted(padded, offsets):
    lead = padded.ndim - 3
    slices = [slice(None)] * lead
    for position in range(2):
        offset = offsets[position]
        length = padded.shape[lead + position]
        slices.append(slice(1 + offset, length - 1 + offset))
    slices.append(slice(None))
    return along_third(padded[tuple(slices)], offsets[2])


def second_parts(padded):
    centre = shifted(padded, [0, 0, 0])
    result = []
    for axis_number in range(3):
        upward = [0, 0, 0]
        upward[axis_number] = 1
        downward = [0, 0, 0]
        downward[axis_number] = -1
        result.append(shifted(padded, upward) + shifted(padded, downward) - 2.0 * centre)
    return tuple(result)


def cross_term(padded, first_axis, second_axis):

    def corner(sign_first, sign_second):
        offsets = [0, 0, 0]
        offsets[first_axis] = sign_first
        offsets[second_axis] = sign_second
        return shifted(padded, offsets)

    return 0.25 * (corner(1, 1) - corner(1, -1) - corner(-1, 1) + corner(-1, -1))


def mixed_of(padded):
    total = None
    for first_axis, second_axis, weight in correlations:
        term = weight * cross_term(padded, first_axis, second_axis)
        total = term if total is None else total + term
    return total


def contract(matrix, field, axis_number, transposed):
    letters = "xyz"
    source = letters[axis_number]
    matrix_form = source + "w" if transposed else "w" + source
    result_form = letters.replace(source, "w")
    return jnp.einsum(
        matrix_form + "," + letters + "->" + result_form,
        matrix,
        field,
        precision=lax.Precision.HIGHEST,
    )


def line_x(field, matrix, transposed):

    def solve_lines(pieces):
        solved = contract(matrix, pieces, 0, transposed)
        return lax.all_to_all(solved, "wide", split_axis=0, concat_axis=1, tiled=True)

    return solve_lines(lax.all_to_all(field, "wide", split_axis=1, concat_axis=0, tiled=True))


def line_y(field, matrix, transposed):

    def solve_lines(pieces):
        solved = contract(matrix, pieces, 1, transposed)
        return lax.all_to_all(solved, "narrow", split_axis=1, concat_axis=2, tiled=True)

    return solve_lines(lax.all_to_all(field, "narrow", split_axis=2, concat_axis=1, tiled=True))


def rimmed(stacked):
    return padded_2(stacked, (("wide", 1), ("narrow", 2)), 1)


def third_second(field):
    return along_third(field, 1) + along_third(field, -1) - 2.0 * field


def on_device_plain(state, volatility, cotangent, solve_first, solve_second, solve_third, patch_index):
    coefficient = 0.5 * volatility * volatility
    padded = rimmed(state[None])
    parts = second_parts(padded)
    second_x, second_y, second_z = (parts[0][0], parts[1][0], parts[2][0])
    source = mixed_of(padded)[0] + second_x + second_y + second_z
    start = state + time_step * coefficient * source
    damping = theta_weight * time_step * frozen_coef
    level = line_x(start - damping * second_x, solve_first, False)
    level = line_y(level - damping * second_y, solve_second, False)
    level = contract(solve_third, level - damping * second_z, 2, False)
    drift = mixed_of(rimmed((level - state)[None]))[0]
    back_third = contract(solve_third, cotangent, 2, True)
    back_second = line_y(back_third, solve_second, True)
    carried = line_x(back_second, solve_first, True)
    reaction = mixed_of(rimmed((correction * coefficient * carried)[None]))[0]
    total = cotangent + reaction
    upper_third = contract(solve_third, total, 2, True)
    upper_second = line_y(upper_third, solve_second, True)
    adjoint_start = line_x(upper_second, solve_first, True)
    scaled = time_step * coefficient * adjoint_start
    padded = rimmed(jnp.stack([scaled, adjoint_start, upper_second]))
    parts = second_parts(padded)
    spread = mixed_of(padded[0:1])[0] + parts[0][0] + parts[1][0] + parts[2][0]
    lines = parts[0][1] + parts[1][2] + third_second(upper_third)
    adjoint = adjoint_start + spread - reaction - damping * lines
    sensitivity = volatility * (correction * carried * drift + time_step * adjoint_start * source)
    column = jnp.sum(sensitivity, axis=2)
    partial_sums = jax.ops.segment_sum(
        column.reshape(-1), patch_index.reshape(-1), num_segments=PATCHES
    )
    vega = lax.psum_scatter(partial_sums, ("wide", "narrow"), scatter_dimension=0, tiled=True)
    return (adjoint, vega * vega_scale)


F32 = jnp.float32
BF16 = jnp.bfloat16
damping = 0.5 * 0.4 * 0.2
MIB = 1024 * 1024
PLANES = 8


def params(mib):
    return pltpu.CompilerParams(vmem_limit_bytes=60 * MIB)


def cost(flops, mib):
    return pl.CostEstimate(flops=int(flops / 50), bytes_accessed=int(mib * MIB / 50), transcendentals=0)


def halves(x):
    high = lax.reduce_precision(x, 8, 7)
    return high.astype(BF16), (x - high).astype(BF16)


def left_form(matrix):
    high, low = halves(matrix)
    return jnp.concatenate([high, high, low], axis=1)


def right_form(matrix):
    high, low = halves(matrix)
    return jnp.concatenate([high, high, low], axis=0)


def split(x):
    high = x.astype(BF16)
    return high, (x - high.astype(F32)).astype(BF16)


def left_product(matrix3, field):
    high, low = split(field)
    return jnp.dot(matrix3, jnp.concatenate([high, low, high], axis=0), preferred_element_type=F32)


def right_product(field, matrix3):
    high, low = split(field)
    return jnp.dot(jnp.concatenate([high, low, high], axis=1), matrix3, preferred_element_type=F32)


def y_pair(v, low_row, high_row):
    n = v.shape[0]
    row = lax.broadcasted_iota(jnp.int32, (8, v.shape[1]), 0)
    up, down = pltpu.roll(v, n - 1, 0), pltpu.roll(v, 1, 0)
    up = jnp.concatenate([up[: n - 8], jnp.where(row == 7, high_row, up[n - 8 :])], axis=0)
    down = jnp.concatenate([jnp.where(row == 0, low_row, down[:8]), down[8:]], axis=0)
    return up, down


def z_pair(v):
    n = v.shape[1]
    lane = lax.broadcasted_iota(jnp.int32, v.shape, 1)
    up = jnp.where(lane == n - 1, 0.0, pltpu.roll(v, n - 1, 1))
    down = jnp.where(lane == 0, 0.0, pltpu.roll(v, 1, 1))
    return up, down


def sweep(count, plane, rows, emit, full):
    v, p, rest, inner = {}, {}, {}, {}
    for k in range(-1, count + 1):
        centre = plane(k)
        y_up, y_down = y_pair(centre, *rows(k))
        z_up, z_down = z_pair(centre)
        e = y_up - y_down
        v[k] = centre
        p[k] = 0.125 * e + 0.075 * (z_up - z_down)
        if 0 <= k < count:
            e_up, e_down = z_pair(e)
            rest[k] = -0.1 * (e_up - e_down)
            if full:
                inner[k] = (y_up + y_down) + (z_up + z_down) - 4.0 * centre
        if k >= 1:
            mixed = (p[k] - p[k - 2]) + rest[k - 1]
            emit(k - 1, v[k - 1], v[k - 2], v[k], mixed, inner.get(k - 1))


def chunk_plane(ref, x):
    value = ref[:, x]
    return value.reshape(value.shape[0] * value.shape[1], value.shape[2])


def plane_specs(step_block, last, shape):
    tail = shape[1:]
    return [
        pl.BlockSpec((PLANES,) + tail, lambda s, i: (step_block(s, i), 0, 0)),
        pl.BlockSpec((1,) + tail, lambda s, i: (jnp.maximum(step_block(s, i) * PLANES - 1, 0), 0, 0)),
        pl.BlockSpec((1,) + tail, lambda s, i: (jnp.minimum(step_block(s, i) * PLANES + PLANES, last), 0, 0)),
    ]


def whole(shape):
    return pl.BlockSpec(shape, lambda s, i: (0,) * len(shape))


def pick_plane(k, count, block, main, before, after, low, high, blocks):
    if k < 0:
        return jnp.where(block == 0, low[0], before[0])
    if k >= count:
        return jnp.where(block == blocks - 1, high[0], after[0])
    return main[k]


def natural(s, i):
    return s


def rotated(per, n):
    def block(s, i):
        return lax.rem(i[0] + s // per, n) * per + lax.rem(s, per)

    return block


def piece_map(d, per):
    return lambda s: jnp.clip(s - d * per, 0, per - 1)


def forward_kernel(i, state, before, after, low, high, y_low, y_high, volatility, a_out, source_out, *, blocks):
    block = pl.program_id(0)

    def emit(k, v, prev, nxt, mixed, inner):
        second_x = prev + nxt - 2.0 * v
        source = mixed + second_x + inner
        sigma = volatility[k]
        a = v + (time_step * 0.5) * sigma * sigma * source - damping * second_x
        a_out[:, k] = a.reshape(a_out.shape[0], a_out.shape[2], a_out.shape[3])
        source_out[k] = time_step * sigma * source

    sweep(
        PLANES,
        lambda k: pick_plane(k, PLANES, block, state, before, after, low, high, blocks),
        lambda k: (y_low[pl.ds(block * PLANES + k + 1, 1), :], y_high[pl.ds(block * PLANES + k + 1, 1), :]),
        emit,
        True,
    )


def forward(index, state, volatility, low, high, y_low, y_high, wide):
    bx, by, bz = state.shape
    blocks = bx // PLANES
    return pl.pallas_call(
        functools.partial(forward_kernel, blocks=blocks),
        grid_spec=pltpu.PrefetchScalarGridSpec(
            num_scalar_prefetch=1,
            grid=(blocks,),
            in_specs=plane_specs(natural, bx - 1, state.shape)
            + [whole(low.shape), whole(high.shape), whole(y_low.shape), whole(y_high.shape)]
            + [pl.BlockSpec((PLANES, by, bz), lambda s, i: (s, 0, 0))],
            out_specs=[
                pl.BlockSpec((wide, PLANES, by // wide, bz), lambda s, i: (0, s, 0, 0)),
                pl.BlockSpec((PLANES, by, bz), lambda s, i: (s, 0, 0)),
            ],
        ),
        out_shape=[
            jax.ShapeDtypeStruct((wide, bx, by // wide, bz), F32),
            jax.ShapeDtypeStruct(state.shape, F32),
        ],
        compiler_params=params(32),
        cost_estimate=cost(5e9, 17),
        name="forward",
    )(index, state, state, state, low, high, y_low, y_high, volatility)


def first_kernel(*refs, count, lines, parts, length, halo):
    pieces, matrix3, out = refs[:count], refs[count], refs[count + 1]
    pieces = [piece.reshape(piece.shape[0] * lines, piece.shape[2]) for piece in pieces]
    out = out.reshape(out.shape[0] * lines, out.shape[2])
    rows = length + 2 * halo

    def pair(step, carry):
        y = step * 2
        field = jnp.concatenate(
            [
                jnp.concatenate(
                    [piece[pl.ds(y + t, piece.shape[0] // lines, stride=lines), :] for piece in pieces], axis=0
                )
                for t in range(2)
            ],
            axis=1,
        )
        solved = left_product(matrix3[...], field)
        width = solved.shape[1] // 2
        for t in range(2):
            half = solved[:, t * width : (t + 1) * width]
            for part in range(parts):
                base = part * rows
                out[pl.ds((base + halo) * lines + y + t, length, stride=lines), :] = half[part * length : (part + 1) * length]
                if halo:
                    zero = jnp.zeros((1, width), F32)
                    before = half[part * length - 1 : part * length] if part > 0 else zero
                    after = half[(part + 1) * length : (part + 1) * length + 1] if part < parts - 1 else zero
                    out[pl.ds(base * lines + y + t, 1), :] = before
                    out[pl.ds((base + rows - 1) * lines + y + t, 1), :] = after
        return carry

    lax.fori_loop(0, lines // 2, pair, 0)


def first(pieces, matrix3, halo):
    wide = pieces[0].shape[0]
    lines, bz = pieces[0].shape[2:]
    length = sum(piece.shape[1] for piece in pieces)
    rows = length + 2 * halo
    flat = [piece.reshape(-1, lines, bz) for piece in pieces]
    block = 8
    out = pl.pallas_call(
        functools.partial(first_kernel, count=len(flat), lines=block, parts=wide, length=length, halo=halo),
        grid=(lines // block,),
        in_specs=[pl.BlockSpec((piece.shape[0], block, bz), lambda s: (0, s, 0)) for piece in flat]
        + [pl.BlockSpec(matrix3.shape, lambda s: (0, 0))],
        out_specs=pl.BlockSpec((wide * rows, block, bz), lambda s: (0, s, 0)),
        out_shape=jax.ShapeDtypeStruct((wide * rows, lines, bz), F32),
        compiler_params=params(40),
        cost_estimate=cost(7e9, 10),
        name="first",
    )(*flat, matrix3)
    return out.reshape(wide, rows, lines, bz)


def second_kernel(*refs, count, chunked):
    pieces, second3, third3, outs = refs[:count], refs[count], refs[count + 1], refs[count + 2 :]
    per, by, bz = pieces[0].shape
    length = count * by
    field = jnp.concatenate([piece[x] for x in range(per) for piece in pieces], axis=0)
    field = right_product(field, third3[...])
    field = jnp.concatenate([field[x * length : (x + 1) * length] for x in range(per)], axis=1)
    solved = left_product(second3[...], field)
    for x in range(per):
        half = solved[:, x * bz : (x + 1) * bz]
        if chunked:
            for d in range(count):
                out = outs[d]
                out[:, x] = half[d * by : (d + 1) * by].reshape(out.shape[0], out.shape[2], bz)
        else:
            outs[0][x] = half


def second(pieces, second3, third3, wide):
    count = len(pieces)
    xs, by, bz = pieces[0].shape
    per = 2
    if wide:
        out_specs = [pl.BlockSpec((wide, per, by // wide, bz), lambda s: (0, s, 0, 0))] * count
        out_shape = [jax.ShapeDtypeStruct((wide, xs, by // wide, bz), F32)] * count
    else:
        out_specs = [pl.BlockSpec((per, count * by, bz), lambda s: (s, 0, 0))]
        out_shape = [jax.ShapeDtypeStruct((xs, count * by, bz), F32)]
    return pl.pallas_call(
        functools.partial(second_kernel, count=count, chunked=bool(wide)),
        grid=(xs // per,),
        in_specs=[pl.BlockSpec((per, by, bz), lambda s: (s, 0, 0))] * count
        + [pl.BlockSpec(second3.shape, lambda s: (0, 0)), pl.BlockSpec(third3.shape, lambda s: (0, 0))],
        out_specs=out_specs,
        out_shape=out_shape,
        compiler_params=params(40),
        cost_estimate=cost(9e9, 10),
        name="second",
    )(*pieces, second3, third3)


def piece_specs(size, tail, per, n):
    return [pl.BlockSpec((size,) + tail, lambda s, i, d=d: (jnp.clip(s - d * per, 0, per - 1), 0, 0)) for d in range(n)]


def chunk_piece_specs(wide, lines, bz, per, order):
    return [
        pl.BlockSpec((wide, PLANES, lines, bz), lambda s, i, d=d: (0, jnp.clip(s - d * per, 0, per - 1), 0, 0))
        for d in order
    ]


def store_piece(outs, turn, kept):
    for d, out in enumerate(outs):

        @pl.when(turn == d)
        def _(out=out):
            out[...] = kept[...]


def select(values, turn):
    result = values[0]
    for d in range(1, len(values)):
        result = jnp.where(turn == d, values[d], result)
    return result


def lifted_kernel(i, solved, state, low, high, y_low, y_high, *refs, per, n, size, xs):
    outs, kept = refs[:n], refs[n]
    step = pl.program_id(0)
    bx = state.shape[0]
    base = lax.rem(i[0] + step // per, n) * xs + lax.rem(step, per) * size
    for k in range(size):
        row = base + k
        v = state[jnp.clip(row - 1, 0, bx - 1)]
        v = jnp.where(row == 0, low[0], jnp.where(row == bx + 1, high[0], v))
        up, down = y_pair(v, y_low[pl.ds(row, 1), :], y_high[pl.ds(row, 1), :])
        kept[k] = chunk_plane(solved, row) - damping * (up + down - 2.0 * v)
    store_piece(outs, step // per, kept)


def lifted(index, solved, state, low, high, y_low, y_high, n):
    bx, by, bz = state.shape
    xs = bx // n
    size = next(k for k in range(9, 0, -1) if (xs + 2) % k == 0)
    per = (xs + 2) // size
    return pl.pallas_call(
        functools.partial(lifted_kernel, per=per, n=n, size=size, xs=xs),
        grid_spec=pltpu.PrefetchScalarGridSpec(
            num_scalar_prefetch=1,
            grid=(n * per,),
            in_specs=[whole(v.shape) for v in (solved, state, low, high, y_low, y_high)],
            out_specs=piece_specs(size, (by, bz), per, n),
            scratch_shapes=[pltpu.VMEM((size, by, bz), F32)],
        ),
        out_shape=[jax.ShapeDtypeStruct((xs + 2, by, bz), F32)] * n,
        compiler_params=params(32),
        cost_estimate=cost(2e9, 13),
        name="lifted",
    )(index, solved, state, low, high, y_low, y_high)


def reaction_kernel(
    i, carried, carried_low, carried_high, vol, before, after, low, high, vol_low, vol_high, cotangent, *refs, per, n, blocks
):
    outs, kept = refs[:n], refs[n]
    step = pl.program_id(0)
    block = rotated(per, n)(step, i)

    def plane(k):
        sigma = pick_plane(k, PLANES, block, vol, before, after, low, high, blocks)
        return (0.5 * correction) * sigma * sigma * chunk_plane(carried, block * PLANES + k + 1)

    def rows(k):
        at = pl.ds(block * PLANES + k + 1, 1)
        s_low, s_high = vol_low[at, :], vol_high[at, :]
        return (
            (0.5 * correction) * s_low * s_low * carried_low[at, :],
            (0.5 * correction) * s_high * s_high * carried_high[at, :],
        )

    def emit(k, v, prev, nxt, mixed, inner):
        kept[k] = cotangent[k] + mixed

    sweep(PLANES, plane, rows, emit, False)
    store_piece(outs, step // per, kept)


def react(index, carried, carried_low, carried_high, vol, low, high, vol_low, vol_high, cotangent, n):
    bx, by, bz = vol.shape
    xs = bx // n
    per = xs // PLANES
    block = rotated(per, n)
    return pl.pallas_call(
        functools.partial(reaction_kernel, per=per, n=n, blocks=bx // PLANES),
        grid_spec=pltpu.PrefetchScalarGridSpec(
            num_scalar_prefetch=1,
            grid=(n * per,),
            in_specs=[whole(carried.shape), whole(carried_low.shape), whole(carried_high.shape)]
            + plane_specs(block, bx - 1, vol.shape)
            + [whole(low.shape), whole(high.shape), whole(vol_low.shape), whole(vol_high.shape)]
            + [pl.BlockSpec((PLANES, by, bz), lambda s, i: (block(s, i), 0, 0))],
            out_specs=piece_specs(PLANES, (by, bz), per, n),
            scratch_shapes=[pltpu.VMEM((PLANES, by, bz), F32)],
        ),
        out_shape=[jax.ShapeDtypeStruct((xs, by, bz), F32)] * n,
        compiler_params=params(40),
        cost_estimate=cost(4e9, 17),
        name="reaction",
    )(index, carried, carried_low, carried_high, vol, vol, vol, low, high, vol_low, vol_high, cotangent)


def lines_kernel(i, *refs, per, n):
    totals, uppers = refs[:n], refs[n : 2 * n]
    cotangent, upper_low, upper_high, third3, out = refs[2 * n :]
    step = pl.program_id(0)
    turn = step // per
    block = rotated(per, n)(step, i)
    for k in range(PLANES):
        total = select([ref[k] for ref in totals], turn)
        upper = select([chunk_plane(ref, k) for ref in uppers], turn)
        at = pl.ds(block * PLANES + k, 1)
        up, down = y_pair(upper, upper_low[at, :], upper_high[at, :])
        third = right_product(total, third3[...])
        z_up, z_down = z_pair(third)
        lines = (up + down - 2.0 * upper) + (z_up + z_down - 2.0 * third)
        out[k] = cotangent[k] - total - damping * lines


def gather_lines(index, totals, uppers, cotangent, upper_low, upper_high, third3):
    n = len(totals)
    bx, by, bz = cotangent.shape
    xs = bx // n
    per = xs // PLANES
    wide, lines = uppers[0].shape[0], uppers[0].shape[2]
    block = rotated(per, n)
    order = [(n - e) % n for e in range(n)]
    return pl.pallas_call(
        functools.partial(lines_kernel, per=per, n=n),
        grid_spec=pltpu.PrefetchScalarGridSpec(
            num_scalar_prefetch=1,
            grid=(n * per,),
            in_specs=piece_specs(PLANES, (by, bz), per, n)
            + chunk_piece_specs(wide, lines, bz, per, range(n))
            + [pl.BlockSpec((PLANES, by, bz), lambda s, i: (block(s, i), 0, 0))]
            + [whole(upper_low.shape), whole(upper_high.shape), whole(third3.shape)],
            out_specs=pl.BlockSpec((PLANES, by, bz), lambda s, i: (block(s, i), 0, 0)),
        ),
        out_shape=jax.ShapeDtypeStruct(cotangent.shape, F32),
        compiler_params=params(40),
        cost_estimate=cost(5e9, 17),
        name="lines",
    )(index, *totals, *[uppers[order[d]] for d in range(n)], cotangent, upper_low, upper_high, third3)


def mixed_kernel(i, field, *refs, n):
    outs, scratch = refs[:n], refs[n]
    by = outs[0].shape[1]

    def emit(k, v, prev, nxt, mixed, inner):
        scratch[...] = mixed
        for d, out in enumerate(outs):
            start = pl.multiple_of(lax.rem(i[0] + d, n) * by, by)
            out[k] = scratch[pl.ds(start, by), :]

    zero = jnp.zeros((1, field.shape[2]), F32)
    sweep(field.shape[0] - 2, lambda k: field[k + 1], lambda k: (zero, zero), emit, False)


def mix(index, field, n):
    rows, ny, bz = field.shape
    xs, by = rows - 2, ny // n
    return pl.pallas_call(
        functools.partial(mixed_kernel, n=n),
        grid_spec=pltpu.PrefetchScalarGridSpec(
            num_scalar_prefetch=1,
            grid=(1,),
            in_specs=[whole(field.shape)],
            out_specs=[whole((xs, by, bz))] * n,
            scratch_shapes=[pltpu.VMEM((ny, bz), F32)],
        ),
        out_shape=[jax.ShapeDtypeStruct((xs, by, bz), F32)] * n,
        compiler_params=params(40),
        cost_estimate=cost(4e9, 9),
        name="mixed",
    )(index, field)


def patch_sums(out, step, planes, patch, patch_t, groups):
    @pl.when(step == 0)
    def _():
        out[...] = jnp.zeros_like(out)

    count, (by, bz) = len(planes), planes[0].shape
    value_high, value_low = split(jnp.concatenate(planes, axis=0))
    ones = jnp.ones((2 * bz, 128), BF16)
    column = jnp.dot(jnp.concatenate([value_high, value_low], axis=1), ones, preferred_element_type=F32)
    number = jnp.concatenate([patch[pl.ds(k, 1), :] for k in range(count)], axis=1)
    coarse = lax.broadcasted_iota(jnp.int32, (groups, count * by), 0) == lax.shift_right_logical(number, 7)
    number_t = patch_t[...].reshape(count * by, 1)
    lane = lax.broadcasted_iota(jnp.int32, (count * by, 128), 1)
    high, low = split(jnp.where(lane == lax.bitwise_and(number_t, 127), column, 0.0))
    out[...] += jnp.dot(
        jnp.where(coarse, 1.0, 0.0).astype(BF16), jnp.concatenate([high, low], axis=1), preferred_element_type=F32
    )


def frozen_kernel(
    i, state, before, after, low, high, q_low, q_high, third3, vol, carried, patch, patch_t, weight, out, *, blocks, groups
):
    block = pl.program_id(0)
    planes = []

    def plane(k):
        v = pick_plane(k, PLANES, block, state, before, after, low, high, blocks)
        up, down = z_pair(v)
        return v + damping * right_product(up + down - 2.0 * v, third3[...])

    def emit(k, v, prev, nxt, mixed, inner):
        w = correction * vol[k] * chunk_plane(carried, block * PLANES + k + 1)
        weight[k] = w
        planes.append(-w * mixed)

    sweep(
        PLANES,
        plane,
        lambda k: (q_low[pl.ds(block * PLANES + k + 1, 1), :], q_high[pl.ds(block * PLANES + k + 1, 1), :]),
        emit,
        False,
    )
    patch_sums(out, block, planes, patch, patch_t, groups)


def frozen(index, state, low, high, q_low, q_high, third3, vol, carried, patch, patch_t, groups):
    bx, by, bz = state.shape
    blocks = bx // PLANES
    main = pl.BlockSpec((PLANES, by, bz), lambda s, i: (s, 0, 0))
    return pl.pallas_call(
        functools.partial(frozen_kernel, blocks=blocks, groups=groups),
        grid_spec=pltpu.PrefetchScalarGridSpec(
            num_scalar_prefetch=1,
            grid=(blocks,),
            in_specs=plane_specs(natural, bx - 1, state.shape)
            + [whole(low.shape), whole(high.shape), whole(q_low.shape), whole(q_high.shape), whole(third3.shape)]
            + [main, whole(carried.shape)]
            + [pl.BlockSpec((PLANES, by), lambda s, i: (s, 0))]
            + [pl.BlockSpec((PLANES, by, 1), lambda s, i: (s, 0, 0))],
            out_specs=[main, whole((groups, 256))],
        ),
        out_shape=[jax.ShapeDtypeStruct(state.shape, F32), jax.ShapeDtypeStruct((groups, 256), F32)],
        compiler_params=params(32),
        cost_estimate=cost(5e9, 17),
        name="frozen",
    )(index, state, state, state, low, high, q_low, q_high, third3, vol, carried, patch, patch_t)


def column_kernel(i, *refs, per, n, groups):
    drifts = refs[:n]
    weight, source, start, patch, patch_t, given, out = refs[n:]
    step = pl.program_id(0)
    turn = step // per
    block = rotated(per, n)(step, i)
    planes = [
        weight[k] * select([ref[k] for ref in drifts], turn)
        + source[k] * chunk_plane(start, block * PLANES + k + 1)
        for k in range(PLANES)
    ]
    patch_sums(out, step, planes, patch, patch_t, groups)

    @pl.when(step == pl.num_programs(0) - 1)
    def _():
        out[...] += given[...]


def column_sums(index, drifts, weight, source, start, patch, patch_t, given):
    n = len(drifts)
    bx, by, bz = source.shape
    xs = bx // n
    per = xs // PLANES
    groups = given.shape[0]
    block = rotated(per, n)
    order = [(n - e) % n for e in range(n)]
    main = pl.BlockSpec((PLANES, by, bz), lambda s, i: (block(s, i), 0, 0))
    return pl.pallas_call(
        functools.partial(column_kernel, per=per, n=n, groups=groups),
        grid_spec=pltpu.PrefetchScalarGridSpec(
            num_scalar_prefetch=1,
            grid=(n * per,),
            in_specs=piece_specs(PLANES, (by, bz), per, n)
            + [main, main, whole(start.shape)]
            + [pl.BlockSpec((PLANES, by), lambda s, i: (block(s, i), 0))]
            + [pl.BlockSpec((PLANES, by, 1), lambda s, i: (block(s, i), 0, 0)), whole(given.shape)],
            out_specs=whole(given.shape),
        ),
        out_shape=jax.ShapeDtypeStruct(given.shape, F32),
        compiler_params=params(40),
        cost_estimate=cost(4e9, 17),
        name="column",
    )(index, *[drifts[order[d]] for d in range(n)], weight, source, start, patch, patch_t, given)


def adjoint_kernel(
    i, start, start_low, start_high, vol, before, after, low, high, vol_low, vol_high, tail, out, *, blocks
):
    block = pl.program_id(0)
    raw = {}

    def plane(k):
        sigma = pick_plane(k, PLANES, block, vol, before, after, low, high, blocks)
        raw[k] = chunk_plane(start, block * PLANES + k + 1)
        return (0.5 * time_step) * sigma * sigma * raw[k]

    def rows(k):
        at = pl.ds(block * PLANES + k + 1, 1)
        s_low, s_high = vol_low[at, :], vol_high[at, :]
        return (
            (0.5 * time_step) * s_low * s_low * start_low[at, :],
            (0.5 * time_step) * s_high * s_high * start_high[at, :],
        )

    def emit(k, v, prev, nxt, mixed, inner):
        spread = mixed + (prev + nxt - 2.0 * v) + inner
        lines = raw[k - 1] + raw[k + 1] - 2.0 * raw[k]
        out[k] = raw[k] + spread + tail[k] - damping * lines

    sweep(PLANES, plane, rows, emit, True)


def finish(index, start, start_low, start_high, vol, low, high, vol_low, vol_high, tail):
    bx, by, bz = vol.shape
    return pl.pallas_call(
        functools.partial(adjoint_kernel, blocks=bx // PLANES),
        grid_spec=pltpu.PrefetchScalarGridSpec(
            num_scalar_prefetch=1,
            grid=(bx // PLANES,),
            in_specs=[whole(start.shape), whole(start_low.shape), whole(start_high.shape)]
            + plane_specs(natural, bx - 1, vol.shape)
            + [whole(low.shape), whole(high.shape), whole(vol_low.shape), whole(vol_high.shape)]
            + [pl.BlockSpec((PLANES, by, bz), lambda s, i: (s, 0, 0))],
            out_specs=pl.BlockSpec((PLANES, by, bz), lambda s, i: (s, 0, 0)),
        ),
        out_shape=jax.ShapeDtypeStruct(vol.shape, F32),
        compiler_params=params(40),
        cost_estimate=cost(5e9, 17),
        name="adjoint",
    )(index, start, start_low, start_high, vol, vol, vol, low, high, vol_low, vol_high, tail)


def neighbours(low_edge, high_edge, axis):
    count = lax.axis_size(axis)
    up = [(k, k + 1) for k in range(count - 1)]
    down = [(k + 1, k) for k in range(count - 1)]
    return lax.ppermute(high_edge, axis, up), lax.ppermute(low_edge, axis, down)


def far_and_near(n):
    return [n // 2] if n > 1 else [], [d for d in range(1, n) if d != n // 2]


def send(pieces, chosen, *earlier):
    n = len(pieces)
    result = list(pieces)
    for d in chosen:
        piece = after(pieces[d], *earlier) if earlier else pieces[d]
        result[d] = lax.ppermute(piece, "narrow", [(k, (k + d) % n) for k in range(n)])
    return result


def pick(pieces, chosen):
    return [pieces[d] for d in chosen]


def after(value, *earlier):
    return lax.optimization_barrier((value, earlier))[0]


def across(piece):
    return lax.all_to_all(piece, "wide", split_axis=0, concat_axis=0, tiled=True)


def row_major(value):
    return with_layout_constraint(value, Layout(major_to_minor=tuple(range(value.ndim))))


def cross_both(pieces, before, between, near, far):
    pieces = [row_major(piece) for piece in pieces]
    lines = send(pieces, near)
    lines = send(lines, far, *pick(lines, near))
    lines = [row_major(line) for line in lines]
    block = jnp.concatenate(pick(lines, [0] + near), axis=1)
    chunks = [across(after(block, *before) if before else block)]
    for d in far:
        chunks.append(across(after(lines[d], chunks[-1], *between)))
    return lines, chunks, pick(lines, far)


def y_edges(chunks):
    return neighbours(chunks[0, :, 0, :], chunks[-1, :, -1, :], "narrow")


def on_device_kernels(state, volatility, cotangent, solve_first, solve_second, solve_third, patch_index):
    n, wide = lax.axis_size("narrow"), lax.axis_size("wide")
    here = lax.axis_index("narrow")
    index = here.astype(jnp.int32).reshape(1)
    bx, by, bz = state.shape
    xs = bx // n
    groups = PATCHES // 128

    ahead = (here + jnp.arange(n)) % n
    back = (here - jnp.arange(n)) % n

    far, near = far_and_near(n)
    every = range(n)

    cot_pieces = [lax.dynamic_slice_in_dim(cotangent, ahead[d] * xs, xs, 0) for d in range(n)]
    early, late = near[:1], near[1:]
    both_low, both_high = neighbours(
        jnp.stack([state[0], volatility[0]]), jnp.stack([state[-1], volatility[-1]]), "wide"
    )
    both = jnp.stack([state[:, :: by - 1], volatility[:, :: by - 1]])
    both = jnp.concatenate([both_low[:, None, :: by - 1], both, both_high[:, None, :: by - 1]], axis=1)
    y_low, y_high = neighbours(both[:, :, 0], both[:, :, 1], "narrow")
    state_x = (both_low[0:1], both_high[0:1])
    vol_x = (both_low[1:2], both_high[1:2])
    state_y = (y_low[0], y_high[0])
    vol_y = (y_low[1], y_high[1])
    cot_lines = send(cot_pieces, near, y_low, y_high)

    second_t = solve_second.T.reshape(n, by, n, by)
    second_t3 = left_form(second_t[ahead][:, :, back].reshape(n * by, n * by))
    second_n = solve_second.reshape(n * by, n, by)
    second_n3 = left_form(second_n[:, back].reshape(n * by, n * by))
    third_t3 = right_form(solve_third)
    third_n3 = right_form(solve_third.T)
    first_n3 = left_form(solve_first)
    first_t = solve_first.T.reshape(wide * bx, wide, n, xs)
    first_t = first_t[:, :, back]
    groups_of = [[0] + near] + [[d] for d in far]
    first_t3 = left_form(
        jnp.concatenate([first_t[:, :, jnp.array(g)].reshape(wide * bx, -1) for g in groups_of], axis=1)
    )

    a, source = forward(index, state, volatility, *state_x, *state_y, wide)
    a = after(a, *pick(cot_lines, early))
    cot_lines = send(cot_lines, far, *pick(cot_lines, near))
    forward_lines = after(first([across(a)], first_n3, 1), *pick(cot_lines, far), second_t3, third_t3)
    back = second(after(cot_lines, forward_lines), second_t3, third_t3, wide)
    solved = across(forward_lines)

    lifted_pieces = lifted(index, solved, state, *state_x, *state_y, n)
    back, carried_chunks, gone = cross_both(back, (solved,), lifted_pieces, near, far)
    carried_lines = first(carried_chunks, first_t3, 1)
    level_lines = send(lifted_pieces, late, gone)
    carried = across(after(carried_lines, *pick(level_lines, late)))

    level_lines = send(level_lines, far, *pick(level_lines, late))
    carried = after(carried, *pick(level_lines, far))
    carried_y = y_edges(carried)
    level_lines = send(level_lines, early, *carried_y)
    totals = react(index, carried, *carried_y, volatility, *vol_x, *vol_y, cotangent, n)
    total_lines = send(totals, near)

    level = second(after(level_lines, totals), second_n3, third_n3, 0)[0]
    drift_pieces = mix(index, level, n)

    def frozen_rows(rows):
        padded = jnp.pad(rows, ((0, 0), (1, 1)))
        curved = padded[:, 2:] + padded[:, :-2] - 2.0 * rows
        return rows + damping * jnp.dot(curved, solve_third.T, precision=lax.Precision.HIGHEST)

    patch_t = patch_index[:, :, None]
    weight, sums = frozen(
        index,
        after(state, *totals),
        *state_x,
        frozen_rows(state_y[0]),
        frozen_rows(state_y[1]),
        third_n3,
        volatility,
        carried,
        patch_index,
        patch_t,
        groups,
    )

    total_lines = send(total_lines, far, sums, *pick(total_lines, near))
    total_lines = after(total_lines, drift_pieces)
    drifts = send(drift_pieces, early, *total_lines)
    uppers = after(second(total_lines, second_t3, third_t3, wide), *pick(drifts, early))
    uppers, start_chunks, gone = cross_both(uppers, (), (), near, far)
    start_lines = first(start_chunks, first_t3, 1)
    drifts = send(drifts, late, gone)
    start = across(after(start_lines, *pick(drifts, late)))

    order = (here - jnp.arange(n)) % n
    edge_low = jnp.stack([piece[0, :, 0] for piece in uppers])[order].reshape(bx, bz)
    edge_high = jnp.stack([piece[-1, :, -1] for piece in uppers])[order].reshape(bx, bz)
    upper_y = neighbours(edge_low, edge_high, "narrow")
    drifts = send(drifts, far, *pick(drifts, late), *upper_y)
    tail = gather_lines(index, totals, uppers, cotangent, *upper_y, third_t3)

    start = after(start, tail)
    start_y = y_edges(start)
    sums = column_sums(index, drifts, weight, source, start, patch_index, patch_t, sums)
    count, joint = n * wide, ("wide", "narrow")
    sums = (sums[:, :128] + sums[:, 128:]).reshape(count, PATCHES // count)
    shares = lax.all_to_all(sums, joint, split_axis=0, concat_axis=0, tiled=True)
    vega = jnp.sum(shares, axis=0)

    adjoint = finish(index, start, *start_y, volatility, *vol_x, *vol_y, tail)
    return (adjoint, vega * vega_scale)


def on_device(*args):
    n, wide = lax.axis_size("narrow"), lax.axis_size("wide")
    bx, by, bz = args[0].shape
    aligned = bx % (n * PLANES) == 0 and by % 128 == 0 and by % (wide * 8) == 0 and bz == 128
    aligned = aligned and PATCHES % (n * wide) == 0 and by // wide % 2 == 0
    return on_device_kernels(*args) if aligned else on_device_plain(*args)


def solution(mesh):
    placed = (
        P("wide", "narrow", None),
        P("wide", "narrow", None),
        P("wide", "narrow", None),
        P(),
        P(),
        P(),
        P("wide", "narrow"),
    )
    return jax.shard_map(
        on_device,
        mesh=mesh,
        in_specs=placed,
        out_specs=(P("wide", "narrow", None), P(("wide", "narrow"))),
        check_vma=False,
    )
```

```python
import functools
import jax
import jax.numpy as jnp
from jax import lax
from jax.experimental import pallas as pl
from jax.experimental.layout import Layout, with_layout_constraint
from jax.experimental.pallas import tpu as pltpu
from jax.sharding import PartitionSpec as P

PATCHES = 3072


time_step = 0.4
theta_weight = 0.5
frozen_coef = 0.2
correction = 0.5 * 0.4
vega_scale = 1.0 / 32.0
correlations = ((0, 1, 0.5), (0, 2, 0.3), (1, 2, -0.4))


def padded_2(cells, sides, width):
    for axis, dim in sides:
        count = lax.axis_size(axis)
        ends = count - 1
        head = lax.slice_in_dim(cells, 0, width, axis=dim)
        tail = lax.slice_in_dim(cells, cells.shape[dim] - width, cells.shape[dim], axis=dim)
        cells = jnp.concatenate(
            [
                lax.ppermute(tail, axis, [(i, (i + 1) % count) for i in range(ends)]),
                cells,
                lax.ppermute(head, axis, [((i + 1) % count, i) for i in range(ends)]),
            ],
            axis=dim,
        )
    return cells


def along_third(values, offset):
    if offset == 0:
        return values
    zero_layer = jnp.zeros_like(values[..., :1])
    if offset > 0:
        return jnp.concatenate([values[..., 1:], zero_layer], axis=-1)
    return jnp.concatenate([zero_layer, values[..., :-1]], axis=-1)


def shifted(padded, offsets):
    lead = padded.ndim - 3
    slices = [slice(None)] * lead
    for position in range(2):
        offset = offsets[position]
        length = padded.shape[lead + position]
        slices.append(slice(1 + offset, length - 1 + offset))
    slices.append(slice(None))
    return along_third(padded[tuple(slices)], offsets[2])


def second_parts(padded):
    centre = shifted(padded, [0, 0, 0])
    result = []
    for axis_number in range(3):
        upward = [0, 0, 0]
        upward[axis_number] = 1
        downward = [0, 0, 0]
        downward[axis_number] = -1
        result.append(shifted(padded, upward) + shifted(padded, downward) - 2.0 * centre)
    return tuple(result)


def cross_term(padded, first_axis, second_axis):

    def corner(sign_first, sign_second):
        offsets = [0, 0, 0]
        offsets[first_axis] = sign_first
        offsets[second_axis] = sign_second
        return shifted(padded, offsets)

    return 0.25 * (corner(1, 1) - corner(1, -1) - corner(-1, 1) + corner(-1, -1))


def mixed_of(padded):
    total = None
    for first_axis, second_axis, weight in correlations:
        term = weight * cross_term(padded, first_axis, second_axis)
        total = term if total is None else total + term
    return total


def contract(matrix, field, axis_number, transposed):
    letters = "xyz"
    source = letters[axis_number]
    matrix_form = source + "w" if transposed else "w" + source
    result_form = letters.replace(source, "w")
    return jnp.einsum(
        matrix_form + "," + letters + "->" + result_form,
        matrix,
        field,
        precision=lax.Precision.HIGHEST,
    )


def line_x(field, matrix, transposed):

    def solve_lines(pieces):
        solved = contract(matrix, pieces, 0, transposed)
        return lax.all_to_all(solved, "wide", split_axis=0, concat_axis=1, tiled=True)

    return solve_lines(lax.all_to_all(field, "wide", split_axis=1, concat_axis=0, tiled=True))


def line_y(field, matrix, transposed):

    def solve_lines(pieces):
        solved = contract(matrix, pieces, 1, transposed)
        return lax.all_to_all(solved, "narrow", split_axis=1, concat_axis=2, tiled=True)

    return solve_lines(lax.all_to_all(field, "narrow", split_axis=2, concat_axis=1, tiled=True))


def rimmed(stacked):
    return padded_2(stacked, (("wide", 1), ("narrow", 2)), 1)


def third_second(field):
    return along_third(field, 1) + along_third(field, -1) - 2.0 * field


def on_device_plain(state, volatility, cotangent, solve_first, solve_second, solve_third, patch_index):
    coefficient = 0.5 * volatility * volatility
    padded = rimmed(state[None])
    parts = second_parts(padded)
    second_x, second_y, second_z = (parts[0][0], parts[1][0], parts[2][0])
    source = mixed_of(padded)[0] + second_x + second_y + second_z
    start = state + time_step * coefficient * source
    damping = theta_weight * time_step * frozen_coef
    level = line_x(start - damping * second_x, solve_first, False)
    level = line_y(level - damping * second_y, solve_second, False)
    level = contract(solve_third, level - damping * second_z, 2, False)
    drift = mixed_of(rimmed((level - state)[None]))[0]
    back_third = contract(solve_third, cotangent, 2, True)
    back_second = line_y(back_third, solve_second, True)
    carried = line_x(back_second, solve_first, True)
    reaction = mixed_of(rimmed((correction * coefficient * carried)[None]))[0]
    total = cotangent + reaction
    upper_third = contract(solve_third, total, 2, True)
    upper_second = line_y(upper_third, solve_second, True)
    adjoint_start = line_x(upper_second, solve_first, True)
    scaled = time_step * coefficient * adjoint_start
    padded = rimmed(jnp.stack([scaled, adjoint_start, upper_second]))
    parts = second_parts(padded)
    spread = mixed_of(padded[0:1])[0] + parts[0][0] + parts[1][0] + parts[2][0]
    lines = parts[0][1] + parts[1][2] + third_second(upper_third)
    adjoint = adjoint_start + spread - reaction - damping * lines
    sensitivity = volatility * (correction * carried * drift + time_step * adjoint_start * source)
    column = jnp.sum(sensitivity, axis=2)
    partial_sums = jax.ops.segment_sum(
        column.reshape(-1), patch_index.reshape(-1), num_segments=PATCHES
    )
    vega = lax.psum_scatter(partial_sums, ("wide", "narrow"), scatter_dimension=0, tiled=True)
    return (adjoint, vega * vega_scale)


F32 = jnp.float32
BF16 = jnp.bfloat16
damping = 0.5 * 0.4 * 0.2
MIB = 1024 * 1024
PLANES = 8


def params(mib):
    return pltpu.CompilerParams(vmem_limit_bytes=60 * MIB)


def cost(flops, mib):
    return pl.CostEstimate(flops=int(flops / 50), bytes_accessed=int(mib * MIB / 50), transcendentals=0)


def halves(x):
    high = lax.reduce_precision(x, 8, 7)
    return high.astype(BF16), (x - high).astype(BF16)


def left_form(matrix):
    high, low = halves(matrix)
    return jnp.concatenate([high, high, low], axis=1)


def right_form(matrix):
    high, low = halves(matrix)
    return jnp.concatenate([high, high, low], axis=0)


def split(x):
    high = x.astype(BF16)
    return high, (x - high.astype(F32)).astype(BF16)


def left_product(matrix3, field):
    high, low = split(field)
    return jnp.dot(matrix3, jnp.concatenate([high, low, high], axis=0), preferred_element_type=F32)


def right_product(field, matrix3):
    high, low = split(field)
    return jnp.dot(jnp.concatenate([high, low, high], axis=1), matrix3, preferred_element_type=F32)


def y_pair(v, low_row, high_row):
    n = v.shape[0]
    row = lax.broadcasted_iota(jnp.int32, (8, v.shape[1]), 0)
    up, down = pltpu.roll(v, n - 1, 0), pltpu.roll(v, 1, 0)
    up = jnp.concatenate([up[: n - 8], jnp.where(row == 7, high_row, up[n - 8 :])], axis=0)
    down = jnp.concatenate([jnp.where(row == 0, low_row, down[:8]), down[8:]], axis=0)
    return up, down


def z_pair(v):
    n = v.shape[1]
    lane = lax.broadcasted_iota(jnp.int32, v.shape, 1)
    up = jnp.where(lane == n - 1, 0.0, pltpu.roll(v, n - 1, 1))
    down = jnp.where(lane == 0, 0.0, pltpu.roll(v, 1, 1))
    return up, down


def sweep(count, plane, rows, emit, full):
    v, p, rest, inner = {}, {}, {}, {}
    for k in range(-1, count + 1):
        centre = plane(k)
        y_up, y_down = y_pair(centre, *rows(k))
        z_up, z_down = z_pair(centre)
        e = y_up - y_down
        v[k] = centre
        p[k] = 0.125 * e + 0.075 * (z_up - z_down)
        if 0 <= k < count:
            e_up, e_down = z_pair(e)
            rest[k] = -0.1 * (e_up - e_down)
            if full:
                inner[k] = (y_up + y_down) + (z_up + z_down) - 4.0 * centre
        if k >= 1:
            mixed = (p[k] - p[k - 2]) + rest[k - 1]
            emit(k - 1, v[k - 1], v[k - 2], v[k], mixed, inner.get(k - 1))


def chunk_plane(ref, x):
    value = ref[:, x]
    return value.reshape(value.shape[0] * value.shape[1], value.shape[2])


def plane_specs(step_block, last, shape):
    tail = shape[1:]
    return [
        pl.BlockSpec((PLANES,) + tail, lambda s, i: (step_block(s, i), 0, 0)),
        pl.BlockSpec((1,) + tail, lambda s, i: (jnp.maximum(step_block(s, i) * PLANES - 1, 0), 0, 0)),
        pl.BlockSpec((1,) + tail, lambda s, i: (jnp.minimum(step_block(s, i) * PLANES + PLANES, last), 0, 0)),
    ]


def whole(shape):
    return pl.BlockSpec(shape, lambda s, i: (0,) * len(shape))


def pick_plane(k, count, block, main, before, after, low, high, blocks):
    if k < 0:
        return jnp.where(block == 0, low[0], before[0])
    if k >= count:
        return jnp.where(block == blocks - 1, high[0], after[0])
    return main[k]


def natural(s, i):
    return s


def rotated(per, n):
    def block(s, i):
        return lax.rem(i[0] + s // per, n) * per + lax.rem(s, per)

    return block


def piece_map(d, per):
    return lambda s: jnp.clip(s - d * per, 0, per - 1)


def forward_kernel(i, state, before, after, low, high, y_low, y_high, volatility, a_out, source_out, *, blocks):
    block = pl.program_id(0)

    def emit(k, v, prev, nxt, mixed, inner):
        second_x = prev + nxt - 2.0 * v
        source = mixed + second_x + inner
        sigma = volatility[k]
        a = v + (time_step * 0.5) * sigma * sigma * source - damping * second_x
        a_out[:, k] = a.reshape(a_out.shape[0], a_out.shape[2], a_out.shape[3])
        source_out[k] = time_step * sigma * source

    sweep(
        PLANES,
        lambda k: pick_plane(k, PLANES, block, state, before, after, low, high, blocks),
        lambda k: (y_low[pl.ds(block * PLANES + k + 1, 1), :], y_high[pl.ds(block * PLANES + k + 1, 1), :]),
        emit,
        True,
    )


def forward(index, state, volatility, low, high, y_low, y_high, wide):
    bx, by, bz = state.shape
    blocks = bx // PLANES
    return pl.pallas_call(
        functools.partial(forward_kernel, blocks=blocks),
        grid_spec=pltpu.PrefetchScalarGridSpec(
            num_scalar_prefetch=1,
            grid=(blocks,),
            in_specs=plane_specs(natural, bx - 1, state.shape)
            + [whole(low.shape), whole(high.shape), whole(y_low.shape), whole(y_high.shape)]
            + [pl.BlockSpec((PLANES, by, bz), lambda s, i: (s, 0, 0))],
            out_specs=[
                pl.BlockSpec((wide, PLANES, by // wide, bz), lambda s, i: (0, s, 0, 0)),
                pl.BlockSpec((PLANES, by, bz), lambda s, i: (s, 0, 0)),
            ],
        ),
        out_shape=[
            jax.ShapeDtypeStruct((wide, bx, by // wide, bz), F32),
            jax.ShapeDtypeStruct(state.shape, F32),
        ],
        compiler_params=params(32),
        cost_estimate=cost(5e9, 17),
        name="forward",
    )(index, state, state, state, low, high, y_low, y_high, volatility)


def first_kernel(*refs, count, lines, parts, length, halo):
    pieces, matrix3, out = refs[:count], refs[count], refs[count + 1]
    pieces = [piece.reshape(piece.shape[0] * lines, piece.shape[2]) for piece in pieces]
    out = out.reshape(out.shape[0] * lines, out.shape[2])
    rows = length + 2 * halo

    def pair(step, carry):
        y = step * 2
        field = jnp.concatenate(
            [
                jnp.concatenate(
                    [piece[pl.ds(y + t, piece.shape[0] // lines, stride=lines), :] for piece in pieces], axis=0
                )
                for t in range(2)
            ],
            axis=1,
        )
        solved = left_product(matrix3[...], field)
        width = solved.shape[1] // 2
        for t in range(2):
            half = solved[:, t * width : (t + 1) * width]
            for part in range(parts):
                base = part * rows
                out[pl.ds((base + halo) * lines + y + t, length, stride=lines), :] = half[part * length : (part + 1) * length]
                if halo:
                    zero = jnp.zeros((1, width), F32)
                    before = half[part * length - 1 : part * length] if part > 0 else zero
                    after = half[(part + 1) * length : (part + 1) * length + 1] if part < parts - 1 else zero
                    out[pl.ds(base * lines + y + t, 1), :] = before
                    out[pl.ds((base + rows - 1) * lines + y + t, 1), :] = after
        return carry

    lax.fori_loop(0, lines // 2, pair, 0)


def first(pieces, matrix3, halo):
    wide = pieces[0].shape[0]
    lines, bz = pieces[0].shape[2:]
    length = sum(piece.shape[1] for piece in pieces)
    rows = length + 2 * halo
    flat = [piece.reshape(-1, lines, bz) for piece in pieces]
    block = 8
    out = pl.pallas_call(
        functools.partial(first_kernel, count=len(flat), lines=block, parts=wide, length=length, halo=halo),
        grid=(lines // block,),
        in_specs=[pl.BlockSpec((piece.shape[0], block, bz), lambda s: (0, s, 0)) for piece in flat]
        + [pl.BlockSpec(matrix3.shape, lambda s: (0, 0))],
        out_specs=pl.BlockSpec((wide * rows, block, bz), lambda s: (0, s, 0)),
        out_shape=jax.ShapeDtypeStruct((wide * rows, lines, bz), F32),
        compiler_params=params(40),
        cost_estimate=cost(7e9, 10),
        name="first",
    )(*flat, matrix3)
    return out.reshape(wide, rows, lines, bz)


def second_kernel(*refs, count, chunked):
    pieces, second3, third3, outs = refs[:count], refs[count], refs[count + 1], refs[count + 2 :]
    per, by, bz = pieces[0].shape
    length = count * by
    field = jnp.concatenate([piece[x] for x in range(per) for piece in pieces], axis=0)
    field = right_product(field, third3[...])
    field = jnp.concatenate([field[x * length : (x + 1) * length] for x in range(per)], axis=1)
    solved = left_product(second3[...], field)
    for x in range(per):
        half = solved[:, x * bz : (x + 1) * bz]
        if chunked:
            for d in range(count):
                out = outs[d]
                out[:, x] = half[d * by : (d + 1) * by].reshape(out.shape[0], out.shape[2], bz)
        else:
            outs[0][x] = half


def second(pieces, second3, third3, wide):
    count = len(pieces)
    xs, by, bz = pieces[0].shape
    per = 2
    if wide:
        out_specs = [pl.BlockSpec((wide, per, by // wide, bz), lambda s: (0, s, 0, 0))] * count
        out_shape = [jax.ShapeDtypeStruct((wide, xs, by // wide, bz), F32)] * count
    else:
        out_specs = [pl.BlockSpec((per, count * by, bz), lambda s: (s, 0, 0))]
        out_shape = [jax.ShapeDtypeStruct((xs, count * by, bz), F32)]
    return pl.pallas_call(
        functools.partial(second_kernel, count=count, chunked=bool(wide)),
        grid=(xs // per,),
        in_specs=[pl.BlockSpec((per, by, bz), lambda s: (s, 0, 0))] * count
        + [pl.BlockSpec(second3.shape, lambda s: (0, 0)), pl.BlockSpec(third3.shape, lambda s: (0, 0))],
        out_specs=out_specs,
        out_shape=out_shape,
        compiler_params=params(40),
        cost_estimate=cost(9e9, 10),
        name="second",
    )(*pieces, second3, third3)


def piece_specs(size, tail, per, n):
    return [pl.BlockSpec((size,) + tail, lambda s, i, d=d: (jnp.clip(s - d * per, 0, per - 1), 0, 0)) for d in range(n)]


def chunk_piece_specs(wide, lines, bz, per, order):
    return [
        pl.BlockSpec((wide, PLANES, lines, bz), lambda s, i, d=d: (0, jnp.clip(s - d * per, 0, per - 1), 0, 0))
        for d in order
    ]


def store_piece(outs, turn, kept):
    for d, out in enumerate(outs):

        @pl.when(turn == d)
        def _(out=out):
            out[...] = kept[...]


def select(values, turn):
    result = values[0]
    for d in range(1, len(values)):
        result = jnp.where(turn == d, values[d], result)
    return result


def lifted_kernel(i, solved, state, low, high, y_low, y_high, *refs, per, n, size, xs):
    outs, kept = refs[:n], refs[n]
    step = pl.program_id(0)
    bx = state.shape[0]
    base = lax.rem(i[0] + step // per, n) * xs + lax.rem(step, per) * size
    for k in range(size):
        row = base + k
        v = state[jnp.clip(row - 1, 0, bx - 1)]
        v = jnp.where(row == 0, low[0], jnp.where(row == bx + 1, high[0], v))
        up, down = y_pair(v, y_low[pl.ds(row, 1), :], y_high[pl.ds(row, 1), :])
        kept[k] = chunk_plane(solved, row) - damping * (up + down - 2.0 * v)
    store_piece(outs, step // per, kept)


def lifted(index, solved, state, low, high, y_low, y_high, n):
    bx, by, bz = state.shape
    xs = bx // n
    size = next(k for k in range(9, 0, -1) if (xs + 2) % k == 0)
    per = (xs + 2) // size
    return pl.pallas_call(
        functools.partial(lifted_kernel, per=per, n=n, size=size, xs=xs),
        grid_spec=pltpu.PrefetchScalarGridSpec(
            num_scalar_prefetch=1,
            grid=(n * per,),
            in_specs=[whole(v.shape) for v in (solved, state, low, high, y_low, y_high)],
            out_specs=piece_specs(size, (by, bz), per, n),
            scratch_shapes=[pltpu.VMEM((size, by, bz), F32)],
        ),
        out_shape=[jax.ShapeDtypeStruct((xs + 2, by, bz), F32)] * n,
        compiler_params=params(32),
        cost_estimate=cost(2e9, 13),
        name="lifted",
    )(index, solved, state, low, high, y_low, y_high)


def reaction_kernel(
    i, carried, carried_low, carried_high, vol, before, after, low, high, vol_low, vol_high, cotangent, *refs, per, n, blocks
):
    outs, kept = refs[:n], refs[n]
    step = pl.program_id(0)
    block = rotated(per, n)(step, i)

    def plane(k):
        sigma = pick_plane(k, PLANES, block, vol, before, after, low, high, blocks)
        return (0.5 * correction) * sigma * sigma * chunk_plane(carried, block * PLANES + k + 1)

    def rows(k):
        at = pl.ds(block * PLANES + k + 1, 1)
        s_low, s_high = vol_low[at, :], vol_high[at, :]
        return (
            (0.5 * correction) * s_low * s_low * carried_low[at, :],
            (0.5 * correction) * s_high * s_high * carried_high[at, :],
        )

    def emit(k, v, prev, nxt, mixed, inner):
        kept[k] = cotangent[k] + mixed

    sweep(PLANES, plane, rows, emit, False)
    store_piece(outs, step // per, kept)


def react(index, carried, carried_low, carried_high, vol, low, high, vol_low, vol_high, cotangent, n):
    bx, by, bz = vol.shape
    xs = bx // n
    per = xs // PLANES
    block = rotated(per, n)
    return pl.pallas_call(
        functools.partial(reaction_kernel, per=per, n=n, blocks=bx // PLANES),
        grid_spec=pltpu.PrefetchScalarGridSpec(
            num_scalar_prefetch=1,
            grid=(n * per,),
            in_specs=[whole(carried.shape), whole(carried_low.shape), whole(carried_high.shape)]
            + plane_specs(block, bx - 1, vol.shape)
            + [whole(low.shape), whole(high.shape), whole(vol_low.shape), whole(vol_high.shape)]
            + [pl.BlockSpec((PLANES, by, bz), lambda s, i: (block(s, i), 0, 0))],
            out_specs=piece_specs(PLANES, (by, bz), per, n),
            scratch_shapes=[pltpu.VMEM((PLANES, by, bz), F32)],
        ),
        out_shape=[jax.ShapeDtypeStruct((xs, by, bz), F32)] * n,
        compiler_params=params(40),
        cost_estimate=cost(4e9, 17),
        name="reaction",
    )(index, carried, carried_low, carried_high, vol, vol, vol, low, high, vol_low, vol_high, cotangent)


def lines_kernel(i, *refs, per, n):
    totals, uppers = refs[:n], refs[n : 2 * n]
    cotangent, upper_low, upper_high, third3, out = refs[2 * n :]
    step = pl.program_id(0)
    turn = step // per
    block = rotated(per, n)(step, i)
    for k in range(PLANES):
        total = select([ref[k] for ref in totals], turn)
        upper = select([chunk_plane(ref, k) for ref in uppers], turn)
        at = pl.ds(block * PLANES + k, 1)
        up, down = y_pair(upper, upper_low[at, :], upper_high[at, :])
        third = right_product(total, third3[...])
        z_up, z_down = z_pair(third)
        lines = (up + down - 2.0 * upper) + (z_up + z_down - 2.0 * third)
        out[k] = cotangent[k] - total - damping * lines


def gather_lines(index, totals, uppers, cotangent, upper_low, upper_high, third3):
    n = len(totals)
    bx, by, bz = cotangent.shape
    xs = bx // n
    per = xs // PLANES
    wide, lines = uppers[0].shape[0], uppers[0].shape[2]
    block = rotated(per, n)
    order = [(n - e) % n for e in range(n)]
    return pl.pallas_call(
        functools.partial(lines_kernel, per=per, n=n),
        grid_spec=pltpu.PrefetchScalarGridSpec(
            num_scalar_prefetch=1,
            grid=(n * per,),
            in_specs=piece_specs(PLANES, (by, bz), per, n)
            + chunk_piece_specs(wide, lines, bz, per, range(n))
            + [pl.BlockSpec((PLANES, by, bz), lambda s, i: (block(s, i), 0, 0))]
            + [whole(upper_low.shape), whole(upper_high.shape), whole(third3.shape)],
            out_specs=pl.BlockSpec((PLANES, by, bz), lambda s, i: (block(s, i), 0, 0)),
        ),
        out_shape=jax.ShapeDtypeStruct(cotangent.shape, F32),
        compiler_params=params(40),
        cost_estimate=cost(5e9, 17),
        name="lines",
    )(index, *totals, *[uppers[order[d]] for d in range(n)], cotangent, upper_low, upper_high, third3)


def mixed_kernel(i, field, *refs, n):
    outs, scratch = refs[:n], refs[n]
    by = outs[0].shape[1]

    def emit(k, v, prev, nxt, mixed, inner):
        scratch[...] = mixed
        for d, out in enumerate(outs):
            start = pl.multiple_of(lax.rem(i[0] + d, n) * by, by)
            out[k] = scratch[pl.ds(start, by), :]

    zero = jnp.zeros((1, field.shape[2]), F32)
    sweep(field.shape[0] - 2, lambda k: field[k + 1], lambda k: (zero, zero), emit, False)


def mix(index, field, n):
    rows, ny, bz = field.shape
    xs, by = rows - 2, ny // n
    return pl.pallas_call(
        functools.partial(mixed_kernel, n=n),
        grid_spec=pltpu.PrefetchScalarGridSpec(
            num_scalar_prefetch=1,
            grid=(1,),
            in_specs=[whole(field.shape)],
            out_specs=[whole((xs, by, bz))] * n,
            scratch_shapes=[pltpu.VMEM((ny, bz), F32)],
        ),
        out_shape=[jax.ShapeDtypeStruct((xs, by, bz), F32)] * n,
        compiler_params=params(40),
        cost_estimate=cost(4e9, 9),
        name="mixed",
    )(index, field)


def patch_sums(out, step, planes, patch, patch_t, groups):
    @pl.when(step == 0)
    def _():
        out[...] = jnp.zeros_like(out)

    count, (by, bz) = len(planes), planes[0].shape
    value_high, value_low = split(jnp.concatenate(planes, axis=0))
    ones = jnp.ones((2 * bz, 128), BF16)
    column = jnp.dot(jnp.concatenate([value_high, value_low], axis=1), ones, preferred_element_type=F32)
    number = jnp.concatenate([patch[pl.ds(k, 1), :] for k in range(count)], axis=1)
    coarse = lax.broadcasted_iota(jnp.int32, (groups, count * by), 0) == lax.shift_right_logical(number, 7)
    number_t = patch_t[...].reshape(count * by, 1)
    lane = lax.broadcasted_iota(jnp.int32, (count * by, 128), 1)
    high, low = split(jnp.where(lane == lax.bitwise_and(number_t, 127), column, 0.0))
    out[...] += jnp.dot(
        jnp.where(coarse, 1.0, 0.0).astype(BF16), jnp.concatenate([high, low], axis=1), preferred_element_type=F32
    )


def frozen_kernel(
    i, state, before, after, low, high, q_low, q_high, third3, vol, carried, patch, patch_t, weight, out, *, blocks, groups
):
    block = pl.program_id(0)
    planes = []

    def plane(k):
        v = pick_plane(k, PLANES, block, state, before, after, low, high, blocks)
        up, down = z_pair(v)
        return v + damping * right_product(up + down - 2.0 * v, third3[...])

    def emit(k, v, prev, nxt, mixed, inner):
        w = correction * vol[k] * chunk_plane(carried, block * PLANES + k + 1)
        weight[k] = w
        planes.append(-w * mixed)

    sweep(
        PLANES,
        plane,
        lambda k: (q_low[pl.ds(block * PLANES + k + 1, 1), :], q_high[pl.ds(block * PLANES + k + 1, 1), :]),
        emit,
        False,
    )
    patch_sums(out, block, planes, patch, patch_t, groups)


def frozen(index, state, low, high, q_low, q_high, third3, vol, carried, patch, patch_t, groups):
    bx, by, bz = state.shape
    blocks = bx // PLANES
    main = pl.BlockSpec((PLANES, by, bz), lambda s, i: (s, 0, 0))
    return pl.pallas_call(
        functools.partial(frozen_kernel, blocks=blocks, groups=groups),
        grid_spec=pltpu.PrefetchScalarGridSpec(
            num_scalar_prefetch=1,
            grid=(blocks,),
            in_specs=plane_specs(natural, bx - 1, state.shape)
            + [whole(low.shape), whole(high.shape), whole(q_low.shape), whole(q_high.shape), whole(third3.shape)]
            + [main, whole(carried.shape)]
            + [pl.BlockSpec((PLANES, by), lambda s, i: (s, 0))]
            + [pl.BlockSpec((PLANES, by, 1), lambda s, i: (s, 0, 0))],
            out_specs=[main, whole((groups, 256))],
        ),
        out_shape=[jax.ShapeDtypeStruct(state.shape, F32), jax.ShapeDtypeStruct((groups, 256), F32)],
        compiler_params=params(32),
        cost_estimate=cost(5e9, 17),
        name="frozen",
    )(index, state, state, state, low, high, q_low, q_high, third3, vol, carried, patch, patch_t)


def column_kernel(i, *refs, per, n, groups):
    drifts = refs[:n]
    weight, source, start, patch, patch_t, given, out = refs[n:]
    step = pl.program_id(0)
    turn = step // per
    block = rotated(per, n)(step, i)
    planes = [
        weight[k] * select([ref[k] for ref in drifts], turn)
        + source[k] * chunk_plane(start, block * PLANES + k + 1)
        for k in range(PLANES)
    ]
    patch_sums(out, step, planes, patch, patch_t, groups)

    @pl.when(step == pl.num_programs(0) - 1)
    def _():
        out[...] += given[...]


def column_sums(index, drifts, weight, source, start, patch, patch_t, given):
    n = len(drifts)
    bx, by, bz = source.shape
    xs = bx // n
    per = xs // PLANES
    groups = given.shape[0]
    block = rotated(per, n)
    order = [(n - e) % n for e in range(n)]
    main = pl.BlockSpec((PLANES, by, bz), lambda s, i: (block(s, i), 0, 0))
    return pl.pallas_call(
        functools.partial(column_kernel, per=per, n=n, groups=groups),
        grid_spec=pltpu.PrefetchScalarGridSpec(
            num_scalar_prefetch=1,
            grid=(n * per,),
            in_specs=piece_specs(PLANES, (by, bz), per, n)
            + [main, main, whole(start.shape)]
            + [pl.BlockSpec((PLANES, by), lambda s, i: (block(s, i), 0))]
            + [pl.BlockSpec((PLANES, by, 1), lambda s, i: (block(s, i), 0, 0)), whole(given.shape)],
            out_specs=whole(given.shape),
        ),
        out_shape=jax.ShapeDtypeStruct(given.shape, F32),
        compiler_params=params(40),
        cost_estimate=cost(4e9, 17),
        name="column",
    )(index, *[drifts[order[d]] for d in range(n)], weight, source, start, patch, patch_t, given)


def adjoint_kernel(
    i, start, start_low, start_high, vol, before, after, low, high, vol_low, vol_high, tail, out, *, blocks
):
    block = pl.program_id(0)
    raw = {}

    def plane(k):
        sigma = pick_plane(k, PLANES, block, vol, before, after, low, high, blocks)
        raw[k] = chunk_plane(start, block * PLANES + k + 1)
        return (0.5 * time_step) * sigma * sigma * raw[k]

    def rows(k):
        at = pl.ds(block * PLANES + k + 1, 1)
        s_low, s_high = vol_low[at, :], vol_high[at, :]
        return (
            (0.5 * time_step) * s_low * s_low * start_low[at, :],
            (0.5 * time_step) * s_high * s_high * start_high[at, :],
        )

    def emit(k, v, prev, nxt, mixed, inner):
        spread = mixed + (prev + nxt - 2.0 * v) + inner
        lines = raw[k - 1] + raw[k + 1] - 2.0 * raw[k]
        out[k] = raw[k] + spread + tail[k] - damping * lines

    sweep(PLANES, plane, rows, emit, True)


def finish(index, start, start_low, start_high, vol, low, high, vol_low, vol_high, tail):
    bx, by, bz = vol.shape
    return pl.pallas_call(
        functools.partial(adjoint_kernel, blocks=bx // PLANES),
        grid_spec=pltpu.PrefetchScalarGridSpec(
            num_scalar_prefetch=1,
            grid=(bx // PLANES,),
            in_specs=[whole(start.shape), whole(start_low.shape), whole(start_high.shape)]
            + plane_specs(natural, bx - 1, vol.shape)
            + [whole(low.shape), whole(high.shape), whole(vol_low.shape), whole(vol_high.shape)]
            + [pl.BlockSpec((PLANES, by, bz), lambda s, i: (s, 0, 0))],
            out_specs=pl.BlockSpec((PLANES, by, bz), lambda s, i: (s, 0, 0)),
        ),
        out_shape=jax.ShapeDtypeStruct(vol.shape, F32),
        compiler_params=params(40),
        cost_estimate=cost(5e9, 17),
        name="adjoint",
    )(index, start, start_low, start_high, vol, vol, vol, low, high, vol_low, vol_high, tail)


def neighbours(low_edge, high_edge, axis):
    count = lax.axis_size(axis)
    up = [(k, k + 1) for k in range(count - 1)]
    down = [(k + 1, k) for k in range(count - 1)]
    return lax.ppermute(high_edge, axis, up), lax.ppermute(low_edge, axis, down)


def far_and_near(n):
    return [n // 2] if n > 1 else [], [d for d in range(1, n) if d != n // 2]


def send(pieces, chosen, *earlier):
    n = len(pieces)
    result = list(pieces)
    for d in chosen:
        piece = after(pieces[d], *earlier) if earlier else pieces[d]
        result[d] = lax.ppermute(piece, "narrow", [(k, (k + d) % n) for k in range(n)])
    return result


def pick(pieces, chosen):
    return [pieces[d] for d in chosen]


def after(value, *earlier):
    return lax.optimization_barrier((value, earlier))[0]


def across(piece):
    return lax.all_to_all(piece, "wide", split_axis=0, concat_axis=0, tiled=True)


def row_major(value):
    return with_layout_constraint(value, Layout(major_to_minor=tuple(range(value.ndim))))


def cross_both(pieces, before, between, near, far):
    pieces = [row_major(piece) for piece in pieces]
    lines = send(pieces, near)
    lines = send(lines, far, *pick(lines, near))
    lines = [row_major(line) for line in lines]
    block = jnp.concatenate(pick(lines, [0] + near), axis=1)
    chunks = [across(after(block, *before) if before else block)]
    for d in far:
        chunks.append(across(after(lines[d], chunks[-1], *between)))
    return lines, chunks, pick(lines, far)


def y_edges(chunks):
    return neighbours(chunks[0, :, 0, :], chunks[-1, :, -1, :], "narrow")


def on_device_kernels(state, volatility, cotangent, solve_first, solve_second, solve_third, patch_index):
    n, wide = lax.axis_size("narrow"), lax.axis_size("wide")
    here = lax.axis_index("narrow")
    index = here.astype(jnp.int32).reshape(1)
    bx, by, bz = state.shape
    xs = bx // n
    groups = PATCHES // 128

    ahead = (here + jnp.arange(n)) % n
    back = (here - jnp.arange(n)) % n

    far, near = far_and_near(n)
    every = range(n)

    cot_pieces = [lax.dynamic_slice_in_dim(cotangent, ahead[d] * xs, xs, 0) for d in range(n)]
    early, late = near[:1], near[1:]
    both_low, both_high = neighbours(
        jnp.stack([state[0], volatility[0]]), jnp.stack([state[-1], volatility[-1]]), "wide"
    )
    both = jnp.stack([state[:, :: by - 1], volatility[:, :: by - 1]])
    both = jnp.concatenate([both_low[:, None, :: by - 1], both, both_high[:, None, :: by - 1]], axis=1)
    y_low, y_high = neighbours(both[:, :, 0], both[:, :, 1], "narrow")
    state_x = (both_low[0:1], both_high[0:1])
    vol_x = (both_low[1:2], both_high[1:2])
    state_y = (y_low[0], y_high[0])
    vol_y = (y_low[1], y_high[1])
    cot_lines = send(cot_pieces, near, y_low, y_high)

    second_t = solve_second.T.reshape(n, by, n, by)
    second_t3 = left_form(second_t[ahead][:, :, back].reshape(n * by, n * by))
    second_n = solve_second.reshape(n * by, n, by)
    second_n3 = left_form(second_n[:, back].reshape(n * by, n * by))
    third_t3 = right_form(solve_third)
    third_n3 = right_form(solve_third.T)
    first_n3 = left_form(solve_first)
    first_t = solve_first.T.reshape(wide * bx, wide, n, xs)
    first_t = first_t[:, :, back]
    groups_of = [[0] + near] + [[d] for d in far]
    first_t3 = left_form(
        jnp.concatenate([first_t[:, :, jnp.array(g)].reshape(wide * bx, -1) for g in groups_of], axis=1)
    )

    a, source = forward(index, state, volatility, *state_x, *state_y, wide)
    a = after(a, *pick(cot_lines, early))
    cot_lines = send(cot_lines, far, *pick(cot_lines, near))
    forward_lines = after(first([across(a)], first_n3, 1), *pick(cot_lines, far), second_t3, third_t3)
    back = second(after(cot_lines, forward_lines), second_t3, third_t3, wide)
    solved = across(after(forward_lines, *back))

    lifted_pieces = lifted(index, solved, state, *state_x, *state_y, n)
    back, carried_chunks, gone = cross_both(back, (solved,), lifted_pieces, near, far)
    carried_lines = first(carried_chunks, first_t3, 1)
    level_lines = send(lifted_pieces, late, gone)
    carried = across(after(carried_lines, *pick(level_lines, late)))

    level_lines = send(level_lines, far, *pick(level_lines, late))
    carried = after(carried, *pick(level_lines, far))
    carried_y = y_edges(carried)
    level_lines = send(level_lines, early, *carried_y)
    totals = react(index, carried, *carried_y, volatility, *vol_x, *vol_y, cotangent, n)
    total_lines = send(totals, near)

    level = second(after(level_lines, totals), second_n3, third_n3, 0)[0]
    drift_pieces = mix(index, level, n)

    def frozen_rows(rows):
        padded = jnp.pad(rows, ((0, 0), (1, 1)))
        curved = padded[:, 2:] + padded[:, :-2] - 2.0 * rows
        return rows + damping * jnp.dot(curved, solve_third.T, precision=lax.Precision.HIGHEST)

    patch_t = patch_index[:, :, None]
    weight, sums = frozen(
        index,
        after(state, *totals),
        *state_x,
        frozen_rows(state_y[0]),
        frozen_rows(state_y[1]),
        third_n3,
        volatility,
        carried,
        patch_index,
        patch_t,
        groups,
    )

    total_lines = send(total_lines, far, sums, *pick(total_lines, near))
    total_lines = after(total_lines, drift_pieces)
    drifts = send(drift_pieces, early, *total_lines)
    uppers = after(second(total_lines, second_t3, third_t3, wide), *pick(drifts, early))
    uppers, start_chunks, gone = cross_both(uppers, (), (), near, far)
    start_lines = first(start_chunks, first_t3, 1)
    drifts = send(drifts, late, gone)
    start = across(after(start_lines, *pick(drifts, late)))

    order = (here - jnp.arange(n)) % n
    edge_low = jnp.stack([piece[0, :, 0] for piece in uppers])[order].reshape(bx, bz)
    edge_high = jnp.stack([piece[-1, :, -1] for piece in uppers])[order].reshape(bx, bz)
    upper_y = neighbours(edge_low, edge_high, "narrow")
    drifts = send(drifts, far, *pick(drifts, late), *upper_y)
    tail = gather_lines(index, totals, uppers, cotangent, *upper_y, third_t3)

    start = after(start, tail)
    start_y = y_edges(start)
    start = after(start, *start_y)
    sums = column_sums(index, drifts, weight, source, start, patch_index, patch_t, sums)
    count, joint = n * wide, ("wide", "narrow")
    sums = (sums[:, :128] + sums[:, 128:]).reshape(count, PATCHES // count)
    shares = lax.all_to_all(sums, joint, split_axis=0, concat_axis=0, tiled=True)
    vega = jnp.sum(shares, axis=0)

    adjoint = finish(index, start, *start_y, volatility, *vol_x, *vol_y, tail)
    return (adjoint, vega * vega_scale)


def on_device(*args):
    n, wide = lax.axis_size("narrow"), lax.axis_size("wide")
    bx, by, bz = args[0].shape
    aligned = bx % (n * PLANES) == 0 and by % 128 == 0 and by % (wide * 8) == 0 and bz == 128
    aligned = aligned and PATCHES % (n * wide) == 0 and by // wide % 2 == 0
    return on_device_kernels(*args) if aligned else on_device_plain(*args)


def solution(mesh):
    placed = (
        P("wide", "narrow", None),
        P("wide", "narrow", None),
        P("wide", "narrow", None),
        P(),
        P(),
        P(),
        P("wide", "narrow"),
    )
    return jax.shard_map(
        on_device,
        mesh=mesh,
        in_specs=placed,
        out_specs=(P("wide", "narrow", None), P(("wide", "narrow"))),
        check_vma=False,
    )
```
